128 devices in a mesh: seq: 8 (over y, core), wide: 16 (over x, z).
Axes of the slice: x: 4, y: 4, z: 4, core: 2. Of those that a mesh axis runs over, the one named last changes fastest.
Arguments:
- tokens: bfloat16 [16384, 1536], P(('wide', 'seq')), may hold values from -6 to 6
- norm1_gain: bfloat16 [1536], P('wide'), may hold values from 0.5 to 1.5
- w_query: bfloat16 [1536, 1536], P('wide'), may hold values from -0.3125 to 0.3125
- w_key: bfloat16 [1536, 768], P('wide'), may hold values from -0.15625 to 0.15625
- w_value: bfloat16 [1536, 768], P('wide'), may hold values from -0.15625 to 0.15625
- w_out: bfloat16 [1536, 1536], P('wide'), may hold values from -2.5 to 2.5
- norm2_gain: bfloat16 [1536], P('wide'), may hold values from 0.5 to 1.5
- w_gate: bfloat16 [1536, 4096], P('wide'), may hold values from -0.15625 to 0.15625
- w_up: bfloat16 [1536, 4096], P('wide'), may hold values from -0.15625 to 0.15625
- w_down: bfloat16 [4096, 1536], P('wide'), may hold values from -0.09375 to 0.09375
- out_cotangent: bfloat16 [16384, 1536], P(('wide', 'seq')), may hold values from -6 to 6
Outputs:
- output: bfloat16 [16384, 1536], P(('wide', 'seq'))
- tokens_grad: bfloat16 [16384, 1536], P(('wide', 'seq'))
- norm1_gain_grad: float32 [1536], P('wide')
- w_query_grad: float32 [1536, 1536], P('wide')
- w_key_grad: float32 [1536, 768], P('wide')
- w_value_grad: float32 [1536, 768], P('wide')
- w_out_grad: float32 [1536, 1536], P('wide')
- norm2_gain_grad: float32 [1536], P('wide')
- w_gate_grad: float32 [1536, 4096], P('wide')
- w_up_grad: float32 [1536, 4096], P('wide')
- w_down_grad: float32 [4096, 1536], P('wide')
The draws below stay inside these ranges and needn't reach their ends.
All inputs are finite; a program needn't handle non-finite values.
Results may differ from the reference program's by a relative error of at most 0.025.
Values may be sent and summed in bfloat16 or wider, within the bound.
No kernel may reach another device: no remote copies, remote signals or barrier semaphores. Data moves between devices by JAX's collectives and lax.ppermute only.
A program may use at most 192 MiB of HBM per device.

```python
import math
import jax
import jax.numpy as jnp
from jax import lax

D = 1536
HEADS = 16
KV_HEADS = 8
HEAD_DIM = 96
FF = 4096
TOKENS = 16384


def level_of(key, shape, cuts, least, largest):
    def one(axis_at, blocks):
        heights = jax.random.uniform(jax.random.fold_in(jax.random.fold_in(key, 6), axis_at), (blocks,), jnp.float32, least / len(cuts), largest / len(cuts))
        return jnp.repeat(jnp.exp(heights), shape[axis_at] // blocks).reshape((-1,) + (1,) * (len(shape) - axis_at - 1))

    level = one(*cuts[0])
    for cut in cuts[1:]:
        level = level * one(*cut)
    return level


def noise(key, shape, width, reach, cuts=(), kind=jnp.bfloat16):
    level = level_of(key, shape, cuts, -0.22, 0.18) if cuts else 1.0
    values = jax.random.normal(key, shape, jnp.float32) * width * level
    return jnp.minimum(jnp.maximum(values, -reach), reach).astype(kind)


def setup_inputs(seed: int = 0) -> dict:
    key_list = jax.random.split(jax.random.key(seed), 12)
    tokens = noise(key_list[0], (TOKENS, D), 1.0, 6.0, ((0, 128),))
    norm1_gain = jnp.clip(1.0 + 0.1 * jax.random.normal(key_list[1], (D,), jnp.float32), 0.5, 1.5).astype(jnp.bfloat16)
    w_query = noise(key_list[2], (D, D), (D // 4) ** -0.5, 0.3125, ((0, 16),))
    w_key = noise(key_list[3], (D, KV_HEADS * HEAD_DIM), D ** -0.5, 0.15625, ((0, 16),))
    w_value = noise(key_list[4], (D, KV_HEADS * HEAD_DIM), D ** -0.5, 0.15625, ((0, 16),))
    w_out = noise(key_list[5], (D, D), (max(D // 256, 1)) ** -0.5, 2.5, ((0, 16),))
    norm2_gain = jnp.clip(1.0 + 0.1 * jax.random.normal(key_list[6], (D,), jnp.float32), 0.5, 1.5).astype(jnp.bfloat16)
    w_gate = noise(key_list[7], (D, FF), D ** -0.5, 0.15625, ((0, 16),))
    w_up = noise(key_list[8], (D, FF), D ** -0.5, 0.15625, ((0, 16),))
    w_down = noise(key_list[9], (FF, D), FF ** -0.5, 0.09375, ((0, 16),))
    out_cotangent = noise(key_list[10], (TOKENS, D), 1.0, 6.0, ((0, 128),))
    return {"tokens": tokens, "norm1_gain": norm1_gain, "w_query": w_query, "w_key": w_key, "w_value": w_value, "w_out": w_out, "norm2_gain": norm2_gain, "w_gate": w_gate, "w_up": w_up, "w_down": w_down, "out_cotangent": out_cotangent}


epsilon = 1e-05
rope_base = 100000.0
negative = -1e+30
highest = lax.Precision.HIGHEST

@jax.custom_vjp
def low(v):
    return lax.optimization_barrier(v.astype(jnp.bfloat16)).astype(jnp.float32)

@jax.custom_vjp
def low_back(v):
    return v

def low_keep(v):
    return (low(v), None)

def low_pass(kept, grad):
    return (grad,)

def back_keep(v):
    return (v, None)

def back_low(kept, grad):
    return (low(grad),)
low.defvjp(low_keep, low_pass)
low_back.defvjp(back_keep, back_low)

def product(left_side, right_side):
    return jnp.dot(left_side, right_side, precision=highest)

def normalize(values):
    return values * lax.rsqrt(lax.optimization_barrier(jnp.mean(values * values, axis=-1, keepdims=True)) + epsilon)

def rotate(values, positions):
    halves = HEAD_DIM // 2
    frequency = jnp.exp(jnp.arange(halves).astype(jnp.float32) * (-2.0 * math.log(rope_base) / HEAD_DIM))
    angles = positions[:, None] * frequency[None, :]
    cosine_table = jnp.cos(angles)[:, None, :]
    sine_table = jnp.sin(angles)[:, None, :]
    first_half = values[..., :halves]
    second_half = values[..., halves:]
    return jnp.concatenate([first_half * cosine_table - second_half * sine_table, second_half * cosine_table + first_half * sine_table], axis=-1)

def attend(query_rot, key_rot, value_rows):
    block_rows = math.gcd(TOKENS, 128)
    block_count = TOKENS // block_rows
    group_size = HEADS // KV_HEADS
    score_scale = 1.0 / math.sqrt(HEAD_DIM)
    query_blocks = query_rot.reshape(block_count, block_rows, KV_HEADS, group_size, HEAD_DIM)
    starts = (jnp.arange(block_count) * block_rows).astype(jnp.int32)
    key_index = jnp.arange(TOKENS).astype(jnp.int32)

    def one_block(packed):
        query_block, first_row = packed
        scores = jnp.einsum('rkgd,skd->kgrs', query_block, key_rot, precision=highest) * score_scale
        scores = low_back(scores)
        query_index = first_row + jnp.arange(block_rows).astype(jnp.int32)
        allowed = key_index[None, :] <= query_index[:, None]
        scores = jnp.where(allowed, scores, negative)
        scores = scores - lax.optimization_barrier(jnp.max(scores, axis=-1, keepdims=True))
        probs_exp = jnp.exp(scores)
        probs_low = low(probs_exp / lax.optimization_barrier(jnp.sum(probs_exp, axis=-1, keepdims=True)))
        return jnp.einsum('kgrs,skd->rkgd', probs_low, value_rows, precision=highest)
    attended = lax.map(jax.checkpoint(one_block), (query_blocks, starts))
    return attended.reshape(TOKENS, D)

def forward(inputs, gain_one, query_weight, key_weight, value_weight, out_weight, gain_two, gate_weight, up_weight, down_weight):
    hidden_one = low(normalize(inputs) * gain_one)
    queries = low(low_back(product(hidden_one, query_weight)))
    keys = low(low_back(product(hidden_one, key_weight)))
    values = low(low_back(product(hidden_one, value_weight)))
    positions = jnp.arange(TOKENS).astype(jnp.float32)
    query_rot = low(rotate(queries.reshape(TOKENS, HEADS, HEAD_DIM), positions))
    key_rot = low(rotate(keys.reshape(TOKENS, KV_HEADS, HEAD_DIM), positions))
    value_rows = values.reshape(TOKENS, KV_HEADS, HEAD_DIM)
    attended = low(low_back(attend(query_rot, key_rot, value_rows)))
    residual = inputs + low_back(product(attended, out_weight))
    hidden_two = low(normalize(residual) * gain_two)
    gate_pre = low_back(product(hidden_two, gate_weight))
    up_pre = low_back(product(hidden_two, up_weight))
    middle = low(jax.nn.silu(gate_pre) * up_pre)
    return residual + product(middle, down_weight)

def reference(tokens, norm1_gain, w_query, w_key, w_value, w_out, norm2_gain, w_gate, w_up, w_down, out_cotangent):
    promoted = [item.astype(jnp.float32) for item in (tokens, norm1_gain, w_query, w_key, w_value, w_out, norm2_gain, w_gate, w_up, w_down)]
    output, pullback = jax.vjp(forward, *promoted)
    grads = pullback(out_cotangent.astype(jnp.float32))
    return (output.astype(jnp.bfloat16), grads[0].astype(jnp.bfloat16), grads[1], grads[2], grads[3], grads[4], grads[5], grads[6], grads[7], grads[8], grads[9])
```

```python
import math

import jax
import jax.numpy as jnp
from jax import lax
from jax.experimental import pallas as pl
from jax.experimental.pallas import tpu as pltpu
from jax.sharding import PartitionSpec as P

HEAD_DIM = 96
CHUNK = 512
CHUNKS = 32
GROUP = 2
Q_ROWS = GROUP * HEAD_DIM
KV_ROWS = 2 * HEAD_DIM
FF_PIECE = 32

epsilon = 1e-05
rope_base = 100000.0
negative = -1e30
log2e = math.log2(math.e)
score_scale = 1.0 / math.sqrt(HEAD_DIM)

F32 = jnp.float32
BF16 = jnp.bfloat16


def dot(left, right, left_dim, right_dim):
    return lax.dot_general(
        left, right, (((left_dim,), (right_dim,)), ((), ())), preferred_element_type=F32
    )


def slot_of(chunk):
    return jnp.where(chunk % 2 == 0, chunk, CHUNKS - chunk)


def causal_mask():
    keys = lax.broadcasted_iota(jnp.int32, (CHUNK, CHUNK), 0)
    rows = lax.broadcasted_iota(jnp.int32, (CHUNK, CHUNK), 1)
    return keys <= rows


def attend_kernel(rank_ref, q_ref, kv_ref, o_ref, lse_ref, max_s, sum_s, acc_s):
    rank = rank_ref[0]
    for part in range(2):
        own = 2 * rank if part == 0 else CHUNKS - 1 - 2 * rank
        cols = slice(part * CHUNK, (part + 1) * CHUNK)
        max_s[...] = jnp.full_like(max_s, negative)
        sum_s[...] = jnp.zeros_like(sum_s)
        acc_s[...] = jnp.zeros_like(acc_s)

        def step(chunk, diagonal):
            slot = slot_of(chunk)
            keys = kv_ref[slot, 0:HEAD_DIM, :].T
            values = kv_ref[slot, HEAD_DIM:KV_ROWS, :]
            for head in range(GROUP):
                rows = slice(head * HEAD_DIM, (head + 1) * HEAD_DIM)
                scores = jnp.dot(keys, q_ref[rows, cols], preferred_element_type=F32)
                if diagonal:
                    scores = jnp.where(causal_mask(), scores, negative)
                old_max = max_s[head : head + 1, :]
                new_max = jnp.maximum(old_max, jnp.max(scores, axis=0, keepdims=True))
                factor = jnp.exp2(old_max - new_max)
                probs = jnp.exp2(scores - new_max)
                sum_s[head : head + 1, :] = sum_s[head : head + 1, :] * factor + jnp.sum(
                    probs, axis=0, keepdims=True
                )
                max_s[head : head + 1, :] = new_max
                acc_s[rows, :] = acc_s[rows, :] * factor + jnp.dot(
                    values, probs.astype(BF16), preferred_element_type=F32
                )

        step(own, True)

        def body(chunk, carry):
            step(chunk, False)
            return carry

        lax.fori_loop(0, own, body, 0)
        for head in range(GROUP):
            rows = slice(head * HEAD_DIM, (head + 1) * HEAD_DIM)
            total = sum_s[head : head + 1, :]
            o_ref[rows, cols] = (acc_s[rows, :] / total).astype(BF16)
            lse_ref[head : head + 1, cols] = max_s[head : head + 1, :] + jnp.log2(total)


def attend_back_kernel(
    rank_ref, q_ref, kv_ref, do_ref, lse_ref, delta_ref, dq_ref, dkv_ref, dkv_s, dq_s
):
    rank = rank_ref[0]
    dkv_s[...] = jnp.zeros_like(dkv_s)
    for part in range(2):
        own = 2 * rank if part == 0 else CHUNKS - 1 - 2 * rank
        cols = slice(part * CHUNK, (part + 1) * CHUNK)
        dq_s[...] = jnp.zeros_like(dq_s)

        def step(chunk, diagonal):
            slot = slot_of(chunk)
            keys = kv_ref[slot, 0:HEAD_DIM, :]
            values_t = kv_ref[slot, HEAD_DIM:KV_ROWS, :].T
            keys_t = keys.T
            dk = dkv_s[slot, 0:HEAD_DIM, :]
            dv = dkv_s[slot, HEAD_DIM:KV_ROWS, :]
            for head in range(GROUP):
                rows = slice(head * HEAD_DIM, (head + 1) * HEAD_DIM)
                q = q_ref[rows, cols]
                do = do_ref[rows, cols]
                scores = jnp.dot(keys_t, q, preferred_element_type=F32)
                probs = jnp.exp2(scores - lse_ref[head : head + 1, cols])
                if diagonal:
                    probs = jnp.where(causal_mask(), probs, 0.0)
                dp = jnp.dot(values_t, do, preferred_element_type=F32)
                ds = (probs * (dp - delta_ref[head : head + 1, cols])).astype(BF16)
                dv = dv + dot(do, probs.astype(BF16), 1, 1)
                dk = dk + dot(q, ds, 1, 1)
                dq_s[rows, :] += jnp.dot(keys, ds, preferred_element_type=F32)
            dkv_s[slot, 0:HEAD_DIM, :] = dk
            dkv_s[slot, HEAD_DIM:KV_ROWS, :] = dv

        step(own, True)

        def body(chunk, carry):
            step(chunk, False)
            return carry

        lax.fori_loop(0, own, body, 0)
        dq_ref[:, cols] = dq_s[...] * score_scale

    def finish(slot, carry):
        dkv_ref[slot, 0:HEAD_DIM, :] = (dkv_s[slot, 0:HEAD_DIM, :] * math.log(2.0)).astype(BF16)
        dkv_ref[slot, HEAD_DIM:KV_ROWS, :] = dkv_s[slot, HEAD_DIM:KV_ROWS, :].astype(BF16)
        return carry

    lax.fori_loop(0, CHUNKS, finish, 0)


in_vmem = pl.BlockSpec(memory_space=pltpu.VMEM)
in_smem = pl.BlockSpec(memory_space=pltpu.SMEM)
kernel_params = pltpu.CompilerParams(vmem_limit_bytes=56 * 1024 * 1024)
pairs = (CHUNKS + 1) * GROUP * CHUNK * CHUNK


def attend(rank, q, kv):
    return pl.pallas_call(
        attend_kernel,
        out_shape=(
            jax.ShapeDtypeStruct((Q_ROWS, 2 * CHUNK), BF16),
            jax.ShapeDtypeStruct((GROUP, 2 * CHUNK), F32),
        ),
        in_specs=[in_smem, in_vmem, in_vmem],
        out_specs=(in_vmem, in_vmem),
        scratch_shapes=[
            pltpu.VMEM((GROUP, CHUNK), F32),
            pltpu.VMEM((GROUP, CHUNK), F32),
            pltpu.VMEM((Q_ROWS, CHUNK), F32),
        ],
        compiler_params=kernel_params,
        cost_estimate=pl.CostEstimate(
            flops=2 * 2 * 256 * pairs, bytes_accessed=8 * 2**20, transcendentals=pairs
        ),
        name="attend",
    )(rank, q, kv)


def attend_back(rank, q, kv, do, lse, delta):
    return pl.pallas_call(
        attend_back_kernel,
        out_shape=(
            jax.ShapeDtypeStruct((Q_ROWS, 2 * CHUNK), F32),
            jax.ShapeDtypeStruct((CHUNKS, KV_ROWS, CHUNK), BF16),
        ),
        in_specs=[in_smem] + [in_vmem] * 5,
        out_specs=(in_vmem, in_vmem),
        scratch_shapes=[
            pltpu.VMEM((CHUNKS, KV_ROWS, CHUNK), F32),
            pltpu.VMEM((Q_ROWS, CHUNK), F32),
        ],
        compiler_params=kernel_params,
        cost_estimate=pl.CostEstimate(
            flops=5 * 2 * 256 * pairs, bytes_accessed=16 * 2**20, transcendentals=pairs
        ),
        name="attend_back",
    )(rank, q, kv, do, lse, delta)


def inverse_rms(values):
    return lax.rsqrt(jnp.mean(values * values, axis=-1, keepdims=True) + epsilon)


def norm_back(scaled_grad, normed, inverse):
    return inverse * (scaled_grad - normed * jnp.mean(scaled_grad * normed, axis=-1, keepdims=True))


def rotate(values, cosine_table, sine_table, direction):
    halves = HEAD_DIM // 2
    first_half = values[..., :halves, :]
    second_half = values[..., halves:, :]
    return jnp.concatenate(
        [
            first_half * cosine_table - direction * second_half * sine_table,
            second_half * cosine_table + direction * first_half * sine_table,
        ],
        axis=-2,
    )


def gather(values, axis_name, axis=0):
    return lax.all_gather(values, axis_name, axis=axis, tiled=True)


def on_device(
    tokens,
    norm1_gain,
    w_query,
    w_key,
    w_value,
    w_out,
    norm2_gain,
    w_gate,
    w_up,
    w_down,
    out_cotangent,
):
    seq_count = lax.axis_size("seq")
    wide_count = lax.axis_size("wide")
    seq_index = lax.axis_index("seq")
    wide_index = lax.axis_index("wide")
    rank = wide_index.astype(jnp.int32).reshape(1)
    model = tokens.shape[1]
    ff = w_gate.shape[1]

    mirror = [
        (s * wide_count + w, s * wide_count + (wide_count - 1 - w if s >= seq_count // 2 else w))
        for s in range(seq_count)
        for w in range(wide_count)
    ]

    def swap(values):
        return lax.ppermute(values, ("seq", "wide"), mirror)

    gain_one = norm1_gain.astype(F32)[:, None]
    gain_two = norm2_gain.astype(F32)[:, None]
    q_cols = lax.dynamic_slice_in_dim(w_query, seq_index * Q_ROWS, Q_ROWS, 1)
    k_cols = lax.dynamic_slice_in_dim(w_key, seq_index * HEAD_DIM, HEAD_DIM, 1)
    v_cols = lax.dynamic_slice_in_dim(w_value, seq_index * HEAD_DIM, HEAD_DIM, 1)
    qkv_shard = (jnp.concatenate([q_cols, k_cols, v_cols], axis=1).astype(F32) * gain_one).astype(
        BF16
    )

    def ff_cols(weight):
        pieces = weight.reshape(weight.shape[0], wide_count, seq_count, FF_PIECE)
        return lax.dynamic_index_in_dim(pieces, seq_index, 2, keepdims=False).reshape(
            weight.shape[0], wide_count * FF_PIECE
        )

    gate_up_shard = (
        jnp.concatenate([ff_cols(w_gate), ff_cols(w_up)], axis=1).astype(F32) * gain_two
    ).astype(BF16)
    down_shard = lax.dynamic_slice_in_dim(w_down, seq_index * FF_PIECE, FF_PIECE, 0)

    tokens_here = swap(tokens)
    cotangent = swap(out_cotangent)
    tokens_all = gather(tokens_here, "seq")
    qkv_weight = gather(qkv_shard, "wide")

    tokens_all = tokens_all.astype(F32)
    normed_one_all = (tokens_all * inverse_rms(tokens_all)).astype(BF16)
    qkv = dot(qkv_weight, normed_one_all, 0, 1).astype(BF16).astype(F32)

    row = jnp.arange(2 * CHUNK, dtype=jnp.int32)
    positions = jnp.where(
        row < CHUNK,
        2 * wide_index * CHUNK + row,
        (CHUNKS - 1 - 2 * wide_index) * CHUNK + row - CHUNK,
    ).astype(F32)
    frequency = jnp.exp(
        jnp.arange(HEAD_DIM // 2).astype(F32) * (-2.0 * math.log(rope_base) / HEAD_DIM)
    )
    angles = frequency[:, None] * positions[None, :]
    cosine_table, sine_table = jnp.cos(angles), jnp.sin(angles)

    qk = rotate(
        qkv[: Q_ROWS + HEAD_DIM].reshape(GROUP + 1, HEAD_DIM, 2 * CHUNK),
        cosine_table,
        sine_table,
        1.0,
    )
    q = (qk[:GROUP] * (score_scale * log2e)).astype(BF16).reshape(Q_ROWS, 2 * CHUNK)
    kv = jnp.concatenate([qk[GROUP].astype(BF16), qkv[Q_ROWS + HEAD_DIM :].astype(BF16)], axis=0)
    kv_chunks = jnp.stack([kv[:, :CHUNK], kv[:, CHUNK:]])
    kv_all = gather(kv_chunks, "wide")
    cotangent_all = gather(cotangent, "seq")
    out_full = gather(w_out, "wide")
    gate_up = gather(gate_up_shard, "wide")
    down = gather(down_shard, "wide")

    attended, log_total = attend(rank, q, kv_all)
    attended_tok = lax.all_to_all(attended, "seq", split_axis=1, concat_axis=0, tiled=True)
    attended_all = gather(attended, "seq")

    inputs = tokens_here.astype(F32)
    inverse_one = inverse_rms(inputs)
    normed_one = inputs * inverse_one
    residual = inputs + dot(attended_tok, out_full, 0, 0)
    inverse_two = inverse_rms(residual)
    normed_two = residual * inverse_two
    normed_two_all = gather(normed_two.astype(BF16), "seq")
    gate_up_pre = dot(normed_two_all, gate_up, 1, 0)
    half = gate_up.shape[1] // 2
    gate_pre, up_pre = gate_up_pre[:, :half], gate_up_pre[:, half:]
    sigmoid_gate = jax.nn.sigmoid(gate_pre)
    activated = gate_pre * sigmoid_gate
    middle = (activated * up_pre).astype(BF16)
    middle_grad = dot(cotangent_all, down, 1, 1)
    up_grad = (middle_grad * activated).astype(BF16)
    gate_grad = (
        middle_grad * up_pre * sigmoid_gate * (1.0 + gate_pre * (1.0 - sigmoid_gate))
    ).astype(BF16)
    gate_up_grad = jnp.concatenate([gate_grad, up_grad], axis=1)
    scaled_two = lax.psum_scatter(
        dot(gate_up_grad, gate_up, 1, 1).astype(BF16), "seq", scatter_dimension=0, tiled=True
    ).astype(F32)
    residual_grad = cotangent.astype(F32) + norm_back(scaled_two, normed_two, inverse_two)
    branch_grad = residual_grad.astype(BF16)
    mixed_grad = dot(out_full, branch_grad, 1, 1).astype(BF16)
    head_grad = lax.all_to_all(mixed_grad, "seq", split_axis=0, concat_axis=1, tiled=True)

    down_part = lax.psum_scatter(
        dot(middle, down, 1, 0).astype(BF16), "seq", scatter_dimension=0, tiled=True
    ).astype(F32)
    output = swap((residual + down_part).astype(BF16))

    row_delta = jnp.sum(
        (head_grad.astype(F32) * attended.astype(F32)).reshape(GROUP, HEAD_DIM, 2 * CHUNK), axis=1
    )
    q_grad_rot, kv_grad_all = attend_back(rank, q, kv_all, head_grad, log_total, row_delta)

    branch_grad_all = gather(branch_grad, "seq")
    branch_grad_cols = lax.dynamic_slice_in_dim(branch_grad_all, seq_index * Q_ROWS, Q_ROWS, 1)
    late_product = jnp.concatenate(
        [
            dot(normed_two_all, gate_up_grad, 0, 0).astype(BF16),
            dot(attended_all, branch_grad_cols, 1, 0).astype(BF16),
        ],
        axis=1,
    )
    late_rows = lax.psum_scatter(late_product, "wide", scatter_dimension=0, tiled=True)
    down_rows = lax.psum_scatter(
        dot(middle, cotangent_all, 0, 0).astype(BF16), "wide", scatter_dimension=0, tiled=True
    )
    late_all = lax.all_gather(late_rows, "seq", axis=0, tiled=False).astype(F32)
    down_grad = gather(down_rows, "seq").astype(F32)

    kv_grad_here = lax.psum_scatter(kv_grad_all, "wide", scatter_dimension=0, tiled=True).astype(
        F32
    )
    kv_grad = jnp.concatenate([kv_grad_here[0], kv_grad_here[1]], axis=1)
    qk_grad = rotate(
        jnp.concatenate([q_grad_rot, kv_grad[:HEAD_DIM]], axis=0).reshape(
            GROUP + 1, HEAD_DIM, 2 * CHUNK
        ),
        cosine_table,
        sine_table,
        -1.0,
    ).reshape(Q_ROWS + HEAD_DIM, 2 * CHUNK)
    qkv_grad = jnp.concatenate([qk_grad.astype(BF16), kv_grad[HEAD_DIM:].astype(BF16)], axis=0)
    scaled_one = lax.psum_scatter(
        dot(qkv_grad, qkv_weight, 0, 1).astype(BF16), "seq", scatter_dimension=0, tiled=True
    ).astype(F32)
    tokens_grad = swap(
        (residual_grad + norm_back(scaled_one, normed_one, inverse_one)).astype(BF16)
    )
    qkv_product = dot(normed_one_all, qkv_grad, 0, 1).astype(BF16)
    qkv_rows = lax.psum_scatter(qkv_product, "wide", scatter_dimension=0, tiled=True)
    qkv_all = lax.all_gather(qkv_rows, "seq", axis=0, tiled=False).astype(F32)

    def join(pieces):
        return pieces.transpose(1, 0, 2).reshape(pieces.shape[1], -1)

    def join_ff(pieces):
        return (
            pieces.reshape(seq_count, pieces.shape[1], wide_count, FF_PIECE)
            .transpose(1, 2, 0, 3)
            .reshape(pieces.shape[1], ff)
        )

    q_product = join(qkv_all[:, :, :Q_ROWS])
    k_product = join(qkv_all[:, :, Q_ROWS : Q_ROWS + HEAD_DIM])
    v_product = join(qkv_all[:, :, Q_ROWS + HEAD_DIM :])
    gate_product = join_ff(late_all[:, :, :half])
    up_product = join_ff(late_all[:, :, half : 2 * half])
    out_grad = join(late_all[:, :, 2 * half :])
    gain_one_grad = (
        jnp.sum(w_query.astype(F32) * q_product, axis=1)
        + jnp.sum(w_key.astype(F32) * k_product, axis=1)
        + jnp.sum(w_value.astype(F32) * v_product, axis=1)
    )
    gain_two_grad = jnp.sum(w_gate.astype(F32) * gate_product, axis=1) + jnp.sum(
        w_up.astype(F32) * up_product, axis=1
    )
    return (
        output,
        tokens_grad,
        gain_one_grad,
        q_product * gain_one,
        k_product * gain_one,
        v_product * gain_one,
        out_grad,
        gain_two_grad,
        gate_product * gain_two,
        up_product * gain_two,
        down_grad,
    )


def solution(mesh):
    placed = (
        P(("wide", "seq"), None),
        P("wide"),
        P("wide", None),
        P("wide", None),
        P("wide", None),
        P("wide", None),
        P("wide"),
        P("wide", None),
        P("wide", None),
        P("wide", None),
        P(("wide", "seq"), None),
    )
    return jax.shard_map(
        on_device,
        mesh=mesh,
        in_specs=placed,
        out_specs=(
            P(("wide", "seq"), None),
            P(("wide", "seq"), None),
            P("wide"),
            P("wide", None),
            P("wide", None),
            P("wide", None),
            P("wide", None),
            P("wide"),
            P("wide", None),
            P("wide", None),
            P("wide", None),
        ),
        check_vma=False,
    )
```

```python
import functools
import math

import jax
import jax.numpy as jnp
from jax import lax
from jax.experimental import pallas as pl
from jax.experimental.pallas import tpu as pltpu
from jax.sharding import PartitionSpec as P

HEAD_DIM = 96
CHUNK = 512
CHUNKS = 32
SIDE = 4
RANKS = SIDE * SIDE
GROUP = 2
Q_ROWS = GROUP * HEAD_DIM
KV_ROWS = 2 * HEAD_DIM
FF_PIECE = 32

epsilon = 1e-05
rope_base = 100000.0
negative = -1e30
log2e = math.log2(math.e)
score_scale = 1.0 / math.sqrt(HEAD_DIM)

F32 = jnp.float32
BF16 = jnp.bfloat16


def dot(left, right, left_dim, right_dim):
    return lax.dot_general(
        left, right, (((left_dim,), (right_dim,)), ((), ())), preferred_element_type=F32
    )


def causal_mask():
    keys = lax.broadcasted_iota(jnp.int32, (CHUNK, CHUNK), 0)
    rows = lax.broadcasted_iota(jnp.int32, (CHUNK, CHUNK), 1)
    return keys <= rows


class Place:
    def __init__(self, rank, piece):
        first = rank < RANKS // 2
        self.early = jnp.where(first, 2 * rank, CHUNKS - 1 - 2 * rank)
        self.early_at = pl.multiple_of(jnp.where(first, 0, piece), piece)
        self.late_at = pl.multiple_of(jnp.where(first, piece, 0), piece)


def source_rank(rank, kind, entry):
    x_back, z_back, x_step, z_step = kind[1:5]
    x = (rank // SIDE - x_back - x_step * entry) & (SIDE - 1)
    z = (rank % SIDE - z_back - z_step * entry) & (SIDE - 1)
    return x * SIDE + z


def for_pieces(rank, kinds, early_only, late_only):
    here = Place(rank, CHUNK)
    for index, kind in enumerate(kinds):

        def body(entry, carry, index=index, kind=kind):
            source = source_rank(rank, kind, entry)
            there = Place(source, CHUNK // 2)
            pl.when(there.early < here.early)(lambda: early_only(index, entry, source, there))
            pl.when(there.early > here.early)(lambda: late_only(index, entry, source, here))
            return carry

        lax.fori_loop(0, kind[0], body, 0)


def attend_block(keys_t, values, q_ref, max_s, sum_s, acc_s, head, cols, diagonal=False):
    rows = slice(head * HEAD_DIM, (head + 1) * HEAD_DIM)
    scores = jnp.dot(keys_t, q_ref[rows, cols], preferred_element_type=F32)
    if diagonal:
        scores = jnp.where(causal_mask(), scores, negative)
    old_max = max_s[head : head + 1, cols]
    new_max = jnp.maximum(old_max, jnp.max(scores, axis=0, keepdims=True))
    factor = jnp.exp2(old_max - new_max)
    probs = jnp.exp2(scores - new_max)
    sum_s[head : head + 1, cols] = sum_s[head : head + 1, cols] * factor + jnp.sum(
        probs, axis=0, keepdims=True
    )
    max_s[head : head + 1, cols] = new_max
    acc_s[rows, cols] = acc_s[rows, cols] * factor + jnp.dot(
        values, probs.astype(BF16), preferred_element_type=F32
    )


key_rows = slice(0, HEAD_DIM)
value_rows = slice(HEAD_DIM, 2 * HEAD_DIM)


def attend_kernel(rank_ref, q_ref, own_ref, kv_ref, o_ref, lse_ref, max_s, sum_s, acc_s):
    rank = rank_ref[0]
    here = Place(rank, CHUNK)
    max_s[...] = jnp.full_like(max_s, negative)
    sum_s[...] = jnp.zeros_like(sum_s)
    acc_s[...] = jnp.zeros_like(acc_s)

    def blocks(keys, values, col_list, diagonal=False):
        keys_t = keys.T
        for cols in col_list:
            for head in range(GROUP):
                attend_block(keys_t, values, q_ref, max_s, sum_s, acc_s, head, cols, diagonal)

    parts = [slice(part * CHUNK, (part + 1) * CHUNK) for part in range(2)]
    late = pl.ds(here.late_at, CHUNK)
    for cols in parts:
        blocks(own_ref[key_rows, cols], own_ref[value_rows, cols], [cols], True)
    early = pl.ds(here.early_at, CHUNK)
    blocks(own_ref[key_rows, early], own_ref[value_rows, early], [late])

    def body(step, carry):
        source = (rank + step) & (RANKS - 1)
        there = Place(source, CHUNK // 2)

        @pl.when(there.early < here.early)
        def _():
            cols = pl.ds(there.early_at, CHUNK // 2)
            keys, values = (
                jnp.concatenate([kv_ref[source, 0, rows, cols], kv_ref[source, 1, rows, cols]], 1)
                for rows in (key_rows, value_rows)
            )
            blocks(keys, values, parts)

        @pl.when(there.early > here.early)
        def _():
            for t in range(2):
                blocks(kv_ref[source, t, key_rows, :], kv_ref[source, t, value_rows, :], [late])

        return carry

    lax.fori_loop(1, RANKS, body, 0)
    for head in range(GROUP):
        rows = slice(head * HEAD_DIM, (head + 1) * HEAD_DIM)
        total = sum_s[head : head + 1, :]
        o_ref[rows, :] = (acc_s[rows, :] / total).astype(BF16)
        lse_ref[head : head + 1, :] = max_s[head : head + 1, :] + jnp.log2(total)


def back_block(keys, keys_t, values_t, refs, head, cols, sums, diagonal=False):
    q_ref, do_ref, lse_ref, delta_ref, dq_s = refs
    rows = slice(head * HEAD_DIM, (head + 1) * HEAD_DIM)
    q = q_ref[rows, cols]
    do = do_ref[rows, cols]
    scores = jnp.dot(keys_t, q, preferred_element_type=F32)
    probs = jnp.exp2(scores - lse_ref[head : head + 1, cols])
    if diagonal:
        probs = jnp.where(causal_mask(), probs, 0.0)
    dp = jnp.dot(values_t, do, preferred_element_type=F32)
    ds = (probs * (dp - delta_ref[head : head + 1, cols])).astype(BF16)
    dk = dot(q, ds, 1, 1)
    dv = dot(do, probs.astype(BF16), 1, 1)
    dq_s[rows, cols] += jnp.dot(keys, ds, preferred_element_type=F32)
    return (dk, dv) if sums is None else (sums[0] + dk, sums[1] + dv)


def attend_back_kernel(
    kinds, own, first, rank_ref, q_ref, do_ref, lse_ref, delta_in, dq_in, kv_ref, *refs
):
    count = len(kinds)
    if own:
        own_ref, refs = refs[0], refs[1:]
    dq_s, outs = refs[0], refs[1 : 1 + count]
    if first:
        delta_ref = refs[-1]
        for head in range(GROUP):
            rows = slice(head * HEAD_DIM, (head + 1) * HEAD_DIM)
            delta_ref[head : head + 1, :] = jnp.sum(
                do_ref[rows, :].astype(F32) * delta_in[rows, :].astype(F32), axis=0, keepdims=True
            )
        dq_s[...] = jnp.zeros_like(dq_s)
    else:
        delta_ref = delta_in
        dq_s[...] = dq_in[...]
    shared = (q_ref, do_ref, lse_ref, delta_ref, dq_s)

    def early_only(index, entry, source, there):
        out, t = outs[index], kinds[index][5]
        cols = pl.ds(there.early_at, CHUNK // 2)
        keys = kv_ref[source, t, key_rows, cols]
        keys_t = keys.T
        values_t = kv_ref[source, t, value_rows, cols].T
        sums = None
        for part in range(2):
            for head in range(GROUP):
                sums = back_block(
                    keys,
                    keys_t,
                    values_t,
                    shared,
                    head,
                    slice(part * CHUNK, (part + 1) * CHUNK),
                    sums,
                )
        dk, dv = sums
        out[entry, key_rows, cols] = (dk * math.log(2.0)).astype(BF16)
        out[entry, value_rows, cols] = dv.astype(BF16)
        out[entry, :, pl.ds(there.late_at, CHUNK // 2)] = jnp.zeros((KV_ROWS, CHUNK // 2), BF16)

    def late_only(index, entry, source, here):
        out, t = outs[index], kinds[index][5]
        keys = kv_ref[source, t, key_rows, :]
        keys_t = keys.T
        values_t = kv_ref[source, t, value_rows, :].T
        sums = None
        for head in range(GROUP):
            sums = back_block(
                keys, keys_t, values_t, shared, head, pl.ds(here.late_at, CHUNK), sums
            )
        dk, dv = sums
        out[entry, key_rows, :] = (dk * math.log(2.0)).astype(BF16)
        out[entry, value_rows, :] = dv.astype(BF16)

    for_pieces(rank_ref[0], kinds, early_only, late_only)
    if own:
        own_out = refs[1 + count]
        here = Place(rank_ref[0], CHUNK)
        early = pl.ds(here.early_at, CHUNK)
        late = pl.ds(here.late_at, CHUNK)

        def block(key_cols, row_cols, sums, diagonal):
            keys = own_ref[key_rows, key_cols]
            keys_t = keys.T
            values_t = own_ref[value_rows, key_cols].T
            for head in range(GROUP):
                sums = back_block(keys, keys_t, values_t, shared, head, row_cols, sums, diagonal)
            return sums

        def store(cols, sums):
            dk, dv = sums
            own_out[key_rows, cols] = (dk * math.log(2.0)).astype(BF16)
            own_out[value_rows, cols] = dv.astype(BF16)

        store(early, block(early, late, block(early, early, None, True), False))
        store(late, block(late, late, None, True))
        dq_s[...] = dq_s[...] * score_scale


in_vmem = pl.BlockSpec(memory_space=pltpu.VMEM)
in_smem = pl.BlockSpec(memory_space=pltpu.SMEM)
kernel_params = pltpu.CompilerParams(vmem_limit_bytes=56 * 1024 * 1024)


def work(units, flops):
    return pl.CostEstimate(
        flops=units * flops, bytes_accessed=2**20, transcendentals=units * GROUP * CHUNK * CHUNK
    )


attend_state = (
    jax.ShapeDtypeStruct((GROUP, 2 * CHUNK), F32),
    jax.ShapeDtypeStruct((GROUP, 2 * CHUNK), F32),
    jax.ShapeDtypeStruct((Q_ROWS, 2 * CHUNK), F32),
)


def attend(rank, q, own, kv):
    return pl.pallas_call(
        attend_kernel,
        out_shape=(jax.ShapeDtypeStruct((Q_ROWS, 2 * CHUNK), BF16), attend_state[0]),
        in_specs=[in_smem] + [in_vmem] * 3,
        out_specs=(in_vmem,) * 2,
        scratch_shapes=[pltpu.VMEM(leaf.shape, leaf.dtype) for leaf in attend_state],
        compiler_params=kernel_params,
        cost_estimate=work(33, 1_400_000_000),
        name="attend",
    )(rank, q, own, kv)


def attend_back(rank, q, do, lse, delta, dq, kv, kinds, own=None, first=False):
    outs = [jax.ShapeDtypeStruct((kind[0], KV_ROWS, CHUNK), BF16) for kind in kinds]
    operands = [kv]
    if own is not None:
        outs.append(jax.ShapeDtypeStruct(own.shape, BF16))
        operands.append(own)
    if first:
        outs.append(jax.ShapeDtypeStruct(lse.shape, F32))
    return pl.pallas_call(
        functools.partial(attend_back_kernel, kinds, own is not None, first),
        out_shape=(jax.ShapeDtypeStruct((Q_ROWS, 2 * CHUNK), F32),) + tuple(outs),
        in_specs=[in_smem] + [in_vmem] * (5 + len(operands)),
        out_specs=(in_vmem,) * (1 + len(outs)),
        compiler_params=kernel_params,
        cost_estimate=work(
            sum(kind[0] for kind in kinds) + (0 if own is None else 3), 1_950_000_000
        ),
        name="attend_back",
    )(rank, q, do, lse, delta, dq, *operands)


def reorder_kernel(order_ref, in_ref, out_ref):
    out_ref[...] = in_ref[...]


def reorder_blocks(order, values):
    block = (1,) + values.shape[1:]
    return pl.pallas_call(
        reorder_kernel,
        grid_spec=pltpu.PrefetchScalarGridSpec(
            num_scalar_prefetch=1,
            grid=(values.shape[0],),
            in_specs=[pl.BlockSpec(block, lambda i, order: (order[i], 0, 0))],
            out_specs=pl.BlockSpec(block, lambda i, order: (i, 0, 0)),
        ),
        out_shape=jax.ShapeDtypeStruct(values.shape, values.dtype),
        cost_estimate=pl.CostEstimate(
            flops=0, bytes_accessed=4 * values.size, transcendentals=0
        ),
        name="reorder_blocks",
    )(order, values)


def project_kernel(
    order_ref, near_ref, other_ref, weight_ref, cos_ref, sin_ref, normed_ref, q_ref, kv_ref, piece_ref
):
    half = HEAD_DIM // 2
    for group, ref in enumerate((near_ref, other_ref)):
        count = ref.shape[0]
        rows = ref.shape[1]
        values = ref[...].astype(F32).reshape(count * rows, ref.shape[2])
        inverse = lax.rsqrt(jnp.mean(values * values, axis=1, keepdims=True) + epsilon)
        normed = (values * inverse).astype(BF16)
        product = jnp.dot(normed, weight_ref[...], preferred_element_type=F32)
        for entry in range(count):
            block = order_ref[group * count + entry]
            at = pl.multiple_of(block * rows, rows)
            here = slice(entry * rows, (entry + 1) * rows)
            normed_ref[pl.ds(at, rows), :] = normed[here]
            turned = product[here].astype(BF16).astype(F32).T
            cosine = cos_ref[:, pl.ds(at, rows)]
            sine = sin_ref[:, pl.ds(at, rows)]
            for head in range(GROUP + 1):
                first = turned[head * HEAD_DIM : head * HEAD_DIM + half]
                second = turned[head * HEAD_DIM + half : (head + 1) * HEAD_DIM]
                rotated = jnp.concatenate(
                    [first * cosine - second * sine, second * cosine + first * sine], axis=0
                )
                if head < GROUP:
                    q_ref[head * HEAD_DIM : (head + 1) * HEAD_DIM, pl.ds(at, rows)] = (
                        rotated * (score_scale * log2e)
                    ).astype(BF16)
                else:
                    keys = rotated.astype(BF16)
            kv = jnp.concatenate([keys, turned[Q_ROWS + HEAD_DIM :].astype(BF16)], axis=0)
            kv_ref[:, pl.ds(at, rows)] = kv
            per_half = CHUNK // 2 // rows
            which = (block // per_half) & 1
            lane = (block // (2 * per_half)) * (CHUNK // 2) + (block % per_half) * rows
            piece_ref[which, :, pl.ds(pl.multiple_of(lane, rows), rows)] = kv


def project(order, near, other, weight, cosine, sine):
    tokens = 2 * CHUNK
    return pl.pallas_call(
        project_kernel,
        out_shape=(
            jax.ShapeDtypeStruct((tokens, near.shape[2]), BF16),
            jax.ShapeDtypeStruct((Q_ROWS, tokens), BF16),
            jax.ShapeDtypeStruct((KV_ROWS, tokens), BF16),
            jax.ShapeDtypeStruct((2, KV_ROWS, CHUNK), BF16),
        ),
        in_specs=[in_smem] + [in_vmem] * 5,
        out_specs=(in_vmem,) * 4,
        compiler_params=kernel_params,
        cost_estimate=pl.CostEstimate(
            flops=2 * tokens * 1536 * 384, bytes_accessed=8 * 2**20, transcendentals=0
        ),
        name="project",
    )(order, near, other, weight, cosine, sine)


FF_HERE = RANKS * FF_PIECE
PACK_ROWS = 3 * FF_PIECE


def ff_product_kernel(hidden_ref, grad_ref, middle_ref, cotangent_ref, out_ref):
    out_ref[:, : 2 * FF_HERE] = jnp.dot(
        hidden_ref[...].T, grad_ref[...], preferred_element_type=F32
    ).astype(BF16)
    down = jnp.dot(
        middle_ref[...].T, cotangent_ref[...], preferred_element_type=F32
    ).astype(BF16)
    for rank in range(down.shape[0] // FF_PIECE):
        for part in range(3):
            out_ref[
                rank * PACK_ROWS + part * FF_PIECE : rank * PACK_ROWS + (part + 1) * FF_PIECE,
                2 * FF_HERE :,
            ] = down[
                rank * FF_PIECE : (rank + 1) * FF_PIECE, part * FF_HERE : (part + 1) * FF_HERE
            ]


def ff_product(hidden, grad, middle, cotangent):
    rows, model = hidden.shape
    steps = 4
    return pl.pallas_call(
        ff_product_kernel,
        grid=(steps,),
        in_specs=[
            pl.BlockSpec((rows, model // steps), lambda i: (0, i)),
            pl.BlockSpec((rows, 2 * FF_HERE), lambda i: (0, 0)),
            pl.BlockSpec((rows, FF_HERE // steps), lambda i: (0, i)),
            pl.BlockSpec((rows, model), lambda i: (0, 0)),
        ],
        out_specs=pl.BlockSpec((model // steps, 3 * FF_HERE), lambda i: (i, 0)),
        out_shape=jax.ShapeDtypeStruct((model, 3 * FF_HERE), BF16),
        compiler_params=kernel_params,
        cost_estimate=pl.CostEstimate(
            flops=2 * rows * model * 3 * FF_HERE, bytes_accessed=16 * 2**20, transcendentals=0
        ),
        name="ff_product",
    )(hidden, grad, middle, cotangent)


def ff_finish_kernel(
    pieces_ref, gate_ref, up_ref, gain_ref, gate_out, up_out, down_out, gain_out
):
    count = pieces_ref.shape[0]
    lanes = 128
    width = count * lanes
    ranks = lanes // FF_PIECE
    row = lax.broadcasted_iota(jnp.int32, (width, width), 0)
    col = lax.broadcasted_iota(jnp.int32, (width, width), 1)
    source = (col % (count * FF_PIECE)) // FF_PIECE * lanes
    source = source + col // (count * FF_PIECE) * FF_PIECE + col % FF_PIECE
    turn = jnp.where(row == source, 1.0, 0.0).astype(BF16)
    gain = gain_ref[...]
    total = jnp.zeros_like(gain)
    for at, weight_ref, out_ref in ((0, gate_ref, gate_out), (FF_HERE, up_ref, up_out)):
        for group in range(RANKS // ranks):
            start = at + group * lanes
            mixed = jnp.concatenate(
                [pieces_ref[s, :, start : start + lanes] for s in range(count)], axis=1
            )
            product = jnp.dot(mixed, turn, preferred_element_type=F32)
            cols = slice(group * width, (group + 1) * width)
            total = total + jnp.sum(
                product * weight_ref[:, cols].astype(F32), axis=1, keepdims=True
            )
            out_ref[:, cols] = product * gain
    gain_out[...] = total
    for s in range(count):
        for part in range(3):
            down_out[
                s * FF_PIECE : (s + 1) * FF_PIECE, part * FF_HERE : (part + 1) * FF_HERE
            ] = pieces_ref[
                s, part * FF_PIECE : (part + 1) * FF_PIECE, 2 * FF_HERE :
            ].astype(F32)


def ff_finish(pieces, w_gate, w_up, gain):
    return pl.pallas_call(
        ff_finish_kernel,
        out_shape=(
            jax.ShapeDtypeStruct(w_gate.shape, F32),
            jax.ShapeDtypeStruct(w_up.shape, F32),
            jax.ShapeDtypeStruct((pieces.shape[0] * FF_PIECE, 3 * FF_HERE), F32),
            jax.ShapeDtypeStruct(gain.shape, F32),
        ),
        in_specs=[in_vmem] * 4,
        out_specs=(in_vmem,) * 4,
        compiler_params=kernel_params,
        cost_estimate=pl.CostEstimate(
            flops=2 * 96 * 8192 * 1024, bytes_accessed=8 * 2**20, transcendentals=0
        ),
        name="ff_finish",
    )(pieces, w_gate, w_up, gain)


def qkv_finish_kernel(
    pieces_ref, q_ref, k_ref, v_ref, gain_ref, q_out, k_out, v_out, o_out, gain_out
):
    count = pieces_ref.shape[0]
    gain = gain_ref[...]
    total = jnp.zeros_like(gain)
    at = 0
    for width, weight_ref, out_ref in (
        (Q_ROWS, q_ref, q_out),
        (HEAD_DIM, k_ref, k_out),
        (HEAD_DIM, v_ref, v_out),
        (Q_ROWS, None, o_out),
    ):
        product = jnp.concatenate(
            [pieces_ref[s, :, at : at + width].astype(F32) for s in range(count)], axis=1
        )
        at += width
        if weight_ref is None:
            out_ref[...] = product
        else:
            total = total + jnp.sum(
                product * weight_ref[...].astype(F32), axis=1, keepdims=True
            )
            out_ref[...] = product * gain
    gain_out[...] = total


def qkv_finish(pieces, w_query, w_key, w_value, gain):
    return pl.pallas_call(
        qkv_finish_kernel,
        out_shape=(
            jax.ShapeDtypeStruct(w_query.shape, F32),
            jax.ShapeDtypeStruct(w_key.shape, F32),
            jax.ShapeDtypeStruct(w_value.shape, F32),
            jax.ShapeDtypeStruct(w_query.shape, F32),
            jax.ShapeDtypeStruct(gain.shape, F32),
        ),
        in_specs=[in_vmem] * 5,
        out_specs=(in_vmem,) * 5,
        compiler_params=kernel_params,
        cost_estimate=pl.CostEstimate(
            flops=10**6, bytes_accessed=4 * 2**20, transcendentals=0
        ),
        name="qkv_finish",
    )(pieces, w_query, w_key, w_value, gain)


def inverse_rms(values):
    return lax.rsqrt(jnp.mean(values * values, axis=-1, keepdims=True) + epsilon)


def norm_back(scaled_grad, normed, inverse):
    return inverse * (scaled_grad - normed * jnp.mean(scaled_grad * normed, axis=-1, keepdims=True))


def rotate(values, cosine_table, sine_table, direction):
    halves = HEAD_DIM // 2
    first_half = values[..., :halves, :]
    second_half = values[..., halves:, :]
    return jnp.concatenate(
        [
            first_half * cosine_table - direction * second_half * sine_table,
            second_half * cosine_table + direction * first_half * sine_table,
        ],
        axis=-2,
    )


def after(values, *done):
    return lax.optimization_barrier((values,) + done)[0]


def gather(values, axis_name, axis=0):
    return lax.all_gather(values, axis_name, axis=axis, tiled=True)


def on_device(
    tokens,
    norm1_gain,
    w_query,
    w_key,
    w_value,
    w_out,
    norm2_gain,
    w_gate,
    w_up,
    w_down,
    out_cotangent,
):
    seq_count = lax.axis_size("seq")
    wide_count = lax.axis_size("wide")
    seq_index = lax.axis_index("seq")
    wide_index = lax.axis_index("wide")
    rank = wide_index.astype(jnp.int32).reshape(1)
    model = tokens.shape[1]
    ff = w_gate.shape[1]

    mirror = [
        (s * wide_count + w, s * wide_count + (wide_count - 1 - w if s >= seq_count // 2 else w))
        for s in range(seq_count)
        for w in range(wide_count)
    ]

    def swap(values):
        return lax.ppermute(values, ("seq", "wide"), mirror)

    def over_seq(source_to_target):
        return [(s, source_to_target(s)) for s in range(seq_count)]

    def y_shift(step):
        return over_seq(lambda s: (s + 2 * step) % seq_count)

    other_core = over_seq(lambda s: s ^ 1)

    def scatter_cores(partial):
        pairs_of = partial.reshape(SIDE, 2, partial.shape[0] // (2 * SIDE), partial.shape[1])
        sent = lax.dynamic_index_in_dim(pairs_of, 1 - core_index, 1, keepdims=False)
        kept = lax.dynamic_index_in_dim(pairs_of, core_index, 1, keepdims=False)
        return kept.astype(F32) + lax.ppermute(sent, "seq", other_core).astype(F32)

    def scatter_y(kept):
        total = lax.dynamic_index_in_dim(kept, y_index, 0, keepdims=False)
        for step in (1, 2, 3):
            sent = lax.dynamic_index_in_dim(kept, (y_index - step) % SIDE, 0, keepdims=False)
            total = total + lax.ppermute(sent.astype(BF16), "seq", y_shift(-step)).astype(F32)
        return total

    def gather_near(values):
        stack = jnp.stack(
            [values] + [lax.ppermute(values, "seq", y_shift(step)) for step in (1, 2, 3)]
        )
        return stack, lax.ppermute(stack, "seq", other_core)

    def near_slot(block):
        return ((block % 2) ^ core_index) * SIDE + (y_index - block // 2) % SIDE

    y_index = seq_index // 2
    core_index = seq_index % 2
    far_order = jnp.stack(
        [
            2 * ((y_index - slot % SIDE) % SIDE) + ((slot // SIDE) ^ core_index)
            for slot in range(seq_count)
        ]
    ).astype(jnp.int32)
    near_order = jnp.stack([near_slot(i) for i in range(seq_count)]).astype(jnp.int32)

    gain_one = norm1_gain.astype(F32)[:, None]
    gain_two = norm2_gain.astype(F32)[:, None]
    q_cols = lax.dynamic_slice_in_dim(w_query, seq_index * Q_ROWS, Q_ROWS, 1)
    k_cols = lax.dynamic_slice_in_dim(w_key, seq_index * HEAD_DIM, HEAD_DIM, 1)
    v_cols = lax.dynamic_slice_in_dim(w_value, seq_index * HEAD_DIM, HEAD_DIM, 1)
    qkv_shard = (jnp.concatenate([q_cols, k_cols, v_cols], axis=1).astype(F32) * gain_one).astype(
        BF16
    )

    def ff_cols(weight):
        pieces = weight.reshape(weight.shape[0], wide_count, seq_count, FF_PIECE)
        return lax.dynamic_index_in_dim(pieces, seq_index, 2, keepdims=False).reshape(
            weight.shape[0], wide_count * FF_PIECE
        )

    out_full = gather(w_out, "wide")
    qkv_weight = lax.all_to_all(
        jnp.broadcast_to(qkv_shard[None], (wide_count,) + qkv_shard.shape),
        "wide",
        split_axis=0,
        concat_axis=0,
        tiled=True,
    ).reshape(model, -1)
    tokens_here, qkv_weight = lax.optimization_barrier((swap(tokens), qkv_weight))
    tokens_near, tokens_other = gather_near(tokens_here)
    cotangent = after(swap(after(out_cotangent, tokens_here)), tokens_other)
    cotangent_rows = reorder_blocks(
        near_order, jnp.concatenate(gather_near(cotangent))
    ).reshape(-1, model)

    gate_up_shard = (
        jnp.concatenate([ff_cols(w_gate), ff_cols(w_up)], axis=1).astype(F32) * gain_two
    ).astype(BF16)
    down_shard = lax.dynamic_slice_in_dim(w_down, seq_index * FF_PIECE, FF_PIECE, 0)
    half = wide_count * FF_PIECE
    late_shard = jnp.concatenate(
        [
            gate_up_shard,
            down_shard.reshape(FF_PIECE, -1, half)
            .transpose(1, 0, 2)
            .reshape(gate_up_shard.shape[0], -1),
        ],
        axis=1,
    )

    row = jnp.arange(2 * CHUNK, dtype=jnp.int32)
    positions = jnp.where(
        row < CHUNK,
        2 * wide_index * CHUNK + row,
        (CHUNKS - 1 - 2 * wide_index) * CHUNK + row - CHUNK,
    ).astype(F32)
    frequency = jnp.exp(
        jnp.arange(HEAD_DIM // 2).astype(F32) * (-2.0 * math.log(rope_base) / HEAD_DIM)
    )
    angles = frequency[:, None] * positions[None, :]
    cosine_table, sine_table = jnp.cos(angles), jnp.sin(angles)

    normed_one_all, q, kv, kv_pieces = project(
        far_order, tokens_near, tokens_other, qkv_weight, cosine_table, sine_table
    )

    def wide_shift(x_step, z_step):
        return [
            (
                x * SIDE + z,
                (x + x_step) % SIDE * SIDE + (z + z_step) % SIDE,
            )
            for x in range(SIDE)
            for z in range(SIDE)
        ]

    def move(values, x_step, z_step):
        return lax.ppermute(values, "wide", wide_shift(x_step, z_step))

    def leg(values, axis, step):
        return move(values, 0, step) if axis == 0 else move(values, step, 0)

    def pick(values, which):
        quarter = CHUNK // 2
        return jnp.concatenate(
            [
                values[:, which * quarter : (which + 1) * quarter],
                values[:, CHUNK + which * quarter : CHUNK + (which + 1) * quarter],
            ],
            axis=1,
        )[None]

    kv_all = lax.all_gather(kv_pieces, "wide", axis=0, tiled=False)
    kv_all, cotangent_rows, out_full, late_shard = lax.optimization_barrier(
        (kv_all, cotangent_rows, out_full, late_shard)
    )
    late_full = gather(late_shard, "wide")
    gate_up = late_full[:, : 2 * half]
    down = (
        late_full[:, 2 * half : 3 * half]
        .reshape(wide_count, -1, FF_PIECE, half)
        .transpose(0, 2, 1, 3)
        .reshape(half, model)
    )

    def kind_of(axis, first, second, count):
        if axis == 0:
            return (count, second, first, 0, 1, 0)
        return (count, first, second, 1, 0, 1)

    line_kinds = [kind_of(t, step, 0, 1) for t in range(2) for step in (1, 2, 3)]
    near_kinds = [kind_of(t, 0, step, SIDE) for t in range(2) for step in (1, 3)]
    far_kinds = [kind_of(t, 0, 2, SIDE) for t in range(2)]
    attended, log_total = attend(rank, q, kv, kv_all)
    attended_tok = lax.all_to_all(attended, "seq", split_axis=1, concat_axis=0, tiled=True)
    middle_grad = dot(cotangent_rows, down, 1, 1)

    inputs = tokens_here.astype(F32)
    inverse_one = inverse_rms(inputs)
    normed_one = inputs * inverse_one
    residual = inputs + dot(attended_tok, out_full, 0, 0)
    inverse_two = inverse_rms(residual)
    normed_two = residual * inverse_two
    normed_two_all = gather(normed_two.astype(BF16), "seq")
    gate_up_pre = dot(normed_two_all, gate_up, 1, 0)
    gate_pre, up_pre = gate_up_pre[:, :half], gate_up_pre[:, half:]
    sigmoid_gate = jax.nn.sigmoid(gate_pre)
    activated = gate_pre * sigmoid_gate
    middle = (activated * up_pre).astype(BF16)
    up_grad = (middle_grad * activated).astype(BF16)
    gate_grad = (
        middle_grad * up_pre * sigmoid_gate * (1.0 + gate_pre * (1.0 - sigmoid_gate))
    ).astype(BF16)
    gate_up_grad = jnp.concatenate([gate_grad, up_grad], axis=1)
    scaled_two = lax.psum_scatter(
        dot(gate_up_grad, gate_up, 1, 1).astype(BF16), "seq", scatter_dimension=0, tiled=True
    ).astype(F32)
    down_cores = scatter_cores(dot(middle, down, 1, 0).astype(BF16))
    scaled_two = after(scaled_two, down_cores)
    residual_grad = cotangent.astype(F32) + norm_back(scaled_two, normed_two, inverse_two)
    branch_grad = residual_grad.astype(BF16)
    mixed_grad = dot(out_full, branch_grad, 1, 1).astype(BF16)
    head_grad = lax.all_to_all(mixed_grad, "seq", split_axis=0, concat_axis=1, tiled=True)

    ff_rows = lax.psum_scatter(
        ff_product(normed_two_all, gate_up_grad, middle, cotangent_rows),
        "wide",
        scatter_dimension=0,
        tiled=True,
    )
    attended_all = gather(after(attended, scaled_two), "seq")
    branch_grad_all = gather(branch_grad, "seq")
    down_part = scatter_y(after(down_cores, head_grad))

    def add(first, second):
        return (first.astype(F32) + second.astype(F32)).astype(BF16)

    q_grad, *near_grads, row_delta = attend_back(
        rank, q, head_grad, log_total, attended, log_total, kv_all, near_kinds, first=True
    )
    near_back = [
        (leg(near_grads[2 * t], 1 - t, -1), leg(near_grads[2 * t + 1], 1 - t, 1))
        for t in range(2)
    ]
    q_grad = after(q_grad, down_part)
    back = (rank, q, head_grad, log_total, row_delta)
    q_grad, *far_grads = attend_back(*back, q_grad, kv_all, far_kinds)
    q_grad, far_grads[0], far_grads[1], *_ = lax.optimization_barrier(
        (q_grad, far_grads[0], far_grads[1], *near_back[0], *near_back[1])
    )
    far_back = [leg(far_grads[t], 1 - t, 2) for t in range(2)]
    q_grad_rot, *line_grads = attend_back(*back, q_grad, kv_all, line_kinds, kv)
    ff_all = lax.all_gather(after(ff_rows, q_grad_rot), "seq", axis=0, tiled=False)
    branch_grad_cols = lax.dynamic_slice_in_dim(
        after(branch_grad_all, q_grad_rot), seq_index * Q_ROWS, Q_ROWS, 1
    )
    out_product = dot(attended_all, branch_grad_cols, 1, 0).astype(BF16)
    own_grad = line_grads[-1]
    piece_grads = []
    for t in range(2):
        arrived = (
            near_back[t][0].astype(F32) + near_back[t][1].astype(F32) + far_back[t].astype(F32)
        )
        total = pick(own_grad, t).astype(F32) + arrived[:1]
        for step in (1, 2, 3):
            sent = (line_grads[3 * t + step - 1].astype(F32) + arrived[step : step + 1]).astype(
                BF16
            )
            total = total + leg(sent, t, -step).astype(F32)
        piece_grads.append(total[0])
    quarter = CHUNK // 2
    kv_grad = jnp.concatenate(
        [
            piece_grads[0][:, :quarter],
            piece_grads[1][:, :quarter],
            piece_grads[0][:, quarter:],
            piece_grads[1][:, quarter:],
        ],
        axis=1,
    )

    qk_grad = rotate(
        jnp.concatenate([q_grad_rot, kv_grad[:HEAD_DIM]], axis=0).reshape(
            GROUP + 1, HEAD_DIM, 2 * CHUNK
        ),
        cosine_table,
        sine_table,
        -1.0,
    ).reshape(Q_ROWS + HEAD_DIM, 2 * CHUNK)
    qkv_grad = jnp.concatenate([qk_grad.astype(BF16), kv_grad[HEAD_DIM:].astype(BF16)], axis=0)
    output = swap((residual + after(down_part, qkv_grad)).astype(BF16))
    scaled_one_cores = scatter_cores(dot(qkv_grad, qkv_weight, 0, 1).astype(BF16))
    scaled_one = scatter_y(scaled_one_cores)
    qkv_product = jnp.concatenate(
        [
            dot(normed_one_all, after(qkv_grad, scaled_one_cores), 0, 1).astype(BF16),
            out_product,
        ],
        axis=1,
    )
    qkv_parts = lax.all_to_all(
        qkv_product.reshape(wide_count, -1, qkv_product.shape[1]),
        "wide",
        split_axis=0,
        concat_axis=0,
        tiled=True,
    )
    qkv_rows = jnp.sum(qkv_parts.astype(F32), axis=0).astype(BF16)
    tokens_grad = swap(
        (residual_grad + norm_back(scaled_one, normed_one, inverse_one)).astype(BF16)
    )
    qkv_all = lax.all_gather(qkv_rows, "seq", axis=0, tiled=False)
    gate_grad_out, up_grad_out, down_grad, gain_two_grad = ff_finish(
        ff_all, w_gate, w_up, gain_two
    )

    q_grad_out, k_grad_out, v_grad_out, out_grad, gain_one_grad = qkv_finish(
        qkv_all, w_query, w_key, w_value, gain_one
    )
    return (
        output,
        tokens_grad,
        gain_one_grad[:, 0],
        q_grad_out,
        k_grad_out,
        v_grad_out,
        out_grad,
        gain_two_grad[:, 0],
        gate_grad_out,
        up_grad_out,
        down_grad,
    )


def solution(mesh):
    placed = (
        P(("wide", "seq"), None),
        P("wide"),
        P("wide", None),
        P("wide", None),
        P("wide", None),
        P("wide", None),
        P("wide"),
        P("wide", None),
        P("wide", None),
        P("wide", None),
        P(("wide", "seq"), None),
    )
    return jax.shard_map(
        on_device,
        mesh=mesh,
        in_specs=placed,
        out_specs=(
            P(("wide", "seq"), None),
            P(("wide", "seq"), None),
            P("wide"),
            P("wide", None),
            P("wide", None),
            P("wide", None),
            P("wide", None),
            P("wide"),
            P("wide", None),
            P("wide", None),
            P("wide", None),
        ),
        check_vma=False,
    )
```

```python
import functools
import math

import jax
import jax.numpy as jnp
from jax import lax
from jax.experimental import pallas as pl
from jax.experimental.pallas import tpu as pltpu
from jax.sharding import PartitionSpec as P

HEAD_DIM = 96
CHUNK = 512
CHUNKS = 32
SIDE = 4
RANKS = SIDE * SIDE
GROUP = 2
Q_ROWS = GROUP * HEAD_DIM
KV_ROWS = 2 * HEAD_DIM
FF_PIECE = 32

epsilon = 1e-05
rope_base = 100000.0
negative = -1e30
log2e = math.log2(math.e)
score_scale = 1.0 / math.sqrt(HEAD_DIM)

F32 = jnp.float32
BF16 = jnp.bfloat16


def dot(left, right, left_dim, right_dim):
    return lax.dot_general(
        left, right, (((left_dim,), (right_dim,)), ((), ())), preferred_element_type=F32
    )


def causal_mask():
    keys = lax.broadcasted_iota(jnp.int32, (CHUNK, CHUNK), 0)
    rows = lax.broadcasted_iota(jnp.int32, (CHUNK, CHUNK), 1)
    return keys <= rows


class Place:
    def __init__(self, rank, piece):
        first = rank < RANKS // 2
        self.early = jnp.where(first, 2 * rank, CHUNKS - 1 - 2 * rank)
        self.early_at = pl.multiple_of(jnp.where(first, 0, piece), piece)
        self.late_at = pl.multiple_of(jnp.where(first, piece, 0), piece)


def source_rank(rank, kind, entry):
    x_back, z_back, x_step, z_step = kind[1:5]
    x = (rank // SIDE - x_back - x_step * entry) & (SIDE - 1)
    z = (rank % SIDE - z_back - z_step * entry) & (SIDE - 1)
    return x * SIDE + z


def for_pieces(rank, kinds, early_only, late_only, before, done):
    here = Place(rank, CHUNK)
    for index, kind in enumerate(kinds):

        def body(entry, carry, index=index, kind=kind):
            source = source_rank(rank, kind, entry)
            there = Place(source, CHUNK // 2)
            before(index, entry)
            pl.when(there.early < here.early)(lambda: early_only(index, entry, there))
            pl.when(there.early > here.early)(lambda: late_only(index, entry, here))
            done(index, entry)
            return carry

        lax.fori_loop(0, kind[0], body, 0)


def attend_blocks(keys_t, values, chains, q_ref, max_s, sum_s, acc_s, diagonal=False):
    rows = [slice(head * HEAD_DIM, (head + 1) * HEAD_DIM) for head, _ in chains]
    lanes = [slice(head, head + 1) for head, _ in chains]
    cols = [c for _, c in chains]
    every = range(len(chains))
    old_max = [max_s[lanes[i], cols[i]] for i in every]
    old_sum = [sum_s[lanes[i], cols[i]] for i in every]
    old_acc = [acc_s[rows[i], cols[i]] for i in every]
    scores = [
        jnp.dot(keys_t, q_ref[rows[i], cols[i]], preferred_element_type=F32) for i in every
    ]
    if diagonal:
        scores = [jnp.where(causal_mask(), one, negative) for one in scores]
    new_max = [
        jnp.maximum(old_max[i], jnp.max(scores[i], axis=0, keepdims=True)) for i in every
    ]
    factor = [jnp.exp2(old_max[i] - new_max[i]) for i in every]
    probs = [jnp.exp2(scores[i] - new_max[i]) for i in every]
    ones = jnp.ones((16, values.shape[1]), BF16)
    values = jnp.concatenate([values, ones], axis=0)
    product = [
        jnp.dot(values, probs[i].astype(BF16), preferred_element_type=F32) for i in every
    ]
    new_sum = [
        old_sum[i] * factor[i] + product[i][HEAD_DIM : HEAD_DIM + 1, :] for i in every
    ]
    new_acc = [old_acc[i] * factor[i] + product[i][:HEAD_DIM, :] for i in every]
    for i in every:
        max_s[lanes[i], cols[i]] = new_max[i]
        sum_s[lanes[i], cols[i]] = new_sum[i]
        acc_s[rows[i], cols[i]] = new_acc[i]


key_rows = slice(0, HEAD_DIM)
value_rows = slice(HEAD_DIM, 2 * HEAD_DIM)


def attend_kernel(
    rank_ref, q_ref, own_ref, kv_in, o_ref, lse_ref, max_s, sum_s, acc_s, kv_ref, arrived
):
    rank = rank_ref[0]

    def fetch(step):
        source = (rank + step) & (RANKS - 1)
        return pltpu.make_async_copy(kv_in.at[source], kv_ref.at[step], arrived.at[step])

    def start(step, carry):
        fetch(step).start()
        return carry

    lax.fori_loop(1, RANKS, start, 0)
    here = Place(rank, CHUNK)
    max_s[...] = jnp.full_like(max_s, negative)
    sum_s[...] = jnp.zeros_like(sum_s)
    acc_s[...] = jnp.zeros_like(acc_s)

    def blocks(keys, values, col_list, diagonal=False):
        chains = [(head, cols) for cols in col_list for head in range(GROUP)]
        attend_blocks(keys.T, values, chains, q_ref, max_s, sum_s, acc_s, diagonal)

    parts = [slice(part * CHUNK, (part + 1) * CHUNK) for part in range(2)]
    late = pl.ds(here.late_at, CHUNK)
    for cols in parts:
        blocks(own_ref[key_rows, cols], own_ref[value_rows, cols], [cols], True)
    early = pl.ds(here.early_at, CHUNK)
    blocks(own_ref[key_rows, early], own_ref[value_rows, early], [late])

    def body(step, carry):
        source = (rank + step) & (RANKS - 1)
        there = Place(source, CHUNK // 2)
        fetch(step).wait()

        @pl.when(there.early < here.early)
        def _():
            cols = pl.ds(there.early_at, CHUNK // 2)
            keys, values = (
                jnp.concatenate([kv_ref[step, 0, rows, cols], kv_ref[step, 1, rows, cols]], 1)
                for rows in (key_rows, value_rows)
            )
            blocks(keys, values, [pl.ds(i * 512, 512) for i in range(2 * CHUNK // 512)])

        @pl.when(there.early > here.early)
        def _():
            keys, values = (
                jnp.concatenate([kv_ref[step, 0, rows, :], kv_ref[step, 1, rows, :]], 1)
                for rows in (key_rows, value_rows)
            )
            blocks(
                keys,
                values,
                [
                    pl.ds(pl.multiple_of(here.late_at + i * 256, 256), 256)
                    for i in range(CHUNK // 256)
                ],
            )

        return carry

    lax.fori_loop(1, RANKS, body, 0)
    for head in range(GROUP):
        rows = slice(head * HEAD_DIM, (head + 1) * HEAD_DIM)
        total = sum_s[head : head + 1, :]
        o_ref[rows, :] = (acc_s[rows, :] / total).astype(BF16)
        lse_ref[head : head + 1, :] = max_s[head : head + 1, :] + jnp.log2(total)


def back_blocks(keys, keys_t, values_t, refs, chains, sums, diagonal=False):
    q_ref, do_ref, lse_ref, delta_ref, dq_s = refs
    rows = [slice(head * HEAD_DIM, (head + 1) * HEAD_DIM) for head, _ in chains]
    lanes = [slice(head, head + 1) for head, _ in chains]
    cols = [c for _, c in chains]
    every = range(len(chains))
    q = [q_ref[rows[i], cols[i]] for i in every]
    do = [do_ref[rows[i], cols[i]] for i in every]
    old = [dq_s[rows[i], cols[i]] for i in every]
    scores = [jnp.dot(keys_t, q[i], preferred_element_type=F32) for i in every]
    dp = [jnp.dot(values_t, do[i], preferred_element_type=F32) for i in every]
    probs = [jnp.exp2(scores[i] - lse_ref[lanes[i], cols[i]]) for i in every]
    if diagonal:
        probs = [jnp.where(causal_mask(), one, 0.0) for one in probs]
    ds = [(probs[i] * (dp[i] - delta_ref[lanes[i], cols[i]])).astype(BF16) for i in every]
    for i in every:
        dk = dot(q[i], ds[i], 1, 1)
        dv = dot(do[i], probs[i].astype(BF16), 1, 1)
        sums = (dk, dv) if sums is None else (sums[0] + dk, sums[1] + dv)
    new = [old[i] + jnp.dot(keys, ds[i], preferred_element_type=F32) for i in every]
    for i in every:
        dq_s[rows[i], cols[i]] = new[i]
    return sums


def attend_back_kernel(
    kinds, own, first, rank_ref, q_ref, do_ref, lse_ref, delta_in, dq_in, kv_in, *refs
):
    count = len(kinds)
    refs, (kv_ref, out_ref, arrived, left) = refs[:-4], refs[-4:]
    rank = rank_ref[0]
    begin = [sum(kind[0] for kind in kinds[:index]) for index in range(count)]

    def fetch(index, entry):
        slot = begin[index] + entry
        source = source_rank(rank, kinds[index], entry)
        return pltpu.make_async_copy(
            kv_in.at[source, kinds[index][5]], kv_ref.at[slot], arrived.at[slot]
        )

    def send(index, entry):
        slot = begin[index] + entry
        return pltpu.make_async_copy(out_ref.at[slot], outs[index].at[entry], left.at[slot])

    for index, kind in enumerate(kinds):

        def start(entry, carry, index=index):
            fetch(index, entry).start()
            return carry

        lax.fori_loop(0, kind[0], start, 0)
    if own:
        own_ref, refs = refs[0], refs[1:]
    dq_s, outs = refs[0], refs[1 : 1 + count]
    if first:
        delta_ref = refs[-1]
        for head in range(GROUP):
            rows = slice(head * HEAD_DIM, (head + 1) * HEAD_DIM)
            delta_ref[head : head + 1, :] = jnp.sum(
                do_ref[rows, :].astype(F32) * delta_in[rows, :].astype(F32), axis=0, keepdims=True
            )
        dq_s[...] = jnp.zeros_like(dq_s)
    else:
        delta_ref = delta_in
        dq_s[...] = dq_in[...]
    shared = (q_ref, do_ref, lse_ref, delta_ref, dq_s)

    def early_only(index, entry, there):
        slot = begin[index] + entry
        cols = pl.ds(there.early_at, CHUNK // 2)
        keys = kv_ref[slot, key_rows, cols]
        keys_t = keys.T
        values_t = kv_ref[slot, value_rows, cols].T
        col_list = [pl.ds(i * 256, 256) for i in range(2 * CHUNK // 256)]
        sums = back_blocks(
            keys,
            keys_t,
            values_t,
            shared,
            [(head, cols) for cols in col_list for head in range(GROUP)],
            None,
        )
        dk, dv = sums
        out_ref[slot, key_rows, cols] = (dk * math.log(2.0)).astype(BF16)
        out_ref[slot, value_rows, cols] = dv.astype(BF16)
        out_ref[slot, :, pl.ds(there.late_at, CHUNK // 2)] = jnp.zeros((KV_ROWS, CHUNK // 2), BF16)

    def late_only(index, entry, here):
        slot = begin[index] + entry
        keys = kv_ref[slot, key_rows, :]
        keys_t = keys.T
        values_t = kv_ref[slot, value_rows, :].T
        col_list = [
            pl.ds(pl.multiple_of(here.late_at + i * 256, 256), 256) for i in range(CHUNK // 256)
        ]
        sums = back_blocks(
            keys,
            keys_t,
            values_t,
            shared,
            [(head, cols) for cols in col_list for head in range(GROUP)],
            None,
        )
        dk, dv = sums
        out_ref[slot, key_rows, :] = (dk * math.log(2.0)).astype(BF16)
        out_ref[slot, value_rows, :] = dv.astype(BF16)

    if own:
        own_out = refs[1 + count]
        here = Place(rank_ref[0], CHUNK)
        early = pl.ds(here.early_at, CHUNK)
        late = pl.ds(here.late_at, CHUNK)

        def block(key_cols, row_cols, sums, diagonal):
            keys = own_ref[key_rows, key_cols]
            keys_t = keys.T
            values_t = own_ref[value_rows, key_cols].T
            chains = [(head, row_cols) for head in range(GROUP)]
            return back_blocks(keys, keys_t, values_t, shared, chains, sums, diagonal)

        def store(cols, sums):
            dk, dv = sums
            own_out[key_rows, cols] = (dk * math.log(2.0)).astype(BF16)
            own_out[value_rows, cols] = dv.astype(BF16)

        store(early, block(early, late, block(early, early, None, True), False))
        store(late, block(late, late, None, True))

    for_pieces(
        rank,
        kinds,
        early_only,
        late_only,
        lambda index, entry: fetch(index, entry).wait(),
        lambda index, entry: send(index, entry).start(),
    )
    for index, kind in enumerate(kinds):

        def finish(entry, carry, index=index):
            send(index, entry).wait()
            return carry

        lax.fori_loop(0, kind[0], finish, 0)
    if own:
        dq_s[...] = dq_s[...] * score_scale


in_vmem = pl.BlockSpec(memory_space=pltpu.VMEM)
in_smem = pl.BlockSpec(memory_space=pltpu.SMEM)
anywhere = pl.BlockSpec(memory_space=pl.ANY)
kernel_params = pltpu.CompilerParams(vmem_limit_bytes=56 * 1024 * 1024)


def work(units, flops):
    return pl.CostEstimate(
        flops=units * flops, bytes_accessed=2**20, transcendentals=units * GROUP * CHUNK * CHUNK
    )


attend_state = (
    jax.ShapeDtypeStruct((GROUP, 2 * CHUNK), F32),
    jax.ShapeDtypeStruct((GROUP, 2 * CHUNK), F32),
    jax.ShapeDtypeStruct((Q_ROWS, 2 * CHUNK), F32),
)


def attend(rank, q, own, kv):
    return pl.pallas_call(
        attend_kernel,
        out_shape=(jax.ShapeDtypeStruct((Q_ROWS, 2 * CHUNK), BF16), attend_state[0]),
        in_specs=[in_smem, in_vmem, in_vmem, anywhere],
        out_specs=(in_vmem,) * 2,
        scratch_shapes=[pltpu.VMEM(leaf.shape, leaf.dtype) for leaf in attend_state]
        + [pltpu.VMEM(kv.shape, kv.dtype), pltpu.SemaphoreType.DMA((RANKS,))],
        compiler_params=kernel_params,
        cost_estimate=work(33, 1_400_000_000),
        name="attend",
    )(rank, q, own, kv)


def attend_back(rank, q, do, lse, delta, dq, kv, kinds, own=None, first=False):
    outs = [jax.ShapeDtypeStruct((kind[0], KV_ROWS, CHUNK), BF16) for kind in kinds]
    operands = [kv]
    pieces = sum(kind[0] for kind in kinds)
    if own is not None:
        outs.append(jax.ShapeDtypeStruct(own.shape, BF16))
        operands.append(own)
    if first:
        outs.append(jax.ShapeDtypeStruct(lse.shape, F32))
    return pl.pallas_call(
        functools.partial(attend_back_kernel, kinds, own is not None, first),
        out_shape=(jax.ShapeDtypeStruct((Q_ROWS, 2 * CHUNK), F32),) + tuple(outs),
        in_specs=[in_smem] + [in_vmem] * 5 + [anywhere] + [in_vmem] * (len(operands) - 1),
        out_specs=(in_vmem,) + (anywhere,) * len(kinds) + (in_vmem,) * (len(outs) - len(kinds)),
        scratch_shapes=[
            pltpu.VMEM((max(pieces, 1), KV_ROWS, CHUNK), BF16),
            pltpu.VMEM((max(pieces, 1), KV_ROWS, CHUNK), BF16),
            pltpu.SemaphoreType.DMA((max(pieces, 1),)),
            pltpu.SemaphoreType.DMA((max(pieces, 1),)),
        ],
        compiler_params=kernel_params,
        cost_estimate=work(
            sum(kind[0] for kind in kinds) + (0 if own is None else 3), 1_950_000_000
        ),
        name="attend_back",
    )(rank, q, do, lse, delta, dq, *operands)


def reorder_kernel(order_ref, near_ref, other_ref, out_ref):
    from_other = order_ref[pl.program_id(0)] >= SIDE

    @pl.when(from_other)
    def _():
        out_ref[...] = other_ref[...]

    @pl.when(jnp.logical_not(from_other))
    def _():
        out_ref[...] = near_ref[...]


def reorder_blocks(order, near, other):
    block = (1,) + near.shape[1:]
    spec = pl.BlockSpec(block, lambda i, order: (order[i] & (SIDE - 1), 0, 0))
    return pl.pallas_call(
        reorder_kernel,
        grid_spec=pltpu.PrefetchScalarGridSpec(
            num_scalar_prefetch=1,
            grid=(2 * SIDE,),
            in_specs=[spec, spec],
            out_specs=pl.BlockSpec(block, lambda i, order: (i, 0, 0)),
        ),
        out_shape=jax.ShapeDtypeStruct((2 * SIDE,) + near.shape[1:], near.dtype),
        cost_estimate=pl.CostEstimate(flops=0, bytes_accessed=12 * near.size, transcendentals=0),
        name="reorder_blocks",
    )(order, near, other)


def project_kernel(
    order_ref, near_ref, other_ref, weight_ref, cos_ref, sin_ref, normed_ref, q_ref, kv_ref, piece_ref
):
    half = HEAD_DIM // 2
    for group, ref in enumerate((near_ref, other_ref)):
        count = ref.shape[0]
        rows = ref.shape[1]
        values = ref[...].astype(F32).reshape(count * rows, ref.shape[2])
        inverse = lax.rsqrt(jnp.mean(values * values, axis=1, keepdims=True) + epsilon)
        normed = (values * inverse).astype(BF16)
        product = jnp.dot(
            normed, weight_ref[:, : Q_ROWS + KV_ROWS], preferred_element_type=F32
        )
        for entry in range(count):
            block = order_ref[group * count + entry]
            at = pl.multiple_of(block * rows, rows)
            here = slice(entry * rows, (entry + 1) * rows)
            normed_ref[pl.ds(at, rows), :] = normed[here]
            turned = product[here].astype(BF16).astype(F32).T
            cosine = cos_ref[:, pl.ds(at, rows)]
            sine = sin_ref[:, pl.ds(at, rows)]
            for head in range(GROUP + 1):
                first = turned[head * HEAD_DIM : head * HEAD_DIM + half]
                second = turned[head * HEAD_DIM + half : (head + 1) * HEAD_DIM]
                rotated = jnp.concatenate(
                    [first * cosine - second * sine, second * cosine + first * sine], axis=0
                )
                if head < GROUP:
                    q_ref[head * HEAD_DIM : (head + 1) * HEAD_DIM, pl.ds(at, rows)] = (
                        rotated * (score_scale * log2e)
                    ).astype(BF16)
                else:
                    keys = rotated.astype(BF16)
            kv = jnp.concatenate([keys, turned[Q_ROWS + HEAD_DIM :].astype(BF16)], axis=0)
            kv_ref[:, pl.ds(at, rows)] = kv
            per_half = CHUNK // 2 // rows
            which = (block // per_half) & 1
            lane = (block // (2 * per_half)) * (CHUNK // 2) + (block % per_half) * rows
            piece_ref[which, :, pl.ds(pl.multiple_of(lane, rows), rows)] = kv


def project(order, near, other, weight, cosine, sine):
    tokens = 2 * CHUNK
    return pl.pallas_call(
        project_kernel,
        out_shape=(
            jax.ShapeDtypeStruct((tokens, near.shape[2]), BF16),
            jax.ShapeDtypeStruct((Q_ROWS, tokens), BF16),
            jax.ShapeDtypeStruct((KV_ROWS, tokens), BF16),
            jax.ShapeDtypeStruct((2, KV_ROWS, CHUNK), BF16),
        ),
        in_specs=[in_smem] + [in_vmem] * 5,
        out_specs=(in_vmem,) * 4,
        compiler_params=kernel_params,
        cost_estimate=pl.CostEstimate(
            flops=2 * tokens * 1536 * 384, bytes_accessed=8 * 2**20, transcendentals=0
        ),
        name="project",
    )(order, near, other, weight, cosine, sine)


FF_HERE = RANKS * FF_PIECE
PACK_ROWS = 3 * FF_PIECE


def unpack_down(weight_ref, down_s):
    for rank in range(RANKS):
        for part in range(3):
            start = rank * PACK_ROWS + part * FF_PIECE
            down_s[
                rank * FF_PIECE : (rank + 1) * FF_PIECE, part * FF_HERE : (part + 1) * FF_HERE
            ] = weight_ref[start : start + FF_PIECE, 2 * FF_HERE :]


def feed_kernel(hidden_ref, weight_ref, cotangent_ref, middle_ref, grad_ref, back_ref, down_s):
    rows = middle_ref.shape[0]
    unpack_down(weight_ref, down_s)
    hidden = hidden_ref[...].reshape(rows, hidden_ref.shape[2])
    weight = weight_ref[:, : 2 * FF_HERE]
    product = jnp.dot(hidden, weight, preferred_element_type=F32)
    middle_grad = dot(cotangent_ref[...], down_s[...], 1, 1)
    gate, up = product[:, :FF_HERE], product[:, FF_HERE:]
    sigmoid = 1.0 / (1.0 + jnp.exp(-gate))
    active = gate * sigmoid
    middle_ref[...] = (active * up).astype(BF16)
    grad_ref[:, FF_HERE:] = (middle_grad * active).astype(BF16)
    grad_ref[:, :FF_HERE] = (
        middle_grad * up * sigmoid * (1.0 + gate * (1.0 - sigmoid))
    ).astype(BF16)
    back_ref[...] = dot(grad_ref[...], weight, 1, 1).astype(BF16)


def feed(hidden, weight, cotangent, half):
    rows = hidden.shape[0] * hidden.shape[1]
    model = hidden.shape[2]
    return pl.pallas_call(
        feed_kernel,
        grid=(1,),
        in_specs=[
            pl.BlockSpec(hidden.shape, lambda i: (0, 0, 0)),
            pl.BlockSpec(weight.shape, lambda i: (0, 0)),
            pl.BlockSpec((rows, model), lambda i: (half, 0)),
        ],
        out_specs=(
            pl.BlockSpec((rows, FF_HERE), lambda i: (0, 0)),
            pl.BlockSpec((rows, 2 * FF_HERE), lambda i: (0, 0)),
            pl.BlockSpec((rows, model), lambda i: (0, 0)),
        ),
        out_shape=(
            jax.ShapeDtypeStruct((rows, FF_HERE), BF16),
            jax.ShapeDtypeStruct((rows, 2 * FF_HERE), BF16),
            jax.ShapeDtypeStruct((rows, model), BF16),
        ),
        scratch_shapes=[pltpu.VMEM((FF_HERE, model), BF16)],
        compiler_params=kernel_params,
        cost_estimate=pl.CostEstimate(
            flops=5 * rows * model * 2 * FF_HERE, bytes_accessed=8 * 2**20, transcendentals=0
        ),
        name="feed",
    )(hidden, weight, cotangent)


def feed_down_kernel(near_ref, other_ref, weight_ref, near_out, other_out, down_s):
    unpack_down(weight_ref, down_s)
    for ref, out in ((near_ref, near_out), (other_ref, other_out)):
        out[...] = jnp.dot(ref[...], down_s[...], preferred_element_type=F32).astype(BF16)


def feed_down(near, other, weight):
    rows = near.shape[0]
    model = weight.shape[0]
    return pl.pallas_call(
        feed_down_kernel,
        out_shape=(jax.ShapeDtypeStruct((rows, model), BF16),) * 2,
        in_specs=[in_vmem] * 3,
        out_specs=(in_vmem,) * 2,
        scratch_shapes=[pltpu.VMEM((FF_HERE, model), BF16)],
        compiler_params=kernel_params,
        cost_estimate=pl.CostEstimate(
            flops=4 * rows * model * FF_HERE, bytes_accessed=8 * 2**20, transcendentals=0
        ),
        name="feed_down",
    )(near, other, weight)


def ff_product_kernel(
    near_ref, other_ref, grad_near, grad_other, middle_near, middle_other, cotangent_ref, out_ref
):
    def turned(ref):
        return ref[...].reshape(-1, ref.shape[-1]).T

    out_ref[:, : 2 * FF_HERE] = (
        jnp.dot(turned(near_ref), grad_near[...], preferred_element_type=F32)
        + jnp.dot(turned(other_ref), grad_other[...], preferred_element_type=F32)
    ).astype(BF16)
    rows = middle_near.shape[0]
    down = (
        jnp.dot(middle_near[...].T, cotangent_ref[:rows], preferred_element_type=F32)
        + jnp.dot(middle_other[...].T, cotangent_ref[rows:], preferred_element_type=F32)
    ).astype(BF16)
    for rank in range(down.shape[0] // FF_PIECE):
        for part in range(3):
            out_ref[
                rank * PACK_ROWS + part * FF_PIECE : rank * PACK_ROWS + (part + 1) * FF_PIECE,
                2 * FF_HERE :,
            ] = down[
                rank * FF_PIECE : (rank + 1) * FF_PIECE, part * FF_HERE : (part + 1) * FF_HERE
            ]


def ff_product(hidden, grad, middle, cotangent):
    rows, model = cotangent.shape
    steps = 4
    token_spec = pl.BlockSpec(hidden[0].shape[:2] + (model // steps,), lambda i: (0, 0, i))
    grad_spec = pl.BlockSpec(grad[0].shape, lambda i: (0, 0))
    middle_spec = pl.BlockSpec((rows // 2, FF_HERE // steps), lambda i: (0, i))
    return pl.pallas_call(
        ff_product_kernel,
        grid=(steps,),
        in_specs=[token_spec] * 2
        + [grad_spec] * 2
        + [middle_spec] * 2
        + [pl.BlockSpec((rows, model), lambda i: (0, 0))],
        out_specs=pl.BlockSpec((model // steps, 3 * FF_HERE), lambda i: (i, 0)),
        out_shape=jax.ShapeDtypeStruct((model, 3 * FF_HERE), BF16),
        compiler_params=kernel_params,
        cost_estimate=pl.CostEstimate(
            flops=2 * rows * model * 3 * FF_HERE, bytes_accessed=16 * 2**20, transcendentals=0
        ),
        name="ff_product",
    )(*hidden, *grad, *middle, cotangent)


def project_back_kernel(
    order_ref, dq_ref, own_ref, weight_ref, cos_ref, sin_ref, *refs
):
    terms, (grad_ref, kept_ref, sent_ref, rows_s) = refs[:-4], refs[-4:]
    half = HEAD_DIM // 2
    quarter = CHUNK // 2
    count = len(terms) // 2
    parts = [None] * 4
    for t in range(2):
        total = terms[t * count][0].astype(F32)
        for ref in terms[t * count + 1 : (t + 1) * count]:
            total = total + ref[0].astype(F32)
        parts[t], parts[2 + t] = total[:, :quarter], total[:, quarter:]
    kv = jnp.concatenate(parts, axis=1) + own_ref[...].astype(F32)
    cosine, sine = cos_ref[...], sin_ref[...]
    for head in range(GROUP + 1):
        rows = slice(head * HEAD_DIM, (head + 1) * HEAD_DIM)
        values = dq_ref[rows, :] if head < GROUP else kv[:HEAD_DIM]
        first, second = values[:half], values[half:]
        grad_ref[rows, :] = jnp.concatenate(
            [first * cosine + second * sine, second * cosine - first * sine], axis=0
        ).astype(BF16)
    grad_ref[Q_ROWS + HEAD_DIM :, :] = kv[HEAD_DIM:].astype(BF16)
    rows_s[...] = grad_ref[...].T
    weight = weight_ref[:, : Q_ROWS + KV_ROWS]
    block = 2 * CHUNK // (2 * SIDE)
    for group, ref in enumerate((kept_ref, sent_ref)):
        rows = jnp.concatenate(
            [
                rows_s[pl.ds(pl.multiple_of(order_ref[group * SIDE + i] * block, block), block), :]
                for i in range(SIDE)
            ],
            axis=0,
        )
        ref[...] = dot(rows, weight, 1, 1).astype(BF16)


def project_back(order, dq, own, weight, cosine, sine, terms):
    tokens = dq.shape[1]
    first_entry = pl.BlockSpec((1, KV_ROWS, CHUNK), lambda i: (0, 0, 0))

    def whole(values):
        return pl.BlockSpec(values.shape, lambda i: (0, 0))

    outs = (
        jax.ShapeDtypeStruct((Q_ROWS + KV_ROWS, tokens), BF16),
        jax.ShapeDtypeStruct((tokens // 2, weight.shape[0]), BF16),
        jax.ShapeDtypeStruct((tokens // 2, weight.shape[0]), BF16),
    )
    return pl.pallas_call(
        project_back_kernel,
        grid=(1,),
        in_specs=[in_smem]
        + [whole(values) for values in (dq, own, weight, cosine, sine)]
        + [first_entry] * len(terms),
        out_specs=tuple(whole(leaf) for leaf in outs),
        out_shape=outs,
        scratch_shapes=[pltpu.VMEM((tokens, Q_ROWS + KV_ROWS), BF16)],
        compiler_params=kernel_params,
        cost_estimate=pl.CostEstimate(
            flops=2 * tokens * 384 * 1536, bytes_accessed=8 * 2**20, transcendentals=0
        ),
        name="project_back",
    )(order, dq, own, weight, cosine, sine, *terms)


def weight_product_kernel(grad_ref, normed_ref, attended_ref, branch_ref, out_ref):
    out_ref[:, : Q_ROWS + KV_ROWS] = (
        jnp.dot(grad_ref[...], normed_ref[...], preferred_element_type=F32).T.astype(BF16)
    )
    out_ref[:, Q_ROWS + KV_ROWS :] = jnp.dot(
        attended_ref[...], branch_ref[...], preferred_element_type=F32
    ).astype(BF16)


def weight_product(grad, normed, attended, branch):
    return pl.pallas_call(
        weight_product_kernel,
        out_shape=jax.ShapeDtypeStruct(
            (normed.shape[1], grad.shape[0] + branch.shape[1]), BF16
        ),
        in_specs=[in_vmem] * 4,
        out_specs=in_vmem,
        compiler_params=kernel_params,
        cost_estimate=pl.CostEstimate(
            flops=2 * 1024 * 576 * 1536, bytes_accessed=8 * 2**20, transcendentals=0
        ),
        name="weight_product",
    )(grad, normed, attended, branch)


def ff_finish_kernel(
    pieces_ref, gate_ref, up_ref, gain_ref, gate_out, up_out, down_out, gain_out
):
    count = pieces_ref.shape[0]
    lanes = 128
    width = count * lanes
    ranks = lanes // FF_PIECE
    row = lax.broadcasted_iota(jnp.int32, (width, width), 0)
    col = lax.broadcasted_iota(jnp.int32, (width, width), 1)
    source = (col % (count * FF_PIECE)) // FF_PIECE * lanes
    source = source + col // (count * FF_PIECE) * FF_PIECE + col % FF_PIECE
    turn = jnp.where(row == source, 1.0, 0.0).astype(BF16)
    gain = gain_ref[...]
    total = jnp.zeros_like(gain)
    for at, weight_ref, out_ref in ((0, gate_ref, gate_out), (FF_HERE, up_ref, up_out)):
        for group in range(RANKS // ranks):
            start = at + group * lanes
            mixed = jnp.concatenate(
                [pieces_ref[s, :, start : start + lanes] for s in range(count)], axis=1
            )
            product = jnp.dot(mixed, turn, preferred_element_type=F32)
            cols = slice(group * width, (group + 1) * width)
            total = total + jnp.sum(
                product * weight_ref[:, cols].astype(F32), axis=1, keepdims=True
            )
            out_ref[:, cols] = product * gain
    gain_out[...] = total
    for s in range(count):
        for part in range(3):
            down_out[
                s * FF_PIECE : (s + 1) * FF_PIECE, part * FF_HERE : (part + 1) * FF_HERE
            ] = pieces_ref[
                s, part * FF_PIECE : (part + 1) * FF_PIECE, 2 * FF_HERE :
            ].astype(F32)


def ff_finish(pieces, w_gate, w_up, gain):
    return pl.pallas_call(
        ff_finish_kernel,
        out_shape=(
            jax.ShapeDtypeStruct(w_gate.shape, F32),
            jax.ShapeDtypeStruct(w_up.shape, F32),
            jax.ShapeDtypeStruct((pieces.shape[0] * FF_PIECE, 3 * FF_HERE), F32),
            jax.ShapeDtypeStruct(gain.shape, F32),
        ),
        in_specs=[in_vmem] * 4,
        out_specs=(in_vmem,) * 4,
        compiler_params=kernel_params,
        cost_estimate=pl.CostEstimate(
            flops=2 * 96 * 8192 * 1024, bytes_accessed=8 * 2**20, transcendentals=0
        ),
        name="ff_finish",
    )(pieces, w_gate, w_up, gain)


def qkv_finish_kernel(
    pieces_ref, q_ref, k_ref, v_ref, gain_ref, q_out, k_out, v_out, o_out, gain_out
):
    count = pieces_ref.shape[0]
    gain = gain_ref[...]
    total = jnp.zeros_like(gain)
    at = 0
    for width, weight_ref, out_ref in (
        (Q_ROWS, q_ref, q_out),
        (HEAD_DIM, k_ref, k_out),
        (HEAD_DIM, v_ref, v_out),
        (Q_ROWS, None, o_out),
    ):
        product = jnp.concatenate(
            [pieces_ref[s, :, at : at + width].astype(F32) for s in range(count)], axis=1
        )
        at += width
        if weight_ref is None:
            out_ref[...] = product
        else:
            total = total + jnp.sum(
                product * weight_ref[...].astype(F32), axis=1, keepdims=True
            )
            out_ref[...] = product * gain
    gain_out[...] = total


def qkv_finish(pieces, w_query, w_key, w_value, gain):
    return pl.pallas_call(
        qkv_finish_kernel,
        out_shape=(
            jax.ShapeDtypeStruct(w_query.shape, F32),
            jax.ShapeDtypeStruct(w_key.shape, F32),
            jax.ShapeDtypeStruct(w_value.shape, F32),
            jax.ShapeDtypeStruct(w_query.shape, F32),
            jax.ShapeDtypeStruct(gain.shape, F32),
        ),
        in_specs=[in_vmem] * 5,
        out_specs=(in_vmem,) * 5,
        compiler_params=kernel_params,
        cost_estimate=pl.CostEstimate(
            flops=10**6, bytes_accessed=4 * 2**20, transcendentals=0
        ),
        name="qkv_finish",
    )(pieces, w_query, w_key, w_value, gain)


def inverse_rms(values):
    return lax.rsqrt(jnp.mean(values * values, axis=-1, keepdims=True) + epsilon)


def norm_back(scaled_grad, normed, inverse):
    return inverse * (scaled_grad - normed * jnp.mean(scaled_grad * normed, axis=-1, keepdims=True))


def rotate(values, cosine_table, sine_table, direction):
    halves = HEAD_DIM // 2
    first_half = values[..., :halves, :]
    second_half = values[..., halves:, :]
    return jnp.concatenate(
        [
            first_half * cosine_table - direction * second_half * sine_table,
            second_half * cosine_table + direction * first_half * sine_table,
        ],
        axis=-2,
    )


def after(values, *done):
    return lax.optimization_barrier((values,) + done)[0]


def gather(values, axis_name, axis=0):
    return lax.all_gather(values, axis_name, axis=axis, tiled=True)


def on_device(
    tokens,
    norm1_gain,
    w_query,
    w_key,
    w_value,
    w_out,
    norm2_gain,
    w_gate,
    w_up,
    w_down,
    out_cotangent,
):
    seq_count = lax.axis_size("seq")
    wide_count = lax.axis_size("wide")
    seq_index = lax.axis_index("seq")
    wide_index = lax.axis_index("wide")
    rank = wide_index.astype(jnp.int32).reshape(1)
    model = tokens.shape[1]
    ff = w_gate.shape[1]

    mirror = [
        (s * wide_count + w, s * wide_count + (wide_count - 1 - w if s >= seq_count // 2 else w))
        for s in range(seq_count)
        for w in range(wide_count)
    ]

    def swap(values):
        return lax.ppermute(values, ("seq", "wide"), mirror)

    def over_seq(source_to_target):
        return [(s, source_to_target(s)) for s in range(seq_count)]

    def y_shift(step):
        return over_seq(lambda s: (s + 2 * step) % seq_count)

    other_core = over_seq(lambda s: s ^ 1)

    def scatter_cores(partial):
        pairs_of = partial.reshape(SIDE, 2, partial.shape[0] // (2 * SIDE), partial.shape[1])
        sent = lax.dynamic_index_in_dim(pairs_of, 1 - core_index, 1, keepdims=False)
        kept = lax.dynamic_index_in_dim(pairs_of, core_index, 1, keepdims=False)
        return kept.astype(F32) + lax.ppermute(sent, "seq", other_core).astype(F32)

    def scatter_y(kept):
        total = lax.dynamic_index_in_dim(kept, y_index, 0, keepdims=False)
        for step in (1, 2, 3):
            sent = lax.dynamic_index_in_dim(kept, (y_index - step) % SIDE, 0, keepdims=False)
            total = total + lax.ppermute(sent.astype(BF16), "seq", y_shift(-step)).astype(F32)
        return total

    def gather_near(values, first=()):
        stack = jnp.stack(
            [values] + [lax.ppermute(values, "seq", y_shift(step)) for step in (1, 2, 3)]
        )
        if first:
            stack = after(stack, *first)
        return stack, lax.ppermute(stack, "seq", other_core)

    def near_slot(block):
        return ((block % 2) ^ core_index) * SIDE + (y_index - block // 2) % SIDE

    y_index = seq_index // 2
    core_index = seq_index % 2
    far_order = jnp.stack(
        [
            2 * ((y_index - slot % SIDE) % SIDE) + ((slot // SIDE) ^ core_index)
            for slot in range(seq_count)
        ]
    ).astype(jnp.int32)
    near_order = jnp.stack([near_slot(i) for i in range(seq_count)]).astype(jnp.int32)

    gain_one = norm1_gain.astype(F32)[:, None]
    gain_two = norm2_gain.astype(F32)[:, None]
    q_cols = lax.dynamic_slice_in_dim(w_query, seq_index * Q_ROWS, Q_ROWS, 1)
    k_cols = lax.dynamic_slice_in_dim(w_key, seq_index * HEAD_DIM, HEAD_DIM, 1)
    v_cols = lax.dynamic_slice_in_dim(w_value, seq_index * HEAD_DIM, HEAD_DIM, 1)
    qkv_shard = (jnp.concatenate([q_cols, k_cols, v_cols], axis=1).astype(F32) * gain_one).astype(
        BF16
    )

    def ff_cols(weight):
        pieces = weight.reshape(weight.shape[0], wide_count, seq_count, FF_PIECE)
        return lax.dynamic_index_in_dim(pieces, seq_index, 2, keepdims=False).reshape(
            weight.shape[0], wide_count * FF_PIECE
        )

    out_shard = lax.dynamic_slice_in_dim(w_out, seq_index * Q_ROWS, Q_ROWS, 1)
    first_weight = gather(jnp.concatenate([qkv_shard, out_shard], axis=1), "wide")
    tokens_here = swap(tokens)
    tokens_near, tokens_other = gather_near(tokens_here)
    cotangent = swap(after(out_cotangent, tokens_here))
    tokens_other, cotangent = lax.optimization_barrier((tokens_other, cotangent))
    cotangent_rows = jnp.concatenate(gather_near(cotangent)).reshape(-1, model)
    out_near = gather_near(after(first_weight[:, Q_ROWS + KV_ROWS :].T, tokens_other))

    gate_up_shard = (
        jnp.concatenate([ff_cols(w_gate), ff_cols(w_up)], axis=1).astype(F32) * gain_two
    ).astype(BF16)
    down_shard = lax.dynamic_slice_in_dim(w_down, seq_index * FF_PIECE, FF_PIECE, 0)
    half = wide_count * FF_PIECE
    late_shard = jnp.concatenate(
        [
            gate_up_shard,
            down_shard.reshape(FF_PIECE, -1, half)
            .transpose(1, 0, 2)
            .reshape(gate_up_shard.shape[0], -1),
        ],
        axis=1,
    )

    row = jnp.arange(2 * CHUNK, dtype=jnp.int32)
    positions = jnp.where(
        row < CHUNK,
        2 * wide_index * CHUNK + row,
        (CHUNKS - 1 - 2 * wide_index) * CHUNK + row - CHUNK,
    ).astype(F32)
    frequency = jnp.exp(
        jnp.arange(HEAD_DIM // 2).astype(F32) * (-2.0 * math.log(rope_base) / HEAD_DIM)
    )
    angles = frequency[:, None] * positions[None, :]
    cosine_table, sine_table = jnp.cos(angles), jnp.sin(angles)

    normed_one_all, q, kv, kv_pieces = project(
        far_order, tokens_near, tokens_other, first_weight, cosine_table, sine_table
    )

    def wide_shift(x_step, z_step):
        return [
            (
                x * SIDE + z,
                (x + x_step) % SIDE * SIDE + (z + z_step) % SIDE,
            )
            for x in range(SIDE)
            for z in range(SIDE)
        ]

    def move(values, x_step, z_step):
        return lax.ppermute(values, "wide", wide_shift(x_step, z_step))

    def leg(values, axis, step):
        return move(values, 0, step) if axis == 0 else move(values, step, 0)

    def pick(values, which):
        quarter = CHUNK // 2
        return jnp.concatenate(
            [
                values[:, which * quarter : (which + 1) * quarter],
                values[:, CHUNK + which * quarter : CHUNK + (which + 1) * quarter],
            ],
            axis=1,
        )[None]

    kv_all = lax.all_gather(kv_pieces, "wide", axis=0, tiled=False)
    kv_all, cotangent_rows, late_shard, *out_near = lax.optimization_barrier(
        (kv_all, cotangent_rows, late_shard, *out_near)
    )
    out_turned = reorder_blocks(near_order, *out_near).reshape(model, model)
    late_full = gather(late_shard, "wide")
    def kind_of(axis, first, second, count):
        if axis == 0:
            return (count, second, first, 0, 1, 0)
        return (count, first, second, 1, 0, 1)

    line_kinds = [kind_of(t, step, 0, 1) for t in range(2) for step in (1, 2, 3)]
    near_kinds = [kind_of(t, 0, step, SIDE) for t in range(2) for step in (1, 3)]
    far_kinds = [kind_of(t, 0, 2, SIDE) for t in range(2)]
    attended, log_total = attend(rank, q, kv, kv_all)
    attended_tok = lax.all_to_all(attended, "seq", split_axis=1, concat_axis=0, tiled=True)

    inputs = tokens_here.astype(F32)
    inverse_one = inverse_rms(inputs)
    normed_one = inputs * inverse_one
    residual = inputs + dot(attended_tok, out_turned, 0, 1)
    inverse_two = inverse_rms(residual)
    normed_two = residual * inverse_two
    hidden_two = gather_near(normed_two.astype(BF16))
    middle_near, grad_near, back_near = feed(hidden_two[0], late_full, cotangent_rows, 0)
    middle_other, grad_other, back_other = feed(hidden_two[1], late_full, cotangent_rows, 1)

    def add_cores(kept, sent):
        return kept.astype(F32) + lax.ppermute(sent, "seq", other_core).astype(F32)

    def scatter_near(kept):
        piece = kept.shape[0] // SIDE
        total = kept[:piece]
        for step in (1, 2, 3):
            total = total + lax.ppermute(
                kept[step * piece : (step + 1) * piece].astype(BF16), "seq", y_shift(-step)
            ).astype(F32)
        return total

    scaled_two = scatter_near(add_cores(back_near, back_other))
    attended_all = gather(after(attended, hidden_two[0]), "seq")
    middle_late = after(middle_near, back_near, back_other, attended_all)
    down_cores = add_cores(*feed_down(middle_late, middle_other, late_full))
    scaled_two = after(scaled_two, down_cores)
    residual_grad = cotangent.astype(F32) + norm_back(scaled_two, normed_two, inverse_two)
    branch_grad = residual_grad.astype(BF16)
    mixed_grad = dot(out_turned, branch_grad, 0, 1).astype(BF16)
    head_grad = lax.all_to_all(mixed_grad, "seq", split_axis=0, concat_axis=1, tiled=True)

    ff_rows = lax.psum_scatter(
        ff_product(
            hidden_two,
            (after(grad_near, mixed_grad), grad_other),
            (middle_near, middle_other),
            cotangent_rows,
        ),
        "wide",
        scatter_dimension=0,
        tiled=True,
    )
    branch_grad_all = gather(branch_grad, "seq")
    down_part = scatter_near(after(down_cores, head_grad))

    def add(first, second):
        return (first.astype(F32) + second.astype(F32)).astype(BF16)

    q_grad, *near_grads, row_delta = attend_back(
        rank, q, head_grad, log_total, attended, log_total, kv_all, near_kinds, first=True
    )
    near_back = [
        (leg(near_grads[2 * t], 1 - t, -1), leg(near_grads[2 * t + 1], 1 - t, 1))
        for t in range(2)
    ]
    q_grad = after(q_grad, down_part)
    back = (rank, q, head_grad, log_total, row_delta)
    q_grad, *far_grads = attend_back(*back, q_grad, kv_all, far_kinds)
    q_grad, far_grads[0], far_grads[1], *_ = lax.optimization_barrier(
        (q_grad, far_grads[0], far_grads[1], *near_back[0], *near_back[1])
    )
    far_back = [leg(far_grads[t], 1 - t, 2) for t in range(2)]
    q_grad, *line_grads = attend_back(*back, q_grad, kv_all, line_kinds)
    q_grad = after(q_grad, *far_back)
    q_grad_rot, own_grad = attend_back(*back, q_grad, kv_all, [], kv)
    ff_all = lax.all_gather(after(ff_rows, q_grad_rot), "seq", axis=0, tiled=False)
    terms = []
    for t in range(2):
        arrived = [*near_back[t], far_back[t]]
        terms += arrived
        for step in (1, 2, 3):
            sent = line_grads[3 * t + step - 1].astype(F32)
            for one in arrived:
                sent = sent + one[step : step + 1].astype(F32)
            terms.append(leg(sent.astype(BF16), t, -step))
    qkv_grad, kept, sent = project_back(
        far_order, q_grad_rot, own_grad, first_weight, cosine_table, sine_table, terms
    )
    output = swap((residual + after(down_part, qkv_grad)).astype(BF16))
    scaled_one_cores = add_cores(kept, sent)
    scaled_one = scatter_near(scaled_one_cores)
    branch_grad_cols = lax.dynamic_slice_in_dim(
        after(branch_grad_all, q_grad_rot), seq_index * Q_ROWS, Q_ROWS, 1
    )
    qkv_product = weight_product(
        qkv_grad, normed_one_all, attended_all, after(branch_grad_cols, kept)
    )
    qkv_parts = lax.all_to_all(
        qkv_product.reshape(wide_count, -1, qkv_product.shape[1]),
        "wide",
        split_axis=0,
        concat_axis=0,
        tiled=True,
    )
    qkv_rows = jnp.sum(qkv_parts.astype(F32), axis=0).astype(BF16)
    gate_grad_out, up_grad_out, down_grad, gain_two_grad = ff_finish(
        ff_all, w_gate, w_up, gain_two
    )
    tokens_grad = swap(
        (residual_grad + norm_back(after(scaled_one, gain_two_grad), normed_one, inverse_one)).astype(BF16)
    )
    qkv_all = lax.all_gather(qkv_rows, "seq", axis=0, tiled=False)

    q_grad_out, k_grad_out, v_grad_out, out_grad, gain_one_grad = qkv_finish(
        qkv_all, w_query, w_key, w_value, gain_one
    )
    return (
        output,
        tokens_grad,
        gain_one_grad[:, 0],
        q_grad_out,
        k_grad_out,
        v_grad_out,
        out_grad,
        gain_two_grad[:, 0],
        gate_grad_out,
        up_grad_out,
        down_grad,
    )


def solution(mesh):
    placed = (
        P(("wide", "seq"), None),
        P("wide"),
        P("wide", None),
        P("wide", None),
        P("wide", None),
        P("wide", None),
        P("wide"),
        P("wide", None),
        P("wide", None),
        P("wide", None),
        P(("wide", "seq"), None),
    )
    return jax.shard_map(
        on_device,
        mesh=mesh,
        in_specs=placed,
        out_specs=(
            P(("wide", "seq"), None),
            P(("wide", "seq"), None),
            P("wide"),
            P("wide", None),
            P("wide", None),
            P("wide", None),
            P("wide", None),
            P("wide"),
            P("wide", None),
            P("wide", None),
            P("wide", None),
        ),
        check_vma=False,
    )
```

```python
import functools
import math

import jax
import jax.numpy as jnp
from jax import lax
from jax.experimental import pallas as pl
from jax.experimental.pallas import tpu as pltpu
from jax.sharding import PartitionSpec as P

HEAD_DIM = 96
CHUNK = 512
CHUNKS = 32
SIDE = 4
RANKS = SIDE * SIDE
GROUP = 2
Q_ROWS = GROUP * HEAD_DIM
KV_ROWS = 2 * HEAD_DIM
FF_PIECE = 32

epsilon = 1e-05
rope_base = 100000.0
negative = -1e30
log2e = math.log2(math.e)
score_scale = 1.0 / math.sqrt(HEAD_DIM)

F32 = jnp.float32
BF16 = jnp.bfloat16


def dot(left, right, left_dim, right_dim):
    return lax.dot_general(
        left, right, (((left_dim,), (right_dim,)), ((), ())), preferred_element_type=F32
    )


def causal_mask():
    keys = lax.broadcasted_iota(jnp.int32, (CHUNK, CHUNK), 0)
    rows = lax.broadcasted_iota(jnp.int32, (CHUNK, CHUNK), 1)
    return keys <= rows


class Place:
    def __init__(self, rank, piece):
        first = rank < RANKS // 2
        self.early = jnp.where(first, 2 * rank, CHUNKS - 1 - 2 * rank)
        self.early_at = pl.multiple_of(jnp.where(first, 0, piece), piece)
        self.late_at = pl.multiple_of(jnp.where(first, piece, 0), piece)


def source_rank(rank, kind, entry):
    x_back, z_back, x_step, z_step = kind[1:5]
    x = (rank // SIDE - x_back - x_step * entry) & (SIDE - 1)
    z = (rank % SIDE - z_back - z_step * entry) & (SIDE - 1)
    return x * SIDE + z


def for_pieces(rank, kinds, early_only, late_only, before, done):
    here = Place(rank, CHUNK)
    for index, kind in enumerate(kinds):

        def body(entry, carry, index=index, kind=kind):
            source = source_rank(rank, kind, entry)
            there = Place(source, CHUNK // 2)
            before(index, entry)
            pl.when(there.early < here.early)(lambda: early_only(index, entry, there))
            pl.when(there.early > here.early)(lambda: late_only(index, entry, here))
            done(index, entry)
            return carry

        lax.fori_loop(0, kind[0], body, 0)


def attend_blocks(keys_t, values, chains, q_ref, max_s, sum_s, acc_s, diagonal=False):
    rows = [slice(head * HEAD_DIM, (head + 1) * HEAD_DIM) for head, _ in chains]
    lanes = [slice(head, head + 1) for head, _ in chains]
    cols = [c for _, c in chains]
    every = range(len(chains))
    old_max = [max_s[lanes[i], cols[i]] for i in every]
    old_sum = [sum_s[lanes[i], cols[i]] for i in every]
    old_acc = [acc_s[rows[i], cols[i]] for i in every]
    scores = [
        jnp.dot(keys_t, q_ref[rows[i], cols[i]], preferred_element_type=F32) for i in every
    ]
    if diagonal:
        scores = [jnp.where(causal_mask(), one, negative) for one in scores]
    new_max = [
        jnp.maximum(old_max[i], jnp.max(scores[i], axis=0, keepdims=True)) for i in every
    ]
    factor = [jnp.exp2(old_max[i] - new_max[i]) for i in every]
    probs = [jnp.exp2(scores[i] - new_max[i]) for i in every]
    ones = jnp.ones((16, values.shape[1]), BF16)
    values = jnp.concatenate([values, ones], axis=0)
    product = [
        jnp.dot(values, probs[i].astype(BF16), preferred_element_type=F32) for i in every
    ]
    new_sum = [
        old_sum[i] * factor[i] + product[i][HEAD_DIM : HEAD_DIM + 1, :] for i in every
    ]
    new_acc = [old_acc[i] * factor[i] + product[i][:HEAD_DIM, :] for i in every]
    for i in every:
        max_s[lanes[i], cols[i]] = new_max[i]
        sum_s[lanes[i], cols[i]] = new_sum[i]
        acc_s[rows[i], cols[i]] = new_acc[i]


key_rows = slice(0, HEAD_DIM)
value_rows = slice(HEAD_DIM, 2 * HEAD_DIM)


def attend_kernel(
    rank_ref, q_ref, own_ref, kv_in, o_ref, lse_ref, max_s, sum_s, acc_s, kv_ref, arrived
):
    rank = rank_ref[0]

    def fetch(step):
        source = (rank + step) & (RANKS - 1)
        return pltpu.make_async_copy(kv_in.at[source], kv_ref.at[step], arrived.at[step])

    def start(step, carry):
        fetch(step).start()
        return carry

    lax.fori_loop(1, RANKS, start, 0)
    here = Place(rank, CHUNK)
    max_s[...] = jnp.full_like(max_s, negative)
    sum_s[...] = jnp.zeros_like(sum_s)
    acc_s[...] = jnp.zeros_like(acc_s)

    def blocks(keys, values, col_list, diagonal=False):
        chains = [(head, cols) for cols in col_list for head in range(GROUP)]
        attend_blocks(keys.T, values, chains, q_ref, max_s, sum_s, acc_s, diagonal)

    parts = [slice(part * CHUNK, (part + 1) * CHUNK) for part in range(2)]
    late = pl.ds(here.late_at, CHUNK)
    for cols in parts:
        blocks(own_ref[key_rows, cols], own_ref[value_rows, cols], [cols], True)
    early = pl.ds(here.early_at, CHUNK)
    blocks(own_ref[key_rows, early], own_ref[value_rows, early], [late])

    def body(step, carry):
        source = (rank + step) & (RANKS - 1)
        there = Place(source, CHUNK // 2)
        fetch(step).wait()

        @pl.when(there.early < here.early)
        def _():
            cols = pl.ds(there.early_at, CHUNK // 2)
            keys, values = (
                jnp.concatenate([kv_ref[step, 0, rows, cols], kv_ref[step, 1, rows, cols]], 1)
                for rows in (key_rows, value_rows)
            )
            blocks(keys, values, [pl.ds(i * 512, 512) for i in range(2 * CHUNK // 512)])

        @pl.when(there.early > here.early)
        def _():
            keys, values = (
                jnp.concatenate([kv_ref[step, 0, rows, :], kv_ref[step, 1, rows, :]], 1)
                for rows in (key_rows, value_rows)
            )
            blocks(
                keys,
                values,
                [
                    pl.ds(pl.multiple_of(here.late_at + i * 256, 256), 256)
                    for i in range(CHUNK // 256)
                ],
            )

        return carry

    lax.fori_loop(1, RANKS, body, 0)
    for head in range(GROUP):
        rows = slice(head * HEAD_DIM, (head + 1) * HEAD_DIM)
        total = sum_s[head : head + 1, :]
        o_ref[rows, :] = (acc_s[rows, :] / total).astype(BF16)
        lse_ref[head : head + 1, :] = max_s[head : head + 1, :] + jnp.log2(total)


def back_blocks(keys, keys_t, values_t, refs, chains, sums, diagonal=False):
    q_ref, do_ref, lse_ref, delta_ref, dq_s = refs
    rows = [slice(head * HEAD_DIM, (head + 1) * HEAD_DIM) for head, _ in chains]
    lanes = [slice(head, head + 1) for head, _ in chains]
    cols = [c for _, c in chains]
    every = range(len(chains))
    q = [q_ref[rows[i], cols[i]] for i in every]
    do = [do_ref[rows[i], cols[i]] for i in every]
    old = [dq_s[rows[i], cols[i]] for i in every]
    scores = [jnp.dot(keys_t, q[i], preferred_element_type=F32) for i in every]
    dp = [jnp.dot(values_t, do[i], preferred_element_type=F32) for i in every]
    probs = [jnp.exp2(scores[i] - lse_ref[lanes[i], cols[i]]) for i in every]
    if diagonal:
        probs = [jnp.where(causal_mask(), one, 0.0) for one in probs]
    ds = [(probs[i] * (dp[i] - delta_ref[lanes[i], cols[i]])).astype(BF16) for i in every]
    for i in every:
        dk = dot(q[i], ds[i], 1, 1)
        dv = dot(do[i], probs[i].astype(BF16), 1, 1)
        sums = (dk, dv) if sums is None else (sums[0] + dk, sums[1] + dv)
    new = [old[i] + jnp.dot(keys, ds[i], preferred_element_type=F32) for i in every]
    for i in every:
        dq_s[rows[i], cols[i]] = new[i]
    return sums


def attend_back_kernel(
    kinds, own, first, rank_ref, q_ref, do_ref, lse_ref, delta_in, dq_in, kv_in, *refs
):
    count = len(kinds)
    refs, (kv_ref, out_ref, arrived, left) = refs[:-4], refs[-4:]
    rank = rank_ref[0]
    begin = [sum(kind[0] for kind in kinds[:index]) for index in range(count)]

    def fetch(index, entry):
        slot = begin[index] + entry
        source = source_rank(rank, kinds[index], entry)
        return pltpu.make_async_copy(
            kv_in.at[source, kinds[index][5]], kv_ref.at[slot], arrived.at[slot]
        )

    def send(index, entry):
        slot = begin[index] + entry
        return pltpu.make_async_copy(out_ref.at[slot], outs[index].at[entry], left.at[slot])

    for index, kind in enumerate(kinds):

        def start(entry, carry, index=index):
            fetch(index, entry).start()
            return carry

        lax.fori_loop(0, kind[0], start, 0)
    if own:
        own_ref, refs = refs[0], refs[1:]
    dq_s, outs = refs[0], refs[1 : 1 + count]
    if first:
        delta_ref = refs[-1]
        for head in range(GROUP):
            rows = slice(head * HEAD_DIM, (head + 1) * HEAD_DIM)
            delta_ref[head : head + 1, :] = jnp.sum(
                do_ref[rows, :].astype(F32) * delta_in[rows, :].astype(F32), axis=0, keepdims=True
            )
        dq_s[...] = jnp.zeros_like(dq_s)
    else:
        delta_ref = delta_in
        dq_s[...] = dq_in[...]
    shared = (q_ref, do_ref, lse_ref, delta_ref, dq_s)

    def early_only(index, entry, there):
        slot = begin[index] + entry
        cols = pl.ds(there.early_at, CHUNK // 2)
        keys = kv_ref[slot, key_rows, cols]
        keys_t = keys.T
        values_t = kv_ref[slot, value_rows, cols].T
        col_list = [pl.ds(i * 256, 256) for i in range(2 * CHUNK // 256)]
        sums = back_blocks(
            keys,
            keys_t,
            values_t,
            shared,
            [(head, cols) for cols in col_list for head in range(GROUP)],
            None,
        )
        dk, dv = sums
        out_ref[slot, key_rows, cols] = (dk * math.log(2.0)).astype(BF16)
        out_ref[slot, value_rows, cols] = dv.astype(BF16)
        out_ref[slot, :, pl.ds(there.late_at, CHUNK // 2)] = jnp.zeros((KV_ROWS, CHUNK // 2), BF16)

    def late_only(index, entry, here):
        slot = begin[index] + entry
        keys = kv_ref[slot, key_rows, :]
        keys_t = keys.T
        values_t = kv_ref[slot, value_rows, :].T
        col_list = [
            pl.ds(pl.multiple_of(here.late_at + i * 256, 256), 256) for i in range(CHUNK // 256)
        ]
        sums = back_blocks(
            keys,
            keys_t,
            values_t,
            shared,
            [(head, cols) for cols in col_list for head in range(GROUP)],
            None,
        )
        dk, dv = sums
        out_ref[slot, key_rows, :] = (dk * math.log(2.0)).astype(BF16)
        out_ref[slot, value_rows, :] = dv.astype(BF16)

    if own:
        own_out = refs[1 + count]
        here = Place(rank_ref[0], CHUNK)
        early = pl.ds(here.early_at, CHUNK)
        late = pl.ds(here.late_at, CHUNK)

        def block(key_cols, row_cols, sums, diagonal):
            keys = own_ref[key_rows, key_cols]
            keys_t = keys.T
            values_t = own_ref[value_rows, key_cols].T
            chains = [(head, row_cols) for head in range(GROUP)]
            return back_blocks(keys, keys_t, values_t, shared, chains, sums, diagonal)

        def store(cols, sums):
            dk, dv = sums
            own_out[key_rows, cols] = (dk * math.log(2.0)).astype(BF16)
            own_out[value_rows, cols] = dv.astype(BF16)

        store(early, block(early, late, block(early, early, None, True), False))
        store(late, block(late, late, None, True))

    for_pieces(
        rank,
        kinds,
        early_only,
        late_only,
        lambda index, entry: fetch(index, entry).wait(),
        lambda index, entry: send(index, entry).start(),
    )
    for index, kind in enumerate(kinds):

        def finish(entry, carry, index=index):
            send(index, entry).wait()
            return carry

        lax.fori_loop(0, kind[0], finish, 0)
    if own:
        dq_s[...] = dq_s[...] * score_scale


in_vmem = pl.BlockSpec(memory_space=pltpu.VMEM)
in_smem = pl.BlockSpec(memory_space=pltpu.SMEM)
anywhere = pl.BlockSpec(memory_space=pl.ANY)
kernel_params = pltpu.CompilerParams(vmem_limit_bytes=56 * 1024 * 1024)


def work(units, flops):
    return pl.CostEstimate(
        flops=units * flops, bytes_accessed=2**20, transcendentals=units * GROUP * CHUNK * CHUNK
    )


attend_state = (
    jax.ShapeDtypeStruct((GROUP, 2 * CHUNK), F32),
    jax.ShapeDtypeStruct((GROUP, 2 * CHUNK), F32),
    jax.ShapeDtypeStruct((Q_ROWS, 2 * CHUNK), F32),
)


def attend(rank, q, own, kv):
    return pl.pallas_call(
        attend_kernel,
        out_shape=(jax.ShapeDtypeStruct((Q_ROWS, 2 * CHUNK), BF16), attend_state[0]),
        in_specs=[in_smem, in_vmem, in_vmem, anywhere],
        out_specs=(in_vmem,) * 2,
        scratch_shapes=[pltpu.VMEM(leaf.shape, leaf.dtype) for leaf in attend_state]
        + [pltpu.VMEM(kv.shape, kv.dtype), pltpu.SemaphoreType.DMA((RANKS,))],
        compiler_params=kernel_params,
        cost_estimate=work(33, 1_400_000_000),
        name="attend",
    )(rank, q, own, kv)


def attend_back(rank, q, do, lse, delta, dq, kv, kinds, own=None, first=False):
    outs = [jax.ShapeDtypeStruct((kind[0], KV_ROWS, CHUNK), BF16) for kind in kinds]
    operands = [kv]
    pieces = sum(kind[0] for kind in kinds)
    if own is not None:
        outs.append(jax.ShapeDtypeStruct(own.shape, BF16))
        operands.append(own)
    if first:
        outs.append(jax.ShapeDtypeStruct(lse.shape, F32))
    return pl.pallas_call(
        functools.partial(attend_back_kernel, kinds, own is not None, first),
        out_shape=(jax.ShapeDtypeStruct((Q_ROWS, 2 * CHUNK), F32),) + tuple(outs),
        in_specs=[in_smem] + [in_vmem] * 5 + [anywhere] + [in_vmem] * (len(operands) - 1),
        out_specs=(in_vmem,) + (anywhere,) * len(kinds) + (in_vmem,) * (len(outs) - len(kinds)),
        scratch_shapes=[
            pltpu.VMEM((max(pieces, 1), KV_ROWS, CHUNK), BF16),
            pltpu.VMEM((max(pieces, 1), KV_ROWS, CHUNK), BF16),
            pltpu.SemaphoreType.DMA((max(pieces, 1),)),
            pltpu.SemaphoreType.DMA((max(pieces, 1),)),
        ],
        compiler_params=kernel_params,
        cost_estimate=work(
            sum(kind[0] for kind in kinds) + (0 if own is None else 3), 1_950_000_000
        ),
        name="attend_back",
    )(rank, q, do, lse, delta, dq, *operands)


def reorder_kernel(order_ref, near_ref, other_ref, out_ref):
    from_other = order_ref[pl.program_id(0)] >= SIDE

    @pl.when(from_other)
    def _():
        out_ref[...] = other_ref[...]

    @pl.when(jnp.logical_not(from_other))
    def _():
        out_ref[...] = near_ref[...]


def reorder_blocks(order, near, other):
    block = (1,) + near.shape[1:]
    spec = pl.BlockSpec(block, lambda i, order: (order[i] & (SIDE - 1), 0, 0))
    return pl.pallas_call(
        reorder_kernel,
        grid_spec=pltpu.PrefetchScalarGridSpec(
            num_scalar_prefetch=1,
            grid=(2 * SIDE,),
            in_specs=[spec, spec],
            out_specs=pl.BlockSpec(block, lambda i, order: (i, 0, 0)),
        ),
        out_shape=jax.ShapeDtypeStruct((2 * SIDE,) + near.shape[1:], near.dtype),
        cost_estimate=pl.CostEstimate(flops=0, bytes_accessed=12 * near.size, transcendentals=0),
        name="reorder_blocks",
    )(order, near, other)


def project_kernel(
    order_ref, near_ref, other_ref, weight_ref, cos_ref, sin_ref, normed_ref, q_ref, kv_ref, piece_ref
):
    half = HEAD_DIM // 2
    for group, ref in enumerate((near_ref, other_ref)):
        count = ref.shape[0]
        rows = ref.shape[1]
        values = ref[...].astype(F32).reshape(count * rows, ref.shape[2])
        inverse = lax.rsqrt(jnp.mean(values * values, axis=1, keepdims=True) + epsilon)
        normed = (values * inverse).astype(BF16)
        product = jnp.dot(
            normed, weight_ref[:, : Q_ROWS + KV_ROWS], preferred_element_type=F32
        )
        for entry in range(count):
            block = order_ref[group * count + entry]
            at = pl.multiple_of(block * rows, rows)
            here = slice(entry * rows, (entry + 1) * rows)
            normed_ref[pl.ds(at, rows), :] = normed[here]
            turned = product[here].astype(BF16).astype(F32).T
            cosine = cos_ref[:, pl.ds(at, rows)]
            sine = sin_ref[:, pl.ds(at, rows)]
            for head in range(GROUP + 1):
                first = turned[head * HEAD_DIM : head * HEAD_DIM + half]
                second = turned[head * HEAD_DIM + half : (head + 1) * HEAD_DIM]
                rotated = jnp.concatenate(
                    [first * cosine - second * sine, second * cosine + first * sine], axis=0
                )
                if head < GROUP:
                    q_ref[head * HEAD_DIM : (head + 1) * HEAD_DIM, pl.ds(at, rows)] = (
                        rotated * (score_scale * log2e)
                    ).astype(BF16)
                else:
                    keys = rotated.astype(BF16)
            kv = jnp.concatenate([keys, turned[Q_ROWS + HEAD_DIM :].astype(BF16)], axis=0)
            kv_ref[:, pl.ds(at, rows)] = kv
            per_half = CHUNK // 2 // rows
            which = (block // per_half) & 1
            lane = (block // (2 * per_half)) * (CHUNK // 2) + (block % per_half) * rows
            piece_ref[which, :, pl.ds(pl.multiple_of(lane, rows), rows)] = kv


def project(order, near, other, weight, cosine, sine):
    tokens = 2 * CHUNK
    return pl.pallas_call(
        project_kernel,
        out_shape=(
            jax.ShapeDtypeStruct((tokens, near.shape[2]), BF16),
            jax.ShapeDtypeStruct((Q_ROWS, tokens), BF16),
            jax.ShapeDtypeStruct((KV_ROWS, tokens), BF16),
            jax.ShapeDtypeStruct((2, KV_ROWS, CHUNK), BF16),
        ),
        in_specs=[in_smem] + [in_vmem] * 5,
        out_specs=(in_vmem,) * 4,
        compiler_params=kernel_params,
        cost_estimate=pl.CostEstimate(
            flops=2 * tokens * 1536 * 384, bytes_accessed=8 * 2**20, transcendentals=0
        ),
        name="project",
    )(order, near, other, weight, cosine, sine)


FF_HERE = RANKS * FF_PIECE
PACK_ROWS = 3 * FF_PIECE


def unpack_down(weight_ref, down_s):
    for rank in range(RANKS):
        for part in range(3):
            start = rank * PACK_ROWS + part * FF_PIECE
            down_s[
                rank * FF_PIECE : (rank + 1) * FF_PIECE, part * FF_HERE : (part + 1) * FF_HERE
            ] = weight_ref[start : start + FF_PIECE, 2 * FF_HERE :]


def feed_kernel(
    hidden_ref, weight_ref, cotangent_ref, middle_ref, grad_ref, back_ref, out_ref, down_s
):
    rows = middle_ref.shape[0]
    unpack_down(weight_ref, down_s)
    hidden = hidden_ref[...].reshape(rows, hidden_ref.shape[2])
    weight = weight_ref[:, : 2 * FF_HERE]
    product = jnp.dot(hidden, weight, preferred_element_type=F32)
    middle_grad = dot(cotangent_ref[...], down_s[...], 1, 1)
    gate, up = product[:, :FF_HERE], product[:, FF_HERE:]
    sigmoid = 1.0 / (1.0 + jnp.exp(-gate))
    active = gate * sigmoid
    middle_ref[...] = (active * up).astype(BF16)
    grad_ref[:, FF_HERE:] = (middle_grad * active).astype(BF16)
    grad_ref[:, :FF_HERE] = (
        middle_grad * up * sigmoid * (1.0 + gate * (1.0 - sigmoid))
    ).astype(BF16)
    back_ref[...] = dot(grad_ref[...], weight, 1, 1).astype(BF16)
    out_ref[...] = jnp.dot(
        middle_ref[...], down_s[...], preferred_element_type=F32
    ).astype(BF16)


def feed(hidden, weight, cotangent, half):
    rows = hidden.shape[0] * hidden.shape[1]
    model = hidden.shape[2]
    return pl.pallas_call(
        feed_kernel,
        grid=(1,),
        in_specs=[
            pl.BlockSpec(hidden.shape, lambda i: (0, 0, 0)),
            pl.BlockSpec(weight.shape, lambda i: (0, 0)),
            pl.BlockSpec((rows, model), lambda i: (half, 0)),
        ],
        out_specs=(
            pl.BlockSpec((rows, FF_HERE), lambda i: (0, 0)),
            pl.BlockSpec((rows, 2 * FF_HERE), lambda i: (0, 0)),
            pl.BlockSpec((rows, model), lambda i: (0, 0)),
            pl.BlockSpec((rows, model), lambda i: (0, 0)),
        ),
        out_shape=(
            jax.ShapeDtypeStruct((rows, FF_HERE), BF16),
            jax.ShapeDtypeStruct((rows, 2 * FF_HERE), BF16),
            jax.ShapeDtypeStruct((rows, model), BF16),
            jax.ShapeDtypeStruct((rows, model), BF16),
        ),
        scratch_shapes=[pltpu.VMEM((FF_HERE, model), BF16)],
        compiler_params=kernel_params,
        cost_estimate=pl.CostEstimate(
            flops=5 * rows * model * 2 * FF_HERE, bytes_accessed=8 * 2**20, transcendentals=0
        ),
        name="feed",
    )(hidden, weight, cotangent)


def ff_product_kernel(
    near_ref, other_ref, grad_near, grad_other, middle_near, middle_other, cotangent_ref, out_ref
):
    def turned(ref):
        return ref[...].reshape(-1, ref.shape[-1]).T

    out_ref[:, : 2 * FF_HERE] = (
        jnp.dot(turned(near_ref), grad_near[...], preferred_element_type=F32)
        + jnp.dot(turned(other_ref), grad_other[...], preferred_element_type=F32)
    ).astype(BF16)
    rows = middle_near.shape[0]
    down = (
        jnp.dot(middle_near[...].T, cotangent_ref[:rows], preferred_element_type=F32)
        + jnp.dot(middle_other[...].T, cotangent_ref[rows:], preferred_element_type=F32)
    ).astype(BF16)
    for rank in range(down.shape[0] // FF_PIECE):
        for part in range(3):
            out_ref[
                rank * PACK_ROWS + part * FF_PIECE : rank * PACK_ROWS + (part + 1) * FF_PIECE,
                2 * FF_HERE :,
            ] = down[
                rank * FF_PIECE : (rank + 1) * FF_PIECE, part * FF_HERE : (part + 1) * FF_HERE
            ]


def ff_product(hidden, grad, middle, cotangent):
    rows, model = cotangent.shape
    steps = 4
    token_spec = pl.BlockSpec(hidden[0].shape[:2] + (model // steps,), lambda i: (0, 0, i))
    grad_spec = pl.BlockSpec(grad[0].shape, lambda i: (0, 0))
    middle_spec = pl.BlockSpec((rows // 2, FF_HERE // steps), lambda i: (0, i))
    return pl.pallas_call(
        ff_product_kernel,
        grid=(steps,),
        in_specs=[token_spec] * 2
        + [grad_spec] * 2
        + [middle_spec] * 2
        + [pl.BlockSpec((rows, model), lambda i: (0, 0))],
        out_specs=pl.BlockSpec((model // steps, 3 * FF_HERE), lambda i: (i, 0)),
        out_shape=jax.ShapeDtypeStruct((model, 3 * FF_HERE), BF16),
        compiler_params=kernel_params,
        cost_estimate=pl.CostEstimate(
            flops=2 * rows * model * 3 * FF_HERE, bytes_accessed=16 * 2**20, transcendentals=0
        ),
        name="ff_product",
    )(*hidden, *grad, *middle, cotangent)


def project_back_kernel(
    order_ref, dq_ref, own_ref, weight_ref, cos_ref, sin_ref, *refs
):
    terms, (grad_ref, kept_ref, sent_ref, rows_s) = refs[:-4], refs[-4:]
    half = HEAD_DIM // 2
    quarter = CHUNK // 2
    count = len(terms) // 2
    parts = [None] * 4
    for t in range(2):
        total = terms[t * count][0].astype(F32)
        for ref in terms[t * count + 1 : (t + 1) * count]:
            total = total + ref[0].astype(F32)
        parts[t], parts[2 + t] = total[:, :quarter], total[:, quarter:]
    kv = jnp.concatenate(parts, axis=1) + own_ref[...].astype(F32)
    cosine, sine = cos_ref[...], sin_ref[...]
    for head in range(GROUP + 1):
        rows = slice(head * HEAD_DIM, (head + 1) * HEAD_DIM)
        values = dq_ref[rows, :] if head < GROUP else kv[:HEAD_DIM]
        first, second = values[:half], values[half:]
        grad_ref[rows, :] = jnp.concatenate(
            [first * cosine + second * sine, second * cosine - first * sine], axis=0
        ).astype(BF16)
    grad_ref[Q_ROWS + HEAD_DIM :, :] = kv[HEAD_DIM:].astype(BF16)
    rows_s[...] = grad_ref[...].T
    weight = weight_ref[:, : Q_ROWS + KV_ROWS]
    block = 2 * CHUNK // (2 * SIDE)
    for group, ref in enumerate((kept_ref, sent_ref)):
        rows = jnp.concatenate(
            [
                rows_s[pl.ds(pl.multiple_of(order_ref[group * SIDE + i] * block, block), block), :]
                for i in range(SIDE)
            ],
            axis=0,
        )
        ref[...] = dot(rows, weight, 1, 1).astype(BF16)


def project_back(order, dq, own, weight, cosine, sine, terms):
    tokens = dq.shape[1]
    first_entry = pl.BlockSpec((1, KV_ROWS, CHUNK), lambda i: (0, 0, 0))

    def whole(values):
        return pl.BlockSpec(values.shape, lambda i: (0, 0))

    outs = (
        jax.ShapeDtypeStruct((Q_ROWS + KV_ROWS, tokens), BF16),
        jax.ShapeDtypeStruct((tokens // 2, weight.shape[0]), BF16),
        jax.ShapeDtypeStruct((tokens // 2, weight.shape[0]), BF16),
    )
    return pl.pallas_call(
        project_back_kernel,
        grid=(1,),
        in_specs=[in_smem]
        + [whole(values) for values in (dq, own, weight, cosine, sine)]
        + [first_entry] * len(terms),
        out_specs=tuple(whole(leaf) for leaf in outs),
        out_shape=outs,
        scratch_shapes=[pltpu.VMEM((tokens, Q_ROWS + KV_ROWS), BF16)],
        compiler_params=kernel_params,
        cost_estimate=pl.CostEstimate(
            flops=2 * tokens * 384 * 1536, bytes_accessed=8 * 2**20, transcendentals=0
        ),
        name="project_back",
    )(order, dq, own, weight, cosine, sine, *terms)


def weight_product_kernel(grad_ref, normed_ref, attended_ref, branch_ref, out_ref):
    out_ref[:, : Q_ROWS + KV_ROWS] = (
        jnp.dot(grad_ref[...], normed_ref[...], preferred_element_type=F32).T.astype(BF16)
    )
    out_ref[:, Q_ROWS + KV_ROWS :] = jnp.dot(
        attended_ref[...], branch_ref[...], preferred_element_type=F32
    ).astype(BF16)


def weight_product(grad, normed, attended, branch):
    return pl.pallas_call(
        weight_product_kernel,
        out_shape=jax.ShapeDtypeStruct(
            (normed.shape[1], grad.shape[0] + branch.shape[1]), BF16
        ),
        in_specs=[in_vmem] * 4,
        out_specs=in_vmem,
        compiler_params=kernel_params,
        cost_estimate=pl.CostEstimate(
            flops=2 * 1024 * 576 * 1536, bytes_accessed=8 * 2**20, transcendentals=0
        ),
        name="weight_product",
    )(grad, normed, attended, branch)


def ff_finish_kernel(
    pieces_ref, gate_ref, up_ref, gain_ref, gate_out, up_out, down_out, gain_out
):
    count = pieces_ref.shape[0]
    lanes = 128
    width = count * lanes
    ranks = lanes // FF_PIECE
    row = lax.broadcasted_iota(jnp.int32, (width, width), 0)
    col = lax.broadcasted_iota(jnp.int32, (width, width), 1)
    source = (col % (count * FF_PIECE)) // FF_PIECE * lanes
    source = source + col // (count * FF_PIECE) * FF_PIECE + col % FF_PIECE
    turn = jnp.where(row == source, 1.0, 0.0).astype(BF16)
    gain = gain_ref[...]
    total = jnp.zeros_like(gain)
    for at, weight_ref, out_ref in ((0, gate_ref, gate_out), (FF_HERE, up_ref, up_out)):
        for group in range(RANKS // ranks):
            start = at + group * lanes
            mixed = jnp.concatenate(
                [pieces_ref[s, :, start : start + lanes] for s in range(count)], axis=1
            )
            product = jnp.dot(mixed, turn, preferred_element_type=F32)
            cols = slice(group * width, (group + 1) * width)
            total = total + jnp.sum(
                product * weight_ref[:, cols].astype(F32), axis=1, keepdims=True
            )
            out_ref[:, cols] = product * gain
    gain_out[...] = total
    for s in range(count):
        for part in range(3):
            down_out[
                s * FF_PIECE : (s + 1) * FF_PIECE, part * FF_HERE : (part + 1) * FF_HERE
            ] = pieces_ref[
                s, part * FF_PIECE : (part + 1) * FF_PIECE, 2 * FF_HERE :
            ].astype(F32)


def ff_finish(pieces, w_gate, w_up, gain):
    return pl.pallas_call(
        ff_finish_kernel,
        out_shape=(
            jax.ShapeDtypeStruct(w_gate.shape, F32),
            jax.ShapeDtypeStruct(w_up.shape, F32),
            jax.ShapeDtypeStruct((pieces.shape[0] * FF_PIECE, 3 * FF_HERE), F32),
            jax.ShapeDtypeStruct(gain.shape, F32),
        ),
        in_specs=[in_vmem] * 4,
        out_specs=(in_vmem,) * 4,
        compiler_params=kernel_params,
        cost_estimate=pl.CostEstimate(
            flops=2 * 96 * 8192 * 1024, bytes_accessed=8 * 2**20, transcendentals=0
        ),
        name="ff_finish",
    )(pieces, w_gate, w_up, gain)


def qkv_finish_kernel(
    pieces_ref, q_ref, k_ref, v_ref, gain_ref, q_out, k_out, v_out, o_out, gain_out
):
    count = pieces_ref.shape[0]
    gain = gain_ref[...]
    total = jnp.zeros_like(gain)
    at = 0
    for width, weight_ref, out_ref in (
        (Q_ROWS, q_ref, q_out),
        (HEAD_DIM, k_ref, k_out),
        (HEAD_DIM, v_ref, v_out),
        (Q_ROWS, None, o_out),
    ):
        product = jnp.concatenate(
            [pieces_ref[s, :, at : at + width].astype(F32) for s in range(count)], axis=1
        )
        at += width
        if weight_ref is None:
            out_ref[...] = product
        else:
            total = total + jnp.sum(
                product * weight_ref[...].astype(F32), axis=1, keepdims=True
            )
            out_ref[...] = product * gain
    gain_out[...] = total


def qkv_finish(pieces, w_query, w_key, w_value, gain):
    return pl.pallas_call(
        qkv_finish_kernel,
        out_shape=(
            jax.ShapeDtypeStruct(w_query.shape, F32),
            jax.ShapeDtypeStruct(w_key.shape, F32),
            jax.ShapeDtypeStruct(w_value.shape, F32),
            jax.ShapeDtypeStruct(w_query.shape, F32),
            jax.ShapeDtypeStruct(gain.shape, F32),
        ),
        in_specs=[in_vmem] * 5,
        out_specs=(in_vmem,) * 5,
        compiler_params=kernel_params,
        cost_estimate=pl.CostEstimate(
            flops=10**6, bytes_accessed=4 * 2**20, transcendentals=0
        ),
        name="qkv_finish",
    )(pieces, w_query, w_key, w_value, gain)


def inverse_rms(values):
    return lax.rsqrt(jnp.mean(values * values, axis=-1, keepdims=True) + epsilon)


def norm_back(scaled_grad, normed, inverse):
    return inverse * (scaled_grad - normed * jnp.mean(scaled_grad * normed, axis=-1, keepdims=True))


def rotate(values, cosine_table, sine_table, direction):
    halves = HEAD_DIM // 2
    first_half = values[..., :halves, :]
    second_half = values[..., halves:, :]
    return jnp.concatenate(
        [
            first_half * cosine_table - direction * second_half * sine_table,
            second_half * cosine_table + direction * first_half * sine_table,
        ],
        axis=-2,
    )


def after(values, *done):
    return lax.optimization_barrier((values,) + done)[0]


def gather(values, axis_name, axis=0):
    return lax.all_gather(values, axis_name, axis=axis, tiled=True)


def on_device(
    tokens,
    norm1_gain,
    w_query,
    w_key,
    w_value,
    w_out,
    norm2_gain,
    w_gate,
    w_up,
    w_down,
    out_cotangent,
):
    seq_count = lax.axis_size("seq")
    wide_count = lax.axis_size("wide")
    seq_index = lax.axis_index("seq")
    wide_index = lax.axis_index("wide")
    rank = wide_index.astype(jnp.int32).reshape(1)
    model = tokens.shape[1]
    ff = w_gate.shape[1]

    mirror = [
        (s * wide_count + w, s * wide_count + (wide_count - 1 - w if s >= seq_count // 2 else w))
        for s in range(seq_count)
        for w in range(wide_count)
    ]

    def swap(values):
        return lax.ppermute(values, ("seq", "wide"), mirror)

    def over_seq(source_to_target):
        return [(s, source_to_target(s)) for s in range(seq_count)]

    def y_shift(step):
        return over_seq(lambda s: (s + 2 * step) % seq_count)

    other_core = over_seq(lambda s: s ^ 1)

    def scatter_cores(partial):
        pairs_of = partial.reshape(SIDE, 2, partial.shape[0] // (2 * SIDE), partial.shape[1])
        sent = lax.dynamic_index_in_dim(pairs_of, 1 - core_index, 1, keepdims=False)
        kept = lax.dynamic_index_in_dim(pairs_of, core_index, 1, keepdims=False)
        return kept.astype(F32) + lax.ppermute(sent, "seq", other_core).astype(F32)

    def scatter_y(kept):
        total = lax.dynamic_index_in_dim(kept, y_index, 0, keepdims=False)
        for step in (1, 2, 3):
            sent = lax.dynamic_index_in_dim(kept, (y_index - step) % SIDE, 0, keepdims=False)
            total = total + lax.ppermute(sent.astype(BF16), "seq", y_shift(-step)).astype(F32)
        return total

    def gather_near(values, first=()):
        stack = jnp.stack(
            [values] + [lax.ppermute(values, "seq", y_shift(step)) for step in (1, 2, 3)]
        )
        if first:
            stack = after(stack, *first)
        return stack, lax.ppermute(stack, "seq", other_core)

    def near_slot(block):
        return ((block % 2) ^ core_index) * SIDE + (y_index - block // 2) % SIDE

    y_index = seq_index // 2
    core_index = seq_index % 2
    far_order = jnp.stack(
        [
            2 * ((y_index - slot % SIDE) % SIDE) + ((slot // SIDE) ^ core_index)
            for slot in range(seq_count)
        ]
    ).astype(jnp.int32)
    near_order = jnp.stack([near_slot(i) for i in range(seq_count)]).astype(jnp.int32)

    gain_one = norm1_gain.astype(F32)[:, None]
    gain_two = norm2_gain.astype(F32)[:, None]
    q_cols = lax.dynamic_slice_in_dim(w_query, seq_index * Q_ROWS, Q_ROWS, 1)
    k_cols = lax.dynamic_slice_in_dim(w_key, seq_index * HEAD_DIM, HEAD_DIM, 1)
    v_cols = lax.dynamic_slice_in_dim(w_value, seq_index * HEAD_DIM, HEAD_DIM, 1)
    qkv_shard = (jnp.concatenate([q_cols, k_cols, v_cols], axis=1).astype(F32) * gain_one).astype(
        BF16
    )

    def ff_cols(weight):
        pieces = weight.reshape(weight.shape[0], wide_count, seq_count, FF_PIECE)
        return lax.dynamic_index_in_dim(pieces, seq_index, 2, keepdims=False).reshape(
            weight.shape[0], wide_count * FF_PIECE
        )

    out_shard = lax.dynamic_slice_in_dim(w_out, seq_index * Q_ROWS, Q_ROWS, 1)
    first_weight = gather(jnp.concatenate([qkv_shard, out_shard], axis=1), "wide")
    tokens_here = swap(tokens)
    tokens_near, tokens_other = gather_near(tokens_here)
    cotangent = swap(after(out_cotangent, tokens_here))
    tokens_other, cotangent = lax.optimization_barrier((tokens_other, cotangent))
    cotangent_rows = jnp.concatenate(gather_near(cotangent)).reshape(-1, model)
    out_near = gather_near(after(first_weight[:, Q_ROWS + KV_ROWS :].T, tokens_other))

    gate_up_shard = (
        jnp.concatenate([ff_cols(w_gate), ff_cols(w_up)], axis=1).astype(F32) * gain_two
    ).astype(BF16)
    down_shard = lax.dynamic_slice_in_dim(w_down, seq_index * FF_PIECE, FF_PIECE, 0)
    half = wide_count * FF_PIECE
    late_shard = jnp.concatenate(
        [
            gate_up_shard,
            down_shard.reshape(FF_PIECE, -1, half)
            .transpose(1, 0, 2)
            .reshape(gate_up_shard.shape[0], -1),
        ],
        axis=1,
    )

    row = jnp.arange(2 * CHUNK, dtype=jnp.int32)
    positions = jnp.where(
        row < CHUNK,
        2 * wide_index * CHUNK + row,
        (CHUNKS - 1 - 2 * wide_index) * CHUNK + row - CHUNK,
    ).astype(F32)
    frequency = jnp.exp(
        jnp.arange(HEAD_DIM // 2).astype(F32) * (-2.0 * math.log(rope_base) / HEAD_DIM)
    )
    angles = frequency[:, None] * positions[None, :]
    cosine_table, sine_table = jnp.cos(angles), jnp.sin(angles)

    normed_one_all, q, kv, kv_pieces = project(
        far_order, tokens_near, tokens_other, first_weight, cosine_table, sine_table
    )

    def wide_shift(x_step, z_step):
        return [
            (
                x * SIDE + z,
                (x + x_step) % SIDE * SIDE + (z + z_step) % SIDE,
            )
            for x in range(SIDE)
            for z in range(SIDE)
        ]

    def move(values, x_step, z_step):
        return lax.ppermute(values, "wide", wide_shift(x_step, z_step))

    def leg(values, axis, step):
        return move(values, 0, step) if axis == 0 else move(values, step, 0)

    def pick(values, which):
        quarter = CHUNK // 2
        return jnp.concatenate(
            [
                values[:, which * quarter : (which + 1) * quarter],
                values[:, CHUNK + which * quarter : CHUNK + (which + 1) * quarter],
            ],
            axis=1,
        )[None]

    kv_all = lax.all_gather(kv_pieces, "wide", axis=0, tiled=False)
    kv_all, cotangent_rows, late_shard, *out_near = lax.optimization_barrier(
        (kv_all, cotangent_rows, late_shard, *out_near)
    )
    out_turned = reorder_blocks(near_order, *out_near).reshape(model, model)
    late_full = gather(late_shard, "wide")
    def kind_of(axis, first, second, count):
        if axis == 0:
            return (count, second, first, 0, 1, 0)
        return (count, first, second, 1, 0, 1)

    line_kinds = [kind_of(t, step, 0, 1) for t in range(2) for step in (1, 2, 3)]
    near_kinds = [kind_of(t, 0, step, SIDE) for t in range(2) for step in (1, 3)]
    far_kinds = [kind_of(t, 0, 2, SIDE) for t in range(2)]
    attended, log_total = attend(rank, q, kv, kv_all)
    attended_tok = lax.all_to_all(attended, "seq", split_axis=1, concat_axis=0, tiled=True)

    inputs = tokens_here.astype(F32)
    inverse_one = inverse_rms(inputs)
    normed_one = inputs * inverse_one
    residual = inputs + dot(attended_tok, out_turned, 0, 1)
    inverse_two = inverse_rms(residual)
    normed_two = residual * inverse_two
    hidden_two = gather_near(normed_two.astype(BF16))
    middle_near, grad_near, back_near, down_near = feed(hidden_two[0], late_full, cotangent_rows, 0)
    middle_other, grad_other, back_other, down_other = feed(hidden_two[1], late_full, cotangent_rows, 1)

    def add_cores(kept, sent):
        total = kept.astype(F32) + lax.ppermute(sent, "seq", other_core).astype(F32)
        return total.astype(BF16)

    def send_near(kept):
        piece = kept.shape[0] // SIDE
        return [kept[:piece]] + [
            lax.ppermute(kept[step * piece : (step + 1) * piece], "seq", y_shift(-step))
            for step in (1, 2, 3)
        ]

    def add_all(terms):
        return sum(term.astype(F32) for term in terms)

    attended_all = gather(after(attended, hidden_two[0]), "seq")
    scaled_two = add_all(send_near(add_cores(back_near, back_other)))
    down_cores = add_cores(down_near, down_other)
    scaled_two = after(scaled_two, down_cores)
    residual_grad = cotangent.astype(F32) + norm_back(scaled_two, normed_two, inverse_two)
    branch_grad = residual_grad.astype(BF16)
    mixed_grad = dot(out_turned, branch_grad, 0, 1).astype(BF16)
    head_grad = lax.all_to_all(mixed_grad, "seq", split_axis=0, concat_axis=1, tiled=True)

    ff_part = ff_product(
        hidden_two,
        (after(grad_near, mixed_grad, attended_all), grad_other),
        (middle_near, middle_other),
        cotangent_rows,
    )
    ff_rows = lax.psum_scatter(
        after(ff_part, head_grad), "wide", scatter_dimension=0, tiled=True
    )
    down_terms = send_near(after(down_cores, mixed_grad))
    branch_grad_all = gather(branch_grad, "seq")

    def add(first, second):
        return (first.astype(F32) + second.astype(F32)).astype(BF16)

    q_grad, *near_grads, row_delta = attend_back(
        rank, q, head_grad, log_total, attended, log_total, kv_all, near_kinds, first=True
    )
    near_back = [
        (leg(near_grads[2 * t], 1 - t, -1), leg(near_grads[2 * t + 1], 1 - t, 1))
        for t in range(2)
    ]
    back = (rank, q, head_grad, log_total, row_delta)
    q_grad = after(q_grad, *down_terms)
    q_grad, *far_grads = attend_back(*back, q_grad, kv_all, far_kinds)
    q_grad, far_grads[0], far_grads[1], *_ = lax.optimization_barrier(
        (q_grad, far_grads[0], far_grads[1], *near_back[0], *near_back[1])
    )
    far_back = [leg(far_grads[t], 1 - t, 2) for t in range(2)]
    q_grad, *line_grads = attend_back(*back, q_grad, kv_all, line_kinds)
    branch_grad_cols = lax.dynamic_slice_in_dim(
        after(branch_grad_all, q_grad), seq_index * Q_ROWS, Q_ROWS, 1
    )
    q_grad = after(q_grad, branch_grad_cols, *far_back)
    q_grad_rot, own_grad = attend_back(*back, q_grad, kv_all, [], kv)
    terms = []
    for t in range(2):
        arrived = [*near_back[t], far_back[t]]
        terms += arrived
        for step in (1, 2, 3):
            sent = line_grads[3 * t + step - 1].astype(F32)
            for one in arrived:
                sent = sent + one[step : step + 1].astype(F32)
            terms.append(leg(sent.astype(BF16), t, -step))
    qkv_grad, kept, sent = project_back(
        far_order,
        q_grad_rot,
        own_grad,
        first_weight,
        cosine_table,
        sine_table,
        terms,
    )
    qkv_product = weight_product(
        qkv_grad, normed_one_all, attended_all, after(branch_grad_cols, kept)
    )
    scaled_one = add_all(send_near(add_cores(kept, sent)))
    ff_all = lax.all_gather(after(ff_rows, qkv_grad), "seq", axis=0, tiled=False)
    qkv_parts = lax.all_to_all(
        qkv_product.reshape(wide_count, -1, qkv_product.shape[1]),
        "wide",
        split_axis=0,
        concat_axis=0,
        tiled=True,
    )
    qkv_rows = jnp.sum(qkv_parts.astype(F32), axis=0).astype(BF16)
    gate_grad_out, up_grad_out, down_grad, gain_two_grad = ff_finish(
        ff_all, w_gate, w_up, gain_two
    )
    tokens_grad = swap(
        (
            residual_grad
            + norm_back(after(scaled_one, gain_two_grad), normed_one, inverse_one)
        ).astype(BF16)
    )
    output = swap((residual + add_all([after(down_terms[0], kept)] + down_terms[1:])).astype(BF16))
    qkv_all = lax.all_gather(qkv_rows, "seq", axis=0, tiled=False)

    q_grad_out, k_grad_out, v_grad_out, out_grad, gain_one_grad = qkv_finish(
        qkv_all, w_query, w_key, w_value, gain_one
    )
    return (
        output,
        tokens_grad,
        gain_one_grad[:, 0],
        q_grad_out,
        k_grad_out,
        v_grad_out,
        out_grad,
        gain_two_grad[:, 0],
        gate_grad_out,
        up_grad_out,
        down_grad,
    )


def solution(mesh):
    placed = (
        P(("wide", "seq"), None),
        P("wide"),
        P("wide", None),
        P("wide", None),
        P("wide", None),
        P("wide", None),
        P("wide"),
        P("wide", None),
        P("wide", None),
        P("wide", None),
        P(("wide", "seq"), None),
    )
    return jax.shard_map(
        on_device,
        mesh=mesh,
        in_specs=placed,
        out_specs=(
            P(("wide", "seq"), None),
            P(("wide", "seq"), None),
            P("wide"),
            P("wide", None),
            P("wide", None),
            P("wide", None),
            P("wide", None),
            P("wide"),
            P("wide", None),
            P("wide", None),
            P("wide", None),
        ),
        check_vma=False,
    )
```

```python
import functools
import math

import jax
import jax.numpy as jnp
from jax import lax
from jax.experimental import pallas as pl
from jax.experimental.pallas import tpu as pltpu
from jax.sharding import PartitionSpec as P

HEAD_DIM = 96
CHUNK = 512
CHUNKS = 32
SIDE = 4
RANKS = SIDE * SIDE
GROUP = 2
Q_ROWS = GROUP * HEAD_DIM
KV_ROWS = 2 * HEAD_DIM
FF_PIECE = 32

epsilon = 1e-05
rope_base = 100000.0
negative = -1e30
log2e = math.log2(math.e)
score_scale = 1.0 / math.sqrt(HEAD_DIM)

F32 = jnp.float32
BF16 = jnp.bfloat16


def dot(left, right, left_dim, right_dim):
    return lax.dot_general(
        left, right, (((left_dim,), (right_dim,)), ((), ())), preferred_element_type=F32
    )


def causal_mask():
    keys = lax.broadcasted_iota(jnp.int32, (CHUNK, CHUNK), 0)
    rows = lax.broadcasted_iota(jnp.int32, (CHUNK, CHUNK), 1)
    return keys <= rows


class Place:
    def __init__(self, rank, piece):
        first = rank < RANKS // 2
        self.early = jnp.where(first, 2 * rank, CHUNKS - 1 - 2 * rank)
        self.early_at = pl.multiple_of(jnp.where(first, 0, piece), piece)
        self.late_at = pl.multiple_of(jnp.where(first, piece, 0), piece)


def source_rank(rank, kind, entry):
    x_back, z_back, x_step, z_step = kind[1:5]
    x = (rank // SIDE - x_back - x_step * entry) & (SIDE - 1)
    z = (rank % SIDE - z_back - z_step * entry) & (SIDE - 1)
    return x * SIDE + z


def for_pieces(rank, kinds, early_only, late_only, before, done):
    here = Place(rank, CHUNK)
    for index, kind in enumerate(kinds):

        def body(entry, carry, index=index, kind=kind):
            source = source_rank(rank, kind, entry)
            there = Place(source, CHUNK // 2)
            before(index, entry)
            pl.when(there.early < here.early)(lambda: early_only(index, entry, there))
            pl.when(there.early > here.early)(lambda: late_only(index, entry, here))
            done(index, entry)
            return carry

        lax.fori_loop(0, kind[0], body, 0)


def attend_blocks(keys_t, values, chains, q_ref, max_s, sum_s, acc_s, diagonal=False):
    rows = [slice(head * HEAD_DIM, (head + 1) * HEAD_DIM) for head, _ in chains]
    lanes = [slice(head, head + 1) for head, _ in chains]
    cols = [c for _, c in chains]
    every = range(len(chains))
    old_max = [max_s[lanes[i], cols[i]] for i in every]
    old_sum = [sum_s[lanes[i], cols[i]] for i in every]
    old_acc = [acc_s[rows[i], cols[i]] for i in every]
    scores = [
        jnp.dot(keys_t, q_ref[rows[i], cols[i]], preferred_element_type=F32) for i in every
    ]
    if diagonal:
        scores = [jnp.where(causal_mask(), one, negative) for one in scores]
    new_max = [
        jnp.maximum(old_max[i], jnp.max(scores[i], axis=0, keepdims=True)) for i in every
    ]
    factor = [jnp.exp2(old_max[i] - new_max[i]) for i in every]
    probs = [jnp.exp2(scores[i] - new_max[i]) for i in every]
    ones = jnp.ones((16, values.shape[1]), BF16)
    values = jnp.concatenate([values, ones], axis=0)
    product = [
        jnp.dot(values, probs[i].astype(BF16), preferred_element_type=F32) for i in every
    ]
    new_sum = [
        old_sum[i] * factor[i] + product[i][HEAD_DIM : HEAD_DIM + 1, :] for i in every
    ]
    new_acc = [old_acc[i] * factor[i] + product[i][:HEAD_DIM, :] for i in every]
    for i in every:
        max_s[lanes[i], cols[i]] = new_max[i]
        sum_s[lanes[i], cols[i]] = new_sum[i]
        acc_s[rows[i], cols[i]] = new_acc[i]


key_rows = slice(0, HEAD_DIM)
value_rows = slice(HEAD_DIM, 2 * HEAD_DIM)


def attend_kernel(
    rank_ref, q_ref, own_ref, kv_in, o_ref, lse_ref, max_s, sum_s, acc_s, kv_ref, arrived
):
    rank = rank_ref[0]

    def fetch(step):
        source = (rank + step) & (RANKS - 1)
        return pltpu.make_async_copy(kv_in.at[source], kv_ref.at[step], arrived.at[step])

    def start(step, carry):
        fetch(step).start()
        return carry

    lax.fori_loop(1, RANKS, start, 0)
    here = Place(rank, CHUNK)
    max_s[...] = jnp.full_like(max_s, negative)
    sum_s[...] = jnp.zeros_like(sum_s)
    acc_s[...] = jnp.zeros_like(acc_s)

    def blocks(keys, values, col_list, diagonal=False):
        chains = [(head, cols) for cols in col_list for head in range(GROUP)]
        attend_blocks(keys.T, values, chains, q_ref, max_s, sum_s, acc_s, diagonal)

    parts = [slice(part * CHUNK, (part + 1) * CHUNK) for part in range(2)]
    late = pl.ds(here.late_at, CHUNK)
    for cols in parts:
        blocks(own_ref[key_rows, cols], own_ref[value_rows, cols], [cols], True)
    early = pl.ds(here.early_at, CHUNK)
    blocks(own_ref[key_rows, early], own_ref[value_rows, early], [late])

    def body(step, carry):
        source = (rank + step) & (RANKS - 1)
        there = Place(source, CHUNK // 2)
        fetch(step).wait()

        @pl.when(there.early < here.early)
        def _():
            cols = pl.ds(there.early_at, CHUNK // 2)
            keys, values = (
                jnp.concatenate([kv_ref[step, 0, rows, cols], kv_ref[step, 1, rows, cols]], 1)
                for rows in (key_rows, value_rows)
            )
            blocks(keys, values, [pl.ds(i * 512, 512) for i in range(2 * CHUNK // 512)])

        @pl.when(there.early > here.early)
        def _():
            keys, values = (
                jnp.concatenate([kv_ref[step, 0, rows, :], kv_ref[step, 1, rows, :]], 1)
                for rows in (key_rows, value_rows)
            )
            blocks(
                keys,
                values,
                [
                    pl.ds(pl.multiple_of(here.late_at + i * 256, 256), 256)
                    for i in range(CHUNK // 256)
                ],
            )

        return carry

    lax.fori_loop(1, RANKS, body, 0)
    for head in range(GROUP):
        rows = slice(head * HEAD_DIM, (head + 1) * HEAD_DIM)
        total = sum_s[head : head + 1, :]
        o_ref[rows, :] = (acc_s[rows, :] / total).astype(BF16)
        lse_ref[head : head + 1, :] = max_s[head : head + 1, :] + jnp.log2(total)


def back_blocks(keys, keys_t, values_t, refs, chains, sums, diagonal=False):
    q_ref, do_ref, lse_ref, delta_ref, dq_s = refs
    rows = [slice(head * HEAD_DIM, (head + 1) * HEAD_DIM) for head, _ in chains]
    lanes = [slice(head, head + 1) for head, _ in chains]
    cols = [c for _, c in chains]
    every = range(len(chains))
    q = [q_ref[rows[i], cols[i]] for i in every]
    do = [do_ref[rows[i], cols[i]] for i in every]
    old = [dq_s[rows[i], cols[i]] for i in every]
    scores = [jnp.dot(keys_t, q[i], preferred_element_type=F32) for i in every]
    dp = [jnp.dot(values_t, do[i], preferred_element_type=F32) for i in every]
    probs = [jnp.exp2(scores[i] - lse_ref[lanes[i], cols[i]]) for i in every]
    if diagonal:
        probs = [jnp.where(causal_mask(), one, 0.0) for one in probs]
    ds = [(probs[i] * (dp[i] - delta_ref[lanes[i], cols[i]])).astype(BF16) for i in every]
    for i in every:
        dk = dot(q[i], ds[i], 1, 1)
        dv = dot(do[i], probs[i].astype(BF16), 1, 1)
        sums = (dk, dv) if sums is None else (sums[0] + dk, sums[1] + dv)
    new = [old[i] + jnp.dot(keys, ds[i], preferred_element_type=F32) for i in every]
    for i in every:
        dq_s[rows[i], cols[i]] = new[i]
    return sums


def attend_back_kernel(
    kinds, own, first, rank_ref, q_ref, do_ref, lse_ref, delta_in, dq_in, kv_in, *refs
):
    count = len(kinds)
    refs, (kv_ref, out_ref, arrived, left) = refs[:-4], refs[-4:]
    rank = rank_ref[0]
    begin = [sum(kind[0] for kind in kinds[:index]) for index in range(count)]

    def fetch(index, entry):
        slot = begin[index] + entry
        source = source_rank(rank, kinds[index], entry)
        return pltpu.make_async_copy(
            kv_in.at[source, kinds[index][5]], kv_ref.at[slot], arrived.at[slot]
        )

    def send(index, entry):
        slot = begin[index] + entry
        return pltpu.make_async_copy(out_ref.at[slot], outs[index].at[entry], left.at[slot])

    for index, kind in enumerate(kinds):

        def start(entry, carry, index=index):
            fetch(index, entry).start()
            return carry

        lax.fori_loop(0, kind[0], start, 0)
    if own:
        own_ref, refs = refs[0], refs[1:]
    dq_s, outs = refs[0], refs[1 : 1 + count]
    if first:
        delta_ref = refs[-1]
        for head in range(GROUP):
            rows = slice(head * HEAD_DIM, (head + 1) * HEAD_DIM)
            delta_ref[head : head + 1, :] = jnp.sum(
                do_ref[rows, :].astype(F32) * delta_in[rows, :].astype(F32), axis=0, keepdims=True
            )
        dq_s[...] = jnp.zeros_like(dq_s)
    else:
        delta_ref = delta_in
        dq_s[...] = dq_in[...]
    shared = (q_ref, do_ref, lse_ref, delta_ref, dq_s)

    def early_only(index, entry, there):
        slot = begin[index] + entry
        cols = pl.ds(there.early_at, CHUNK // 2)
        keys = kv_ref[slot, key_rows, cols]
        keys_t = keys.T
        values_t = kv_ref[slot, value_rows, cols].T
        col_list = [pl.ds(i * 256, 256) for i in range(2 * CHUNK // 256)]
        sums = back_blocks(
            keys,
            keys_t,
            values_t,
            shared,
            [(head, cols) for cols in col_list for head in range(GROUP)],
            None,
        )
        dk, dv = sums
        out_ref[slot, key_rows, cols] = (dk * math.log(2.0)).astype(BF16)
        out_ref[slot, value_rows, cols] = dv.astype(BF16)
        out_ref[slot, :, pl.ds(there.late_at, CHUNK // 2)] = jnp.zeros((KV_ROWS, CHUNK // 2), BF16)

    def late_only(index, entry, here):
        slot = begin[index] + entry
        keys = kv_ref[slot, key_rows, :]
        keys_t = keys.T
        values_t = kv_ref[slot, value_rows, :].T
        col_list = [
            pl.ds(pl.multiple_of(here.late_at + i * 256, 256), 256) for i in range(CHUNK // 256)
        ]
        sums = back_blocks(
            keys,
            keys_t,
            values_t,
            shared,
            [(head, cols) for cols in col_list for head in range(GROUP)],
            None,
        )
        dk, dv = sums
        out_ref[slot, key_rows, :] = (dk * math.log(2.0)).astype(BF16)
        out_ref[slot, value_rows, :] = dv.astype(BF16)

    if own:
        own_out = refs[1 + count]
        here = Place(rank_ref[0], CHUNK)
        early = pl.ds(here.early_at, CHUNK)
        late = pl.ds(here.late_at, CHUNK)

        def block(key_cols, row_cols, sums, diagonal):
            keys = own_ref[key_rows, key_cols]
            keys_t = keys.T
            values_t = own_ref[value_rows, key_cols].T
            chains = [(head, row_cols) for head in range(GROUP)]
            return back_blocks(keys, keys_t, values_t, shared, chains, sums, diagonal)

        def store(cols, sums):
            dk, dv = sums
            own_out[key_rows, cols] = (dk * math.log(2.0)).astype(BF16)
            own_out[value_rows, cols] = dv.astype(BF16)

        store(early, block(early, late, block(early, early, None, True), False))
        store(late, block(late, late, None, True))

    for_pieces(
        rank,
        kinds,
        early_only,
        late_only,
        lambda index, entry: fetch(index, entry).wait(),
        lambda index, entry: send(index, entry).start(),
    )
    for index, kind in enumerate(kinds):

        def finish(entry, carry, index=index):
            send(index, entry).wait()
            return carry

        lax.fori_loop(0, kind[0], finish, 0)
    if own:
        dq_s[...] = dq_s[...] * score_scale


in_vmem = pl.BlockSpec(memory_space=pltpu.VMEM)
in_smem = pl.BlockSpec(memory_space=pltpu.SMEM)
anywhere = pl.BlockSpec(memory_space=pl.ANY)
kernel_params = pltpu.CompilerParams(vmem_limit_bytes=56 * 1024 * 1024)


def work(units, flops):
    return pl.CostEstimate(
        flops=units * flops, bytes_accessed=2**20, transcendentals=units * GROUP * CHUNK * CHUNK
    )


attend_state = (
    jax.ShapeDtypeStruct((GROUP, 2 * CHUNK), F32),
    jax.ShapeDtypeStruct((GROUP, 2 * CHUNK), F32),
    jax.ShapeDtypeStruct((Q_ROWS, 2 * CHUNK), F32),
)


def attend(rank, q, own, kv):
    return pl.pallas_call(
        attend_kernel,
        out_shape=(jax.ShapeDtypeStruct((Q_ROWS, 2 * CHUNK), BF16), attend_state[0]),
        in_specs=[in_smem, in_vmem, in_vmem, anywhere],
        out_specs=(in_vmem,) * 2,
        scratch_shapes=[pltpu.VMEM(leaf.shape, leaf.dtype) for leaf in attend_state]
        + [pltpu.VMEM(kv.shape, kv.dtype), pltpu.SemaphoreType.DMA((RANKS,))],
        compiler_params=kernel_params,
        cost_estimate=work(33, 1_400_000_000),
        name="attend",
    )(rank, q, own, kv)


def attend_back(rank, q, do, lse, delta, dq, kv, kinds, own=None, first=False):
    outs = [jax.ShapeDtypeStruct((kind[0], KV_ROWS, CHUNK), BF16) for kind in kinds]
    operands = [kv]
    pieces = sum(kind[0] for kind in kinds)
    if own is not None:
        outs.append(jax.ShapeDtypeStruct(own.shape, BF16))
        operands.append(own)
    if first:
        outs.append(jax.ShapeDtypeStruct(lse.shape, F32))
    return pl.pallas_call(
        functools.partial(attend_back_kernel, kinds, own is not None, first),
        out_shape=(jax.ShapeDtypeStruct((Q_ROWS, 2 * CHUNK), F32),) + tuple(outs),
        in_specs=[in_smem] + [in_vmem] * 5 + [anywhere] + [in_vmem] * (len(operands) - 1),
        out_specs=(in_vmem,) + (anywhere,) * len(kinds) + (in_vmem,) * (len(outs) - len(kinds)),
        scratch_shapes=[
            pltpu.VMEM((max(pieces, 1), KV_ROWS, CHUNK), BF16),
            pltpu.VMEM((max(pieces, 1), KV_ROWS, CHUNK), BF16),
            pltpu.SemaphoreType.DMA((max(pieces, 1),)),
            pltpu.SemaphoreType.DMA((max(pieces, 1),)),
        ],
        compiler_params=kernel_params,
        cost_estimate=work(
            sum(kind[0] for kind in kinds) + (0 if own is None else 3), 1_950_000_000
        ),
        name="attend_back",
    )(rank, q, do, lse, delta, dq, *operands)


def reorder_kernel(order_ref, near_ref, other_ref, out_ref):
    from_other = order_ref[pl.program_id(0)] >= SIDE

    @pl.when(from_other)
    def _():
        out_ref[...] = other_ref[...]

    @pl.when(jnp.logical_not(from_other))
    def _():
        out_ref[...] = near_ref[...]


def reorder_blocks(order, near, other):
    block = (1,) + near.shape[1:]
    spec = pl.BlockSpec(block, lambda i, order: (order[i] & (SIDE - 1), 0, 0))
    return pl.pallas_call(
        reorder_kernel,
        grid_spec=pltpu.PrefetchScalarGridSpec(
            num_scalar_prefetch=1,
            grid=(2 * SIDE,),
            in_specs=[spec, spec],
            out_specs=pl.BlockSpec(block, lambda i, order: (i, 0, 0)),
        ),
        out_shape=jax.ShapeDtypeStruct((2 * SIDE,) + near.shape[1:], near.dtype),
        cost_estimate=pl.CostEstimate(flops=0, bytes_accessed=12 * near.size, transcendentals=0),
        name="reorder_blocks",
    )(order, near, other)


def project_kernel(
    order_ref, near_ref, other_ref, weight_ref, cos_ref, sin_ref, normed_ref, q_ref, kv_ref, piece_ref
):
    half = HEAD_DIM // 2
    for group, ref in enumerate((near_ref, other_ref)):
        count = ref.shape[0]
        rows = ref.shape[1]
        values = ref[...].astype(F32).reshape(count * rows, ref.shape[2])
        inverse = lax.rsqrt(jnp.mean(values * values, axis=1, keepdims=True) + epsilon)
        normed = (values * inverse).astype(BF16)
        product = jnp.dot(
            normed, weight_ref[:, : Q_ROWS + KV_ROWS], preferred_element_type=F32
        )
        for entry in range(count):
            block = order_ref[group * count + entry]
            at = pl.multiple_of(block * rows, rows)
            here = slice(entry * rows, (entry + 1) * rows)
            normed_ref[pl.ds(at, rows), :] = normed[here]
            turned = product[here].astype(BF16).astype(F32).T
            cosine = cos_ref[:, pl.ds(at, rows)]
            sine = sin_ref[:, pl.ds(at, rows)]
            for head in range(GROUP + 1):
                first = turned[head * HEAD_DIM : head * HEAD_DIM + half]
                second = turned[head * HEAD_DIM + half : (head + 1) * HEAD_DIM]
                rotated = jnp.concatenate(
                    [first * cosine - second * sine, second * cosine + first * sine], axis=0
                )
                if head < GROUP:
                    q_ref[head * HEAD_DIM : (head + 1) * HEAD_DIM, pl.ds(at, rows)] = (
                        rotated * (score_scale * log2e)
                    ).astype(BF16)
                else:
                    keys = rotated.astype(BF16)
            kv = jnp.concatenate([keys, turned[Q_ROWS + HEAD_DIM :].astype(BF16)], axis=0)
            kv_ref[:, pl.ds(at, rows)] = kv
            per_half = CHUNK // 2 // rows
            which = (block // per_half) & 1
            lane = (block // (2 * per_half)) * (CHUNK // 2) + (block % per_half) * rows
            piece_ref[which, :, pl.ds(pl.multiple_of(lane, rows), rows)] = kv


def project(order, near, other, weight, cosine, sine):
    tokens = 2 * CHUNK
    return pl.pallas_call(
        project_kernel,
        out_shape=(
            jax.ShapeDtypeStruct((tokens, near.shape[2]), BF16),
            jax.ShapeDtypeStruct((Q_ROWS, tokens), BF16),
            jax.ShapeDtypeStruct((KV_ROWS, tokens), BF16),
            jax.ShapeDtypeStruct((2, KV_ROWS, CHUNK), BF16),
        ),
        in_specs=[in_smem] + [in_vmem] * 5,
        out_specs=(in_vmem,) * 4,
        compiler_params=kernel_params,
        cost_estimate=pl.CostEstimate(
            flops=2 * tokens * 1536 * 384, bytes_accessed=8 * 2**20, transcendentals=0
        ),
        name="project",
    )(order, near, other, weight, cosine, sine)


FF_HERE = RANKS * FF_PIECE
PACK_ROWS = 3 * FF_PIECE


def unpack_down(weight_ref, down_s):
    for rank in range(RANKS):
        for part in range(3):
            start = rank * PACK_ROWS + part * FF_PIECE
            down_s[
                rank * FF_PIECE : (rank + 1) * FF_PIECE, part * FF_HERE : (part + 1) * FF_HERE
            ] = weight_ref[start : start + FF_PIECE, 2 * FF_HERE :]


def feed_kernel(
    hidden_ref, weight_ref, cotangent_ref, middle_ref, grad_ref, back_ref, out_ref, down_s
):
    rows = middle_ref.shape[0]
    unpack_down(weight_ref, down_s)
    hidden = hidden_ref[...].reshape(rows, hidden_ref.shape[2])
    weight = weight_ref[:, : 2 * FF_HERE]
    product = jnp.dot(hidden, weight, preferred_element_type=F32)
    middle_grad = dot(cotangent_ref[...], down_s[...], 1, 1)
    gate, up = product[:, :FF_HERE], product[:, FF_HERE:]
    sigmoid = 1.0 / (1.0 + jnp.exp(-gate))
    active = gate * sigmoid
    middle_ref[...] = (active * up).astype(BF16)
    grad_ref[:, FF_HERE:] = (middle_grad * active).astype(BF16)
    grad_ref[:, :FF_HERE] = (
        middle_grad * up * sigmoid * (1.0 + gate * (1.0 - sigmoid))
    ).astype(BF16)
    back_ref[...] = dot(grad_ref[...], weight, 1, 1).astype(BF16)
    out_ref[...] = jnp.dot(
        middle_ref[...], down_s[...], preferred_element_type=F32
    ).astype(BF16)


def feed(hidden, weight, cotangent, half):
    rows = hidden.shape[0] * hidden.shape[1]
    model = hidden.shape[2]
    return pl.pallas_call(
        feed_kernel,
        grid=(1,),
        in_specs=[
            pl.BlockSpec(hidden.shape, lambda i: (0, 0, 0)),
            pl.BlockSpec(weight.shape, lambda i: (0, 0)),
            pl.BlockSpec((rows, model), lambda i: (half, 0)),
        ],
        out_specs=(
            pl.BlockSpec((rows, FF_HERE), lambda i: (0, 0)),
            pl.BlockSpec((rows, 2 * FF_HERE), lambda i: (0, 0)),
            pl.BlockSpec((rows, model), lambda i: (0, 0)),
            pl.BlockSpec((rows, model), lambda i: (0, 0)),
        ),
        out_shape=(
            jax.ShapeDtypeStruct((rows, FF_HERE), BF16),
            jax.ShapeDtypeStruct((rows, 2 * FF_HERE), BF16),
            jax.ShapeDtypeStruct((rows, model), BF16),
            jax.ShapeDtypeStruct((rows, model), BF16),
        ),
        scratch_shapes=[pltpu.VMEM((FF_HERE, model), BF16)],
        compiler_params=kernel_params,
        cost_estimate=pl.CostEstimate(
            flops=5 * rows * model * 2 * FF_HERE, bytes_accessed=8 * 2**20, transcendentals=0
        ),
        name="feed",
    )(hidden, weight, cotangent)


def ff_product_kernel(
    near_ref, other_ref, grad_near, grad_other, middle_near, middle_other, cotangent_ref, out_ref
):
    def turned(ref):
        return ref[...].reshape(-1, ref.shape[-1]).T

    out_ref[:, : 2 * FF_HERE] = (
        jnp.dot(turned(near_ref), grad_near[...], preferred_element_type=F32)
        + jnp.dot(turned(other_ref), grad_other[...], preferred_element_type=F32)
    ).astype(BF16)
    rows = middle_near.shape[0]
    down = (
        jnp.dot(middle_near[...].T, cotangent_ref[:rows], preferred_element_type=F32)
        + jnp.dot(middle_other[...].T, cotangent_ref[rows:], preferred_element_type=F32)
    ).astype(BF16)
    for rank in range(down.shape[0] // FF_PIECE):
        for part in range(3):
            out_ref[
                rank * PACK_ROWS + part * FF_PIECE : rank * PACK_ROWS + (part + 1) * FF_PIECE,
                2 * FF_HERE :,
            ] = down[
                rank * FF_PIECE : (rank + 1) * FF_PIECE, part * FF_HERE : (part + 1) * FF_HERE
            ]


def ff_product(hidden, grad, middle, cotangent):
    rows, model = cotangent.shape
    steps = 4
    token_spec = pl.BlockSpec(hidden[0].shape[:2] + (model // steps,), lambda i: (0, 0, i))
    grad_spec = pl.BlockSpec(grad[0].shape, lambda i: (0, 0))
    middle_spec = pl.BlockSpec((rows // 2, FF_HERE // steps), lambda i: (0, i))
    return pl.pallas_call(
        ff_product_kernel,
        grid=(steps,),
        in_specs=[token_spec] * 2
        + [grad_spec] * 2
        + [middle_spec] * 2
        + [pl.BlockSpec((rows, model), lambda i: (0, 0))],
        out_specs=pl.BlockSpec((model // steps, 3 * FF_HERE), lambda i: (i, 0)),
        out_shape=jax.ShapeDtypeStruct((model, 3 * FF_HERE), BF16),
        compiler_params=kernel_params,
        cost_estimate=pl.CostEstimate(
            flops=2 * rows * model * 3 * FF_HERE, bytes_accessed=16 * 2**20, transcendentals=0
        ),
        name="ff_product",
    )(*hidden, *grad, *middle, cotangent)


def project_back_kernel(
    order_ref, dq_ref, own_ref, weight_ref, cos_ref, sin_ref, *refs
):
    terms, (grad_ref, kept_ref, sent_ref, rows_s) = refs[:-4], refs[-4:]
    half = HEAD_DIM // 2
    quarter = CHUNK // 2
    count = len(terms) // 2
    parts = [None] * 4
    for t in range(2):
        total = terms[t * count][0].astype(F32)
        for ref in terms[t * count + 1 : (t + 1) * count]:
            total = total + ref[0].astype(F32)
        parts[t], parts[2 + t] = total[:, :quarter], total[:, quarter:]
    kv = jnp.concatenate(parts, axis=1) + own_ref[...].astype(F32)
    cosine, sine = cos_ref[...], sin_ref[...]
    for head in range(GROUP + 1):
        rows = slice(head * HEAD_DIM, (head + 1) * HEAD_DIM)
        values = dq_ref[rows, :] if head < GROUP else kv[:HEAD_DIM]
        first, second = values[:half], values[half:]
        grad_ref[rows, :] = jnp.concatenate(
            [first * cosine + second * sine, second * cosine - first * sine], axis=0
        ).astype(BF16)
    grad_ref[Q_ROWS + HEAD_DIM :, :] = kv[HEAD_DIM:].astype(BF16)
    rows_s[...] = grad_ref[...].T
    weight = weight_ref[:, : Q_ROWS + KV_ROWS]
    block = 2 * CHUNK // (2 * SIDE)
    for group, ref in enumerate((kept_ref, sent_ref)):
        rows = jnp.concatenate(
            [
                rows_s[pl.ds(pl.multiple_of(order_ref[group * SIDE + i] * block, block), block), :]
                for i in range(SIDE)
            ],
            axis=0,
        )
        ref[...] = dot(rows, weight, 1, 1).astype(BF16)


def project_back(order, dq, own, weight, cosine, sine, terms):
    tokens = dq.shape[1]
    first_entry = pl.BlockSpec((1, KV_ROWS, CHUNK), lambda i: (0, 0, 0))

    def whole(values):
        return pl.BlockSpec(values.shape, lambda i: (0, 0))

    outs = (
        jax.ShapeDtypeStruct((Q_ROWS + KV_ROWS, tokens), BF16),
        jax.ShapeDtypeStruct((tokens // 2, weight.shape[0]), BF16),
        jax.ShapeDtypeStruct((tokens // 2, weight.shape[0]), BF16),
    )
    return pl.pallas_call(
        project_back_kernel,
        grid=(1,),
        in_specs=[in_smem]
        + [whole(values) for values in (dq, own, weight, cosine, sine)]
        + [first_entry] * len(terms),
        out_specs=tuple(whole(leaf) for leaf in outs),
        out_shape=outs,
        scratch_shapes=[pltpu.VMEM((tokens, Q_ROWS + KV_ROWS), BF16)],
        compiler_params=kernel_params,
        cost_estimate=pl.CostEstimate(
            flops=2 * tokens * 384 * 1536, bytes_accessed=8 * 2**20, transcendentals=0
        ),
        name="project_back",
    )(order, dq, own, weight, cosine, sine, *terms)


def weight_product_kernel(grad_ref, normed_ref, attended_ref, branch_ref, out_ref):
    out_ref[:, : Q_ROWS + KV_ROWS] = (
        jnp.dot(grad_ref[...], normed_ref[...], preferred_element_type=F32).T.astype(BF16)
    )
    out_ref[:, Q_ROWS + KV_ROWS :] = jnp.dot(
        attended_ref[...], branch_ref[...], preferred_element_type=F32
    ).astype(BF16)


def weight_product(grad, normed, attended, branch):
    return pl.pallas_call(
        weight_product_kernel,
        out_shape=jax.ShapeDtypeStruct(
            (normed.shape[1], grad.shape[0] + branch.shape[1]), BF16
        ),
        in_specs=[in_vmem] * 4,
        out_specs=in_vmem,
        compiler_params=kernel_params,
        cost_estimate=pl.CostEstimate(
            flops=2 * 1024 * 576 * 1536, bytes_accessed=8 * 2**20, transcendentals=0
        ),
        name="weight_product",
    )(grad, normed, attended, branch)


def ff_finish_kernel(
    pieces_ref, gate_ref, up_ref, gain_ref, gate_out, up_out, down_out, gain_out
):
    count = pieces_ref.shape[0]
    lanes = 128
    width = count * lanes
    ranks = lanes // FF_PIECE
    row = lax.broadcasted_iota(jnp.int32, (width, width), 0)
    col = lax.broadcasted_iota(jnp.int32, (width, width), 1)
    source = (col % (count * FF_PIECE)) // FF_PIECE * lanes
    source = source + col // (count * FF_PIECE) * FF_PIECE + col % FF_PIECE
    turn = jnp.where(row == source, 1.0, 0.0).astype(BF16)
    gain = gain_ref[...]
    total = jnp.zeros_like(gain)
    for at, weight_ref, out_ref in ((0, gate_ref, gate_out), (FF_HERE, up_ref, up_out)):
        for group in range(RANKS // ranks):
            start = at + group * lanes
            mixed = jnp.concatenate(
                [pieces_ref[s, :, start : start + lanes] for s in range(count)], axis=1
            )
            product = jnp.dot(mixed, turn, preferred_element_type=F32)
            cols = slice(group * width, (group + 1) * width)
            total = total + jnp.sum(
                product * weight_ref[:, cols].astype(F32), axis=1, keepdims=True
            )
            out_ref[:, cols] = product * gain
    gain_out[...] = jnp.broadcast_to(total, (total.shape[0], 128)).T[0:1, :]
    for s in range(count):
        for part in range(3):
            down_out[
                s * FF_PIECE : (s + 1) * FF_PIECE, part * FF_HERE : (part + 1) * FF_HERE
            ] = pieces_ref[
                s, part * FF_PIECE : (part + 1) * FF_PIECE, 2 * FF_HERE :
            ].astype(F32)


def ff_finish(pieces, w_gate, w_up, gain):
    return pl.pallas_call(
        ff_finish_kernel,
        out_shape=(
            jax.ShapeDtypeStruct(w_gate.shape, F32),
            jax.ShapeDtypeStruct(w_up.shape, F32),
            jax.ShapeDtypeStruct((pieces.shape[0] * FF_PIECE, 3 * FF_HERE), F32),
            jax.ShapeDtypeStruct((1, gain.shape[0]), F32),
        ),
        in_specs=[in_vmem] * 4,
        out_specs=(in_vmem,) * 4,
        compiler_params=kernel_params,
        cost_estimate=pl.CostEstimate(
            flops=2 * 96 * 8192 * 1024, bytes_accessed=8 * 2**20, transcendentals=0
        ),
        name="ff_finish",
    )(pieces, w_gate, w_up, gain)


def qkv_finish_kernel(
    pieces_ref, q_ref, k_ref, v_ref, gain_ref, q_out, k_out, v_out, o_out, gain_out
):
    count = pieces_ref.shape[0]
    gain = gain_ref[...]
    total = jnp.zeros_like(gain)
    at = 0
    for width, weight_ref, out_ref in (
        (Q_ROWS, q_ref, q_out),
        (HEAD_DIM, k_ref, k_out),
        (HEAD_DIM, v_ref, v_out),
        (Q_ROWS, None, o_out),
    ):
        product = jnp.concatenate(
            [pieces_ref[s, :, at : at + width].astype(F32) for s in range(count)], axis=1
        )
        at += width
        if weight_ref is None:
            out_ref[...] = product
        else:
            total = total + jnp.sum(
                product * weight_ref[...].astype(F32), axis=1, keepdims=True
            )
            out_ref[...] = product * gain
    gain_out[...] = jnp.broadcast_to(total, (total.shape[0], 128)).T[0:1, :]


def qkv_finish(pieces, w_query, w_key, w_value, gain):
    return pl.pallas_call(
        qkv_finish_kernel,
        out_shape=(
            jax.ShapeDtypeStruct(w_query.shape, F32),
            jax.ShapeDtypeStruct(w_key.shape, F32),
            jax.ShapeDtypeStruct(w_value.shape, F32),
            jax.ShapeDtypeStruct(w_query.shape, F32),
            jax.ShapeDtypeStruct((1, gain.shape[0]), F32),
        ),
        in_specs=[in_vmem] * 5,
        out_specs=(in_vmem,) * 5,
        compiler_params=kernel_params,
        cost_estimate=pl.CostEstimate(
            flops=10**6, bytes_accessed=4 * 2**20, transcendentals=0
        ),
        name="qkv_finish",
    )(pieces, w_query, w_key, w_value, gain)


def inverse_rms(values):
    return lax.rsqrt(jnp.mean(values * values, axis=-1, keepdims=True) + epsilon)


def norm_back(scaled_grad, normed, inverse):
    return inverse * (scaled_grad - normed * jnp.mean(scaled_grad * normed, axis=-1, keepdims=True))


def rotate(values, cosine_table, sine_table, direction):
    halves = HEAD_DIM // 2
    first_half = values[..., :halves, :]
    second_half = values[..., halves:, :]
    return jnp.concatenate(
        [
            first_half * cosine_table - direction * second_half * sine_table,
            second_half * cosine_table + direction * first_half * sine_table,
        ],
        axis=-2,
    )


def after(values, *done):
    return lax.optimization_barrier((values,) + done)[0]


def gather(values, axis_name, axis=0):
    return lax.all_gather(values, axis_name, axis=axis, tiled=True)


def on_device(
    tokens,
    norm1_gain,
    w_query,
    w_key,
    w_value,
    w_out,
    norm2_gain,
    w_gate,
    w_up,
    w_down,
    out_cotangent,
):
    seq_count = lax.axis_size("seq")
    wide_count = lax.axis_size("wide")
    seq_index = lax.axis_index("seq")
    wide_index = lax.axis_index("wide")
    rank = wide_index.astype(jnp.int32).reshape(1)
    model = tokens.shape[1]
    ff = w_gate.shape[1]

    mirror = [
        (s * wide_count + w, s * wide_count + (wide_count - 1 - w if s >= seq_count // 2 else w))
        for s in range(seq_count)
        for w in range(wide_count)
    ]

    def swap(values):
        return lax.ppermute(values, ("seq", "wide"), mirror)

    def over_seq(source_to_target):
        return [(s, source_to_target(s)) for s in range(seq_count)]

    def y_shift(step):
        return over_seq(lambda s: (s + 2 * step) % seq_count)

    other_core = over_seq(lambda s: s ^ 1)

    def scatter_cores(partial):
        pairs_of = partial.reshape(SIDE, 2, partial.shape[0] // (2 * SIDE), partial.shape[1])
        sent = lax.dynamic_index_in_dim(pairs_of, 1 - core_index, 1, keepdims=False)
        kept = lax.dynamic_index_in_dim(pairs_of, core_index, 1, keepdims=False)
        return kept.astype(F32) + lax.ppermute(sent, "seq", other_core).astype(F32)

    def scatter_y(kept):
        total = lax.dynamic_index_in_dim(kept, y_index, 0, keepdims=False)
        for step in (1, 2, 3):
            sent = lax.dynamic_index_in_dim(kept, (y_index - step) % SIDE, 0, keepdims=False)
            total = total + lax.ppermute(sent.astype(BF16), "seq", y_shift(-step)).astype(F32)
        return total

    def gather_near(values, first=()):
        stack = jnp.stack(
            [values] + [lax.ppermute(values, "seq", y_shift(step)) for step in (1, 2, 3)]
        )
        if first:
            stack = after(stack, *first)
        return stack, lax.ppermute(stack, "seq", other_core)

    def near_slot(block):
        return ((block % 2) ^ core_index) * SIDE + (y_index - block // 2) % SIDE

    y_index = seq_index // 2
    core_index = seq_index % 2
    far_order = jnp.stack(
        [
            2 * ((y_index - slot % SIDE) % SIDE) + ((slot // SIDE) ^ core_index)
            for slot in range(seq_count)
        ]
    ).astype(jnp.int32)
    near_order = jnp.stack([near_slot(i) for i in range(seq_count)]).astype(jnp.int32)

    gain_one = norm1_gain.astype(F32)[:, None]
    gain_two = norm2_gain.astype(F32)[:, None]
    q_cols = lax.dynamic_slice_in_dim(w_query, seq_index * Q_ROWS, Q_ROWS, 1)
    k_cols = lax.dynamic_slice_in_dim(w_key, seq_index * HEAD_DIM, HEAD_DIM, 1)
    v_cols = lax.dynamic_slice_in_dim(w_value, seq_index * HEAD_DIM, HEAD_DIM, 1)
    qkv_shard = (jnp.concatenate([q_cols, k_cols, v_cols], axis=1).astype(F32) * gain_one).astype(
        BF16
    )

    def ff_cols(weight):
        pieces = weight.reshape(weight.shape[0], wide_count, seq_count, FF_PIECE)
        return lax.dynamic_index_in_dim(pieces, seq_index, 2, keepdims=False).reshape(
            weight.shape[0], wide_count * FF_PIECE
        )

    out_shard = lax.dynamic_slice_in_dim(w_out, seq_index * Q_ROWS, Q_ROWS, 1)
    first_weight = gather(jnp.concatenate([qkv_shard, out_shard], axis=1), "wide")
    tokens_here = swap(tokens)
    tokens_near, tokens_other = gather_near(tokens_here)
    cotangent = swap(after(out_cotangent, tokens_here))
    tokens_other, cotangent = lax.optimization_barrier((tokens_other, cotangent))
    cotangent_rows = jnp.concatenate(gather_near(cotangent)).reshape(-1, model)
    out_near = gather_near(after(first_weight[:, Q_ROWS + KV_ROWS :].T, tokens_other))

    gate_up_shard = (
        jnp.concatenate([ff_cols(w_gate), ff_cols(w_up)], axis=1).astype(F32) * gain_two
    ).astype(BF16)
    down_shard = lax.dynamic_slice_in_dim(w_down, seq_index * FF_PIECE, FF_PIECE, 0)
    half = wide_count * FF_PIECE
    late_shard = jnp.concatenate(
        [
            gate_up_shard,
            down_shard.reshape(FF_PIECE, -1, half)
            .transpose(1, 0, 2)
            .reshape(gate_up_shard.shape[0], -1),
        ],
        axis=1,
    )

    row = jnp.arange(2 * CHUNK, dtype=jnp.int32)
    positions = jnp.where(
        row < CHUNK,
        2 * wide_index * CHUNK + row,
        (CHUNKS - 1 - 2 * wide_index) * CHUNK + row - CHUNK,
    ).astype(F32)
    frequency = jnp.exp(
        jnp.arange(HEAD_DIM // 2).astype(F32) * (-2.0 * math.log(rope_base) / HEAD_DIM)
    )
    angles = frequency[:, None] * positions[None, :]
    cosine_table, sine_table = jnp.cos(angles), jnp.sin(angles)

    normed_one_all, q, kv, kv_pieces = project(
        far_order, tokens_near, tokens_other, first_weight, cosine_table, sine_table
    )

    def wide_shift(x_step, z_step):
        return [
            (
                x * SIDE + z,
                (x + x_step) % SIDE * SIDE + (z + z_step) % SIDE,
            )
            for x in range(SIDE)
            for z in range(SIDE)
        ]

    def move(values, x_step, z_step):
        return lax.ppermute(values, "wide", wide_shift(x_step, z_step))

    def leg(values, axis, step):
        return move(values, 0, step) if axis == 0 else move(values, step, 0)

    def pick(values, which):
        quarter = CHUNK // 2
        return jnp.concatenate(
            [
                values[:, which * quarter : (which + 1) * quarter],
                values[:, CHUNK + which * quarter : CHUNK + (which + 1) * quarter],
            ],
            axis=1,
        )[None]

    kv_all = lax.all_gather(kv_pieces, "wide", axis=0, tiled=False)
    kv_all, cotangent_rows, late_shard, *out_near = lax.optimization_barrier(
        (kv_all, cotangent_rows, late_shard, *out_near)
    )
    out_turned = reorder_blocks(near_order, *out_near).reshape(model, model)
    late_full = gather(late_shard, "wide")
    def kind_of(axis, first, second, count):
        if axis == 0:
            return (count, second, first, 0, 1, 0)
        return (count, first, second, 1, 0, 1)

    line_kinds = [kind_of(t, step, 0, 1) for t in range(2) for step in (1, 2, 3)]
    near_kinds = [kind_of(t, 0, step, SIDE) for t in range(2) for step in (1, 3)]
    far_kinds = [kind_of(t, 0, 2, SIDE) for t in range(2)]
    attended, log_total = attend(rank, q, kv, kv_all)
    attended_tok = lax.all_to_all(attended, "seq", split_axis=1, concat_axis=0, tiled=True)

    inputs = tokens_here.astype(F32)
    inverse_one = inverse_rms(inputs)
    normed_one = inputs * inverse_one
    residual = inputs + dot(attended_tok, out_turned, 0, 1)
    inverse_two = inverse_rms(residual)
    normed_two = residual * inverse_two
    hidden_two = gather_near(normed_two.astype(BF16))
    middle_near, grad_near, back_near, down_near = feed(hidden_two[0], late_full, cotangent_rows, 0)
    middle_other, grad_other, back_other, down_other = feed(hidden_two[1], late_full, cotangent_rows, 1)

    def add_cores(kept, sent):
        total = kept.astype(F32) + lax.ppermute(sent, "seq", other_core).astype(F32)
        return total.astype(BF16)

    def send_near(kept):
        piece = kept.shape[0] // SIDE
        return [kept[:piece]] + [
            lax.ppermute(kept[step * piece : (step + 1) * piece], "seq", y_shift(-step))
            for step in (1, 2, 3)
        ]

    def add_all(terms):
        return sum(term.astype(F32) for term in terms)

    attended_all = gather(after(attended, hidden_two[0]), "seq")
    scaled_two = add_all(send_near(add_cores(back_near, back_other)))
    down_cores = add_cores(down_near, down_other)
    scaled_two = after(scaled_two, down_cores)
    residual_grad = cotangent.astype(F32) + norm_back(scaled_two, normed_two, inverse_two)
    branch_grad = residual_grad.astype(BF16)
    mixed_grad = dot(out_turned, branch_grad, 0, 1).astype(BF16)
    head_grad = lax.all_to_all(mixed_grad, "seq", split_axis=0, concat_axis=1, tiled=True)

    ff_part = ff_product(
        hidden_two,
        (after(grad_near, mixed_grad, attended_all), grad_other),
        (middle_near, middle_other),
        cotangent_rows,
    )
    ff_rows = lax.psum_scatter(
        after(ff_part, head_grad), "wide", scatter_dimension=0, tiled=True
    )
    down_terms = send_near(after(down_cores, mixed_grad))
    branch_grad_all = gather(branch_grad, "seq")

    def add(first, second):
        return (first.astype(F32) + second.astype(F32)).astype(BF16)

    q_grad, *near_grads, row_delta = attend_back(
        rank, q, head_grad, log_total, attended, log_total, kv_all, near_kinds, first=True
    )
    near_back = [
        (leg(near_grads[2 * t], 1 - t, -1), leg(near_grads[2 * t + 1], 1 - t, 1))
        for t in range(2)
    ]
    back = (rank, q, head_grad, log_total, row_delta)
    q_grad = after(q_grad, *down_terms)
    q_grad, *far_grads = attend_back(*back, q_grad, kv_all, far_kinds)
    branch_grad_cols = lax.dynamic_slice_in_dim(
        after(branch_grad_all, q_grad), seq_index * Q_ROWS, Q_ROWS, 1
    )
    q_grad, branch_grad_cols, far_grads[0], far_grads[1], *_ = lax.optimization_barrier(
        (q_grad, branch_grad_cols, *far_grads, *near_back[0], *near_back[1])
    )
    far_back = [leg(far_grads[t], 1 - t, 2) for t in range(2)]
    q_grad, *line_grads = attend_back(*back, q_grad, kv_all, line_kinds)
    q_grad = after(q_grad, *far_back)
    q_grad_rot, own_grad = attend_back(*back, q_grad, kv_all, [], kv)
    terms = []
    for t in range(2):
        arrived = [*near_back[t], far_back[t]]
        terms += arrived
        for step in (1, 2, 3):
            sent = line_grads[3 * t + step - 1].astype(F32)
            for one in arrived:
                sent = sent + one[step : step + 1].astype(F32)
            terms.append(leg(sent.astype(BF16), t, -step))
    qkv_grad, kept, sent = project_back(
        far_order,
        q_grad_rot,
        own_grad,
        first_weight,
        cosine_table,
        sine_table,
        terms,
    )
    qkv_product = weight_product(
        qkv_grad, normed_one_all, attended_all, after(branch_grad_cols, kept)
    )
    scaled_one = add_all(send_near(add_cores(kept, sent)))
    ff_all = lax.all_gather(after(ff_rows, qkv_grad), "seq", axis=0, tiled=False)
    qkv_parts = lax.all_to_all(
        qkv_product.reshape(wide_count, -1, qkv_product.shape[1]),
        "wide",
        split_axis=0,
        concat_axis=0,
        tiled=True,
    )
    qkv_rows = jnp.sum(qkv_parts.astype(F32), axis=0).astype(BF16)
    gate_grad_out, up_grad_out, down_grad, gain_two_grad = ff_finish(
        ff_all, w_gate, w_up, gain_two
    )
    tokens_grad = swap(
        (
            residual_grad
            + norm_back(after(scaled_one, gain_two_grad), normed_one, inverse_one)
        ).astype(BF16)
    )
    output = swap((residual + add_all([after(down_terms[0], kept)] + down_terms[1:])).astype(BF16))
    qkv_all = lax.all_gather(qkv_rows, "seq", axis=0, tiled=False)

    q_grad_out, k_grad_out, v_grad_out, out_grad, gain_one_grad = qkv_finish(
        qkv_all, w_query, w_key, w_value, gain_one
    )
    return (
        output,
        tokens_grad,
        gain_one_grad[0],
        q_grad_out,
        k_grad_out,
        v_grad_out,
        out_grad,
        gain_two_grad[0],
        gate_grad_out,
        up_grad_out,
        down_grad,
    )


def solution(mesh):
    placed = (
        P(("wide", "seq"), None),
        P("wide"),
        P("wide", None),
        P("wide", None),
        P("wide", None),
        P("wide", None),
        P("wide"),
        P("wide", None),
        P("wide", None),
        P("wide", None),
        P(("wide", "seq"), None),
    )
    return jax.shard_map(
        on_device,
        mesh=mesh,
        in_specs=placed,
        out_specs=(
            P(("wide", "seq"), None),
            P(("wide", "seq"), None),
            P("wide"),
            P("wide", None),
            P("wide", None),
            P("wide", None),
            P("wide", None),
            P("wide"),
            P("wide", None),
            P("wide", None),
            P("wide", None),
        ),
        check_vma=False,
    )
```
